256 devices in a mesh: roll: 32 (over y, x, core), mp: 8 (over z).
Axes of the slice: x: 4, y: 4, z: 8, core: 2. Of those that a mesh axis runs over, the one named last changes fastest.
Arguments:
- tokens: bfloat16 [12288, 5120], P('roll', 'mp'), may hold values from -24 to 24
- dest_shard: int32 [12288], P('roll'), may hold values from 0 to 31, as said below
- dest_offset: int32 [12288], P('roll'), may hold values from 0 to 383, as said below
- seg_lengths: int32 [32, 4], P('roll'), may hold values from 1 to 192, 384 in all within a row
- rewards: int32 [128], P('roll'), may hold values from 0 to 19
- groups: int32 [128], P('roll'), may hold values from 0 to 7, as said below
- reference_head_weight: bfloat16 [5120, 8, 640], P('roll', 'mp'), may hold values from -0.078125 to 0.078125
- policy_head_weight: bfloat16 [5120, 8, 640], P('roll', 'mp'), may hold values from -0.078125 to 0.078125
- upstream: bfloat16 [12288, 8, 384], P('roll', 'mp'), may hold values from -6 to 6
Outputs:
- grad_policy: float32 [5120, 8, 640], P('roll', 'mp')
The draws below stay inside these ranges and needn't reach their ends.
Inputs may be any that keep to these rules, and one draw needn't show every extreme that they name: `dest_shard`: one rollout worker sends at most 24 rows to one trainer shard, and exactly 24 to some; every trainer shard receives exactly 384 rows. `dest_offset`: the rows bound for one trainer shard have distinct offsets. `groups`: every prompt has exactly 16 responses.
All inputs are finite; a program needn't handle non-finite values.
Results may differ from the reference program's by a relative error of at most 0.02.
The reference program's roundings to bfloat16 on the way count: a program that leaves them out, or rounds other values in their place, can miss the bound.
Values may be sent and summed in bfloat16 or wider, within the bound.
No kernel may reach another device: no remote copies, remote signals or barrier semaphores. Data moves between devices by JAX's collectives and lax.ppermute only.
A program may use at most 128 MiB of HBM per device.

```python
import math
import jax
import jax.numpy as jnp
import numpy as np
from jax import lax

MODEL_WIDTH = 5120
KV_HEAD_COUNT = 8
HEAD_WIDTH = 128
QUERY_PER_KV = 3
GSIZE = 16
SHARD_TOKENS = 384
SEG_DEV = 4
HEAD_COLUMNS = 640
TOTAL_TOKENS = 12288
RESP = 128
NGROUP = 8
N_ROLL = 32


def permute_rows(row_key):
    return jax.random.permutation(row_key, SHARD_TOKENS).astype(jnp.int32)


def routing_tables(key):
    key = jax.random.fold_in(key, 11)
    device_count = N_ROLL
    capacity = 2 * SHARD_TOKENS // N_ROLL
    shuffle_key, source_key, target_key = jax.random.split(key, 3)
    shuffle = jax.random.permutation(shuffle_key, device_count).astype(jnp.int32)
    quarter = device_count // 4
    pattern = jnp.where(shuffle < quarter, capacity, jnp.where(shuffle < 3 * quarter, capacity // 2, 0)).astype(jnp.int32)
    source = jnp.arange(device_count, dtype=jnp.int32)
    shifted = (source[None, :] - source[:, None]) % device_count
    amounts = pattern[shifted]
    send_begin = jnp.cumsum(amounts, axis=1).astype(jnp.int32) - amounts
    recv_begin = jnp.cumsum(amounts, axis=0).astype(jnp.int32) - amounts
    send_end = send_begin + amounts
    source_order = jax.vmap(permute_rows)(jax.random.split(source_key, device_count))
    target_order = jax.vmap(permute_rows)(jax.random.split(target_key, device_count))
    position = jnp.arange(SHARD_TOKENS, dtype=jnp.int32)
    target_of = jnp.sum((send_end[:, None, :] <= position[None, :, None]).astype(jnp.int32), axis=2).astype(jnp.int32)
    within = position[None, :] - jnp.take_along_axis(send_begin, target_of, axis=1)
    landing = recv_begin[source[:, None], target_of] + within
    offset_rows = target_order[target_of, landing]
    shard_table = jnp.zeros((device_count, SHARD_TOKENS), jnp.int32).at[source[:, None], source_order].set(target_of)
    offset_table = jnp.zeros((device_count, SHARD_TOKENS), jnp.int32).at[source[:, None], source_order].set(offset_rows)
    return (shard_table.reshape(TOTAL_TOKENS), offset_table.reshape(TOTAL_TOKENS))


def draw_dest_shard(key, part):
    return routing_tables(key)[0]


def draw_dest_offset(key, part):
    return routing_tables(key)[1]


def draw_groups(key, part):
    key = jax.random.fold_in(key, 5)
    return (jax.random.permutation(key, RESP) // GSIZE).astype(jnp.int32)


def draw_rewards(key, part):
    key = jax.random.fold_in(key, 13)
    index = jnp.arange(RESP, dtype=jnp.int32)
    device = index // SEG_DEV
    upper = 2 + 18 * device // max(N_ROLL - 1, 1)
    raw = jax.random.randint(key, (RESP,), 0, 1 << 20, jnp.int32)
    values = raw % upper
    values = jnp.where(index % SEG_DEV == SEG_DEV - 1, upper - 1, values)
    return values.astype(jnp.int32)


def draw_tokens(key, part):
    key = jax.random.fold_in(key, 7)
    base_key = jax.random.fold_in(key, 0)
    values = jnp.clip(jax.random.normal(base_key, (TOTAL_TOKENS, MODEL_WIDTH), jnp.float32), -6.0, 6.0)
    return values.astype(jnp.bfloat16)


def block_levels(key, dims, pieces, smallest, largest):
    def one(dim, blocks):
        heights = jax.random.uniform(jax.random.fold_in(jax.random.fold_in(key, 6), dim), (blocks,), jnp.float32, smallest / len(pieces), largest / len(pieces))
        return jnp.repeat(jnp.exp(heights), dims[dim] // blocks).reshape((-1,) + (1,) * (len(dims) - dim - 1))

    loudness = one(*pieces[0])
    for cut in pieces[1:]:
        loudness = loudness * one(*cut)
    return loudness


def split_up(count, total, limit, lean):
    portions = [(1 << 20) // math.isqrt(grade ** lean) + 1 for grade in range(2, count + 1)]
    surplus, given = total - limit - (count - 1), [1] * (count - 1)
    while surplus > 0:
        candidates = [i for i in range(count - 1) if given[i] < limit]
        mass, left = sum([portions[i] for i in candidates]), surplus
        for i in candidates:
            addition = min(limit - given[i], max(1, left * portions[i] // mass), surplus)
            given[i] = given[i] + addition
            surplus = surplus - addition
    return np.array([limit] + given)


def ragged_sizes(rng, count, total, limit, lean):
    if count == 2:
        one = jax.random.randint(rng, (), max(1, total - limit), min(limit, total - 1) + 1)
        return jnp.stack([one, total - one])
    tallies = jnp.asarray(split_up(count, total, limit, lean), jnp.int32)
    couples = (count - 1) // 2
    source_of, sink = tallies[1:1 + 2 * couples:2], tallies[2:2 + 2 * couples:2]
    slack = jnp.minimum(source_of - 1, limit - sink)
    passed = jax.random.randint(jax.random.fold_in(rng, 1), (couples,), 0, 1 << 20) % (slack + 1)
    tallies = tallies.at[1:1 + 2 * couples:2].set(source_of - passed).at[2:2 + 2 * couples:2].set(sink + passed)
    return tallies[jax.random.permutation(jax.random.fold_in(rng, 2), count)]


def gaussian(own_key, dims, scale, bound, shards=(), kind=jnp.bfloat16):
    loudness = block_levels(own_key, dims, shards, -0.22, 0.18) if shards else 1.0
    values = jax.random.normal(own_key, dims, jnp.float32) * scale * loudness
    return jnp.minimum(jnp.maximum(values, -bound), bound).astype(kind)


def setup_inputs(seed: int = 0) -> dict:
    streams_of = jax.random.split(jax.random.key(seed), 10)
    tokens = draw_tokens(jax.random.fold_in(streams_of[9], 71), 0)
    dest_shard = draw_dest_shard(jax.random.fold_in(streams_of[9], 71), 0)
    dest_offset = draw_dest_offset(jax.random.fold_in(streams_of[9], 71), 0)
    seg_lengths = jax.vmap(lambda own: ragged_sizes(own, SEG_DEV, SHARD_TOKENS, SHARD_TOKENS // 2, 2))(jax.random.split(streams_of[3], N_ROLL)).reshape((N_ROLL, SEG_DEV)).astype(jnp.int32)
    rewards = draw_rewards(jax.random.fold_in(streams_of[9], 71), 0)
    groups = draw_groups(jax.random.fold_in(streams_of[9], 71), 0)
    reference_head_weight = gaussian(streams_of[6], (MODEL_WIDTH, KV_HEAD_COUNT, HEAD_COLUMNS), MODEL_WIDTH ** -0.5, 0.078125, ((0, 32), (1, 8)))
    policy_head_weight = gaussian(streams_of[7], (MODEL_WIDTH, KV_HEAD_COUNT, HEAD_COLUMNS), MODEL_WIDTH ** -0.5, 0.078125, ((0, 32), (1, 8)))
    upstream = gaussian(streams_of[8], (TOTAL_TOKENS, KV_HEAD_COUNT, QUERY_PER_KV * HEAD_WIDTH), 1.0, 6.0, ((0, 32), (1, 8)))
    return {"tokens": tokens, "dest_shard": dest_shard, "dest_offset": dest_offset, "seg_lengths": seg_lengths, "rewards": rewards, "groups": groups, "reference_head_weight": reference_head_weight, "policy_head_weight": policy_head_weight, "upstream": upstream}


KL_WEIGHT = 1.0
MASKED_SCORE = -1e+30
HIGHEST_PRECISION = lax.Precision.HIGHEST

def segment_index(lengths_row, row_count):
    segment_ends = jnp.cumsum(lengths_row)
    position = jnp.arange(row_count, dtype=jnp.int32)
    return lax.optimization_barrier(jnp.sum((position[:, None] >= segment_ends[None, :]).astype(jnp.int32), axis=1)).astype(jnp.int32)

def group_sums(reward_values, labels, group_count):
    member_table = (labels[:, None] == jnp.arange(group_count, dtype=jnp.int32)[None, :]).astype(jnp.float32)
    reward_value = reward_values.astype(jnp.float32)
    member_count = lax.optimization_barrier(jnp.sum(member_table, axis=0))
    group_total = jnp.dot(reward_value, member_table, precision=HIGHEST_PRECISION)
    group_square = jnp.dot(reward_value * reward_value, member_table, precision=HIGHEST_PRECISION)
    return (member_count, group_total, group_square)

def advantage_of(reward_values, labels, member_count, group_total, group_square):
    group_count = member_count.shape[0]
    member_table = (labels[:, None] == jnp.arange(group_count, dtype=jnp.int32)[None, :]).astype(jnp.float32)
    group_mean = group_total / member_count
    spread = jnp.maximum(jnp.sqrt(member_count * group_square - group_total * group_total) / member_count, 1.0)
    centred = reward_values.astype(jnp.float32) - jnp.dot(member_table, group_mean, precision=HIGHEST_PRECISION)
    return centred / jnp.dot(member_table, spread, precision=HIGHEST_PRECISION)

def split_heads(projection, head_count, head_size):
    widened = projection.astype(jnp.float32)
    queries = widened[:, :head_count * head_size].reshape(widened.shape[0], head_count, head_size)
    key_rows = widened[:, head_count * head_size:(head_count + 1) * head_size]
    value_rows = widened[:, (head_count + 1) * head_size:]
    return (queries, key_rows, value_rows)

def attend(queries, key_rows, value_rows, allowed):
    head_scale = queries.shape[2] ** (-0.5)
    scores = jnp.einsum('qgh,kh->gqk', queries, key_rows, precision=HIGHEST_PRECISION) * head_scale
    scores = jnp.where(allowed[None], scores, MASKED_SCORE)
    row_max = lax.optimization_barrier(jnp.max(scores, axis=2, keepdims=True))
    weights = jnp.exp(scores - row_max)
    probability = weights / lax.optimization_barrier(jnp.sum(weights, axis=2, keepdims=True))
    rounded = lax.optimization_barrier(probability.astype(jnp.bfloat16)).astype(jnp.float32)
    output = jnp.einsum('gqk,kh->qgh', rounded, value_rows, precision=HIGHEST_PRECISION)
    return (probability, rounded, output)

def group_gradient(reference_output_rows, policy_output_rows, allowed, row_advantage, cotangent, loss_scale):
    head_size = HEAD_WIDTH
    head_count = cotangent.shape[1] // head_size
    ref_queries, ref_keys, ref_values = split_heads(reference_output_rows, head_count, head_size)
    queries, key_rows, value_rows = split_heads(policy_output_rows, head_count, head_size)
    _, _, out_ref = attend(ref_queries, ref_keys, ref_values, allowed)
    probability, rounded, out_policy = attend(queries, key_rows, value_rows, allowed)
    upstream_rows = cotangent.astype(jnp.float32).reshape(cotangent.shape[0], head_count, head_size)
    grad_out = (row_advantage[:, None, None] * upstream_rows + KL_WEIGHT * (out_policy - out_ref)) * loss_scale
    grad_values = jnp.einsum('gqk,qgh->kh', rounded, grad_out, precision=HIGHEST_PRECISION)
    grad_probs = jnp.einsum('qgh,kh->gqk', grad_out, value_rows, precision=HIGHEST_PRECISION)
    grad_scores = probability * (grad_probs - lax.optimization_barrier(jnp.sum(grad_probs * probability, axis=2, keepdims=True)))
    head_scale = head_size ** (-0.5)
    grad_query = jnp.einsum('gqk,kh->qgh', grad_scores, key_rows, precision=HIGHEST_PRECISION) * head_scale
    grad_keys = jnp.einsum('gqk,qgh->kh', grad_scores, queries, precision=HIGHEST_PRECISION) * head_scale
    joined = jnp.concatenate([grad_query.reshape(grad_query.shape[0], head_count * head_size), grad_keys, grad_values], axis=1)
    return joined.astype(jnp.bfloat16)

def reference(tokens, dest_shard, dest_offset, seg_lengths, rewards, groups, reference_head_weight, policy_head_weight, upstream):
    target_rows = (dest_shard * SHARD_TOKENS + dest_offset).astype(jnp.int32)
    packed = jnp.zeros((TOTAL_TOKENS, MODEL_WIDTH), jnp.bfloat16).at[target_rows].set(tokens)
    member_count, group_total, group_square = group_sums(rewards, groups, NGROUP)
    advantage = advantage_of(rewards, groups, member_count, group_total, group_square)
    reference_matrix = reference_head_weight.reshape(MODEL_WIDTH, KV_HEAD_COUNT * HEAD_COLUMNS)
    policy_weight_matrix = policy_head_weight.reshape(MODEL_WIDTH, KV_HEAD_COUNT * HEAD_COLUMNS)
    loss_scale = TOTAL_TOKENS ** (-0.5)
    position = jnp.arange(SHARD_TOKENS, dtype=jnp.int32)

    def shard_partial(shard_index):
        shard_index = shard_index.astype(jnp.int32)
        trainer_shard_rows = lax.dynamic_slice_in_dim(packed, shard_index * SHARD_TOKENS, SHARD_TOKENS, 0)
        segment = segment_index(seg_lengths[shard_index], SHARD_TOKENS)
        allowed = (segment[:, None] == segment[None, :]) & (position[None, :] <= position[:, None])
        local_advantage = lax.dynamic_slice_in_dim(advantage, shard_index * SEG_DEV, SEG_DEV, 0)
        member_rows = (segment[:, None] == jnp.arange(SEG_DEV, dtype=jnp.int32)[None, :]).astype(jnp.float32)
        row_advantage = lax.optimization_barrier(jnp.sum(member_rows * local_advantage[None, :], axis=1))
        reference_output_rows = jnp.dot(trainer_shard_rows, reference_matrix, preferred_element_type=jnp.float32).astype(jnp.bfloat16).reshape(SHARD_TOKENS, KV_HEAD_COUNT, HEAD_COLUMNS)
        policy_output_rows = jnp.dot(trainer_shard_rows, policy_weight_matrix, preferred_element_type=jnp.float32).astype(jnp.bfloat16).reshape(SHARD_TOKENS, KV_HEAD_COUNT, HEAD_COLUMNS)
        cotangent = lax.dynamic_slice_in_dim(upstream, shard_index * SHARD_TOKENS, SHARD_TOKENS, 0)
        gradient_list = jax.vmap(group_gradient, in_axes=(1, 1, None, None, 1, None), out_axes=1)(reference_output_rows, policy_output_rows, allowed, row_advantage, cotangent, loss_scale)
        projection_gradient = gradient_list.reshape(SHARD_TOKENS, KV_HEAD_COUNT * HEAD_COLUMNS)
        partial_value = lax.dot_general(trainer_shard_rows, projection_gradient, (((0,), (0,)), ((), ())), preferred_element_type=jnp.float32)
        return lax.optimization_barrier(partial_value.astype(jnp.bfloat16)).astype(jnp.float32)

    def accumulate_shard(shard_index, running):
        return running + shard_partial(shard_index)
    gradient_sum = lax.fori_loop(0, N_ROLL, accumulate_shard, jnp.zeros((MODEL_WIDTH, KV_HEAD_COUNT * HEAD_COLUMNS), jnp.float32))
    return gradient_sum.reshape(MODEL_WIDTH, KV_HEAD_COUNT, HEAD_COLUMNS)
```

```python
import jax
import jax.numpy as jnp
from jax import lax
from jax.experimental import pallas as pl
from jax.experimental.pallas import tpu as pltpu
from jax.sharding import Mesh
from jax.sharding import PartitionSpec as P

HEAD_WIDTH = 128
KL_WEIGHT = 1.0
MASKED_SCORE = -1e30

ROWS = 384
CAP = 24
MODEL_BLOCK = 640
COLS = 640
CHUNK = 160
HALF = 2 * CHUNK
LANES = 384
F32 = jnp.float32
BF16 = jnp.bfloat16
I32 = jnp.int32

NOTE_HIGH, NOTE_LOW, NOTE_REWARD, NOTE_GROUP = 64, 65, 66, 70

VMEM = pl.BlockSpec(memory_space=pltpu.VMEM)
SMEM = pl.BlockSpec(memory_space=pltpu.SMEM)
PARAMS = pltpu.CompilerParams(vmem_limit_bytes=56 * 1024 * 1024)


def iota(shape, dim):
    return lax.broadcasted_iota(I32, shape, dim)


def dot(a, b, contract=((1,), (0,))):
    return lax.dot_general(a, b, (contract, ((), ())), preferred_element_type=F32)


def shift(value, axis, size, by):
    return lax.ppermute(value, axis, [(i, (i + by) % size) for i in range(size)])


def wrapped(index, size):
    return lax.rem(index + size, size)


def route_kernel(tokens, shard, offset, rewards, groups, out):
    shard_row = shard[...]
    table = iota((32, ROWS), 0) == shard_row
    before = (iota((ROWS, ROWS), 0) < iota((ROWS, ROWS), 1)).astype(BF16)
    counts = dot(table.astype(BF16), before)
    rank = jnp.sum(jnp.where(table, counts, 0.0), axis=0, keepdims=True).astype(I32)
    slot = shard_row * CAP + rank
    hot = iota((32 * CAP, ROWS), 0) == slot
    lane = iota((MODEL_BLOCK, 2 * LANES), 1)
    half = (lane >= LANES).astype(I32)
    within = lane - half * LANES
    source = jnp.where(within < CHUNK, within, within + CHUNK) + CHUNK * half
    pick = (iota((MODEL_BLOCK, 2 * LANES), 0) == source) & (within < HALF)
    ordered = dot(tokens[...], pick.astype(BF16)).astype(BF16)
    gathered = dot(hot.astype(BF16), ordered)
    odd = shard_row & 1
    note_lane = iota((1, 128), 1)
    common = jnp.zeros((1, 128), F32)
    for i in range(4):
        common = jnp.where(note_lane == NOTE_REWARD + i, rewards[i].astype(F32), common)
        common = jnp.where(note_lane == NOTE_GROUP + i, groups[i].astype(F32), common)
    for core in range(2):
        place = offset[...] + 1 + ROWS * (odd ^ core)
        mark = jnp.sum(jnp.where(hot, place, 0), axis=1, keepdims=True)
        high = (mark >> 4).astype(F32)
        low = (mark & 15).astype(F32)
        notes = jnp.where(note_lane == NOTE_HIGH, high, jnp.where(note_lane == NOTE_LOW, low, common))
        first = LANES * core
        plain = gathered[:, first : first + 256].astype(BF16)
        last = (gathered[:, first + 256 : first + 384] + notes).astype(BF16)
        for chip in range(16):
            rows = slice(2 * CAP * chip, 2 * CAP * (chip + 1))
            out[2 * chip + core, :, 0:256] = plain[rows]
            out[2 * chip + core, :, 256:384] = last[rows]


def route(tokens, shard, offset, rewards, groups):
    return pl.pallas_call(
        route_kernel,
        out_shape=jax.ShapeDtypeStruct((32, 2 * CAP, LANES), BF16),
        in_specs=[VMEM, VMEM, VMEM, SMEM, SMEM],
        out_specs=VMEM,
        compiler_params=PARAMS,
        name="route",
    )(tokens, shard.reshape(1, ROWS), offset.reshape(1, ROWS), rewards, groups)


def place_kernel(arrived, out):
    rows = arrived[...].reshape(32 * 2 * CAP, LANES)
    notes = rows[:, 256:384].astype(F32)
    note_lane = iota((1, 128), 1)
    weight = jnp.where(note_lane == NOTE_HIGH, 16.0, jnp.where(note_lane == NOTE_LOW, 1.0, 0.0))
    mark = jnp.sum(notes * weight, axis=1, keepdims=True).astype(I32) - 1
    hot = (mark == iota((32 * 2 * CAP, 2 * ROWS), 1)).astype(BF16)
    out[...] = dot(rows, hot, ((0,), (0,)))[:HALF].astype(BF16)


def place(arrived):
    return pl.pallas_call(
        place_kernel,
        out_shape=jax.ShapeDtypeStruct((HALF, 2 * ROWS), BF16),
        in_specs=[VMEM],
        out_specs=VMEM,
        compiler_params=PARAMS,
        name="place",
    )(arrived)


def advantage_kernel(all_rewards, all_groups, rewards, groups, lengths, out):
    reward = all_rewards[...].astype(F32)
    group = all_groups[...].astype(I32)
    position = iota((ROWS, 128), 0)
    result = jnp.zeros((ROWS, 128), F32)
    start = 0
    for i in range(4):
        member = group == groups[i]
        count = jnp.sum(jnp.where(member, 1.0, 0.0), keepdims=True)
        total = jnp.sum(jnp.where(member, reward, 0.0), keepdims=True)
        square = jnp.sum(jnp.where(member, reward * reward, 0.0), keepdims=True)
        mean = total / count
        spread = jnp.maximum(jnp.sqrt(count * square - total * total) / count, 1.0)
        advantage = (rewards[i].astype(F32) - mean) / spread
        result = jnp.where(position >= start, advantage, result)
        start = start + lengths[0, i]
    out[...] = result


def row_advantages(all_rewards, all_groups, rewards, groups, lengths):
    return pl.pallas_call(
        advantage_kernel,
        out_shape=jax.ShapeDtypeStruct((ROWS, 128), F32),
        in_specs=[VMEM, VMEM, SMEM, SMEM, SMEM],
        out_specs=VMEM,
        name="advantage",
    )(all_rewards, all_groups, rewards, groups, lengths)


def gather_ring(block, axis):
    half = block.shape[0] // 2
    right = shift(block, axis, 4, 1)
    left = shift(block, axis, 4, -1)
    right2 = shift(right[:half], axis, 4, 1)
    left2 = shift(left[half:], axis, 4, -1)
    return [block, right, left, right2, left2]


def first_kernel(where, a0, a1, a2, a3, a4, b0, b1, b2, b3, b4, a_out, b_out):
    for me, pieces, out in ((where[1], (a0, a1, a2, a3, a4), a_out), (where[0], (b0, b1, b2, b3, b4), b_out)):
        for step, extra, piece in zip((0, -1, 1, 2, 2), (0, 0, 0, 0, CHUNK // 2), pieces):
            begin = wrapped(me + step, 4) * CHUNK + extra
            out[pl.ds(pl.multiple_of(begin, 16), piece.shape[0]), :] = piece[...]


def first_assembly(where, a, b):
    shape = jax.ShapeDtypeStruct((4 * CHUNK, COLS), BF16)
    return pl.pallas_call(
        first_kernel,
        out_shape=(shape, shape),
        in_specs=[SMEM] + [VMEM] * 10,
        out_specs=(VMEM, VMEM),
        compiler_params=PARAMS,
        name="assemble",
    )(where, *a, *b)


def project_kernel(where, *refs):
    tokens, a, b = refs[0:9], refs[9:14], refs[14:19]
    own, other, whole, a_all, b_all = refs[19:]
    y, x, z = where[0], where[1], where[3]
    steps = (0, -1, 1, -2, 2, -3, 3, 4, 4)
    for step, extra, piece in zip(steps, (0,) * 8 + (CHUNK,), tokens):
        begin = wrapped(z + step, 8) * HALF + extra
        whole[pl.ds(pl.multiple_of(begin, 16), piece.shape[0]), :] = piece[...]
    for step, extra, piece in zip((0, -1, 1, 2, 2), (0, 0, 0, 0, HALF), a):
        begin = wrapped(y + step, 4) * (4 * CHUNK) + extra
        a_all[pl.ds(pl.multiple_of(begin, 16), piece.shape[0]), :] = piece[...]
    for step, first, piece in zip((0, -1, 1, 2, 2), (0, 0, 0, 0, 2), b):
        for k in range(piece.shape[0] // CHUNK):
            begin = (4 * (first + k) + wrapped(x + step, 4)) * CHUNK
            b_all[pl.ds(pl.multiple_of(begin, 16), CHUNK), :] = piece[k * CHUNK : (k + 1) * CHUNK, :]
    for weights, begin in ((a_all, 0), (b_all, COLS)):
        result = dot(whole[...], weights[...], ((0,), (0,)))
        own[:, begin : begin + COLS] = result[:ROWS]
        other[:, begin : begin + COLS] = result[ROWS:]


def project(where, tokens, a, b):
    shape = jax.ShapeDtypeStruct((ROWS, 2 * COLS), F32)
    whole = jax.ShapeDtypeStruct((16 * CHUNK, 2 * ROWS), BF16)
    return pl.pallas_call(
        project_kernel,
        out_shape=(shape, shape, whole),
        in_specs=[SMEM] + [VMEM] * 19,
        out_specs=(VMEM, VMEM, VMEM),
        scratch_shapes=[pltpu.VMEM((16 * CHUNK, COLS), BF16)] * 2,
        compiler_params=PARAMS,
        name="project",
    )(where, *tokens, *a, *b)


def two_parts(value):
    high = value.astype(BF16)
    return high, (value - high.astype(F32)).astype(BF16)


def attention_kernel(lengths, own, received, upstream, advantage, out):
    scale = HEAD_WIDTH**-0.5
    key_at = iota((ROWS, ROWS), 1)
    query_at = iota((ROWS, ROWS), 0)
    begin = jnp.zeros((ROWS, 1), I32)
    row_at = iota((ROWS, 1), 0)
    start = 0
    for i in range(4):
        begin = jnp.where(row_at >= start, start, begin)
        start = start + lengths[0, i]
    allowed = (key_at <= query_at) & (key_at >= begin)
    allowed = jnp.concatenate([allowed] * 3, axis=0)

    def heads(value):
        return jnp.concatenate([value[:, 128 * i : 128 * (i + 1)] for i in range(3)], axis=0)

    def attend(first):
        projection = (own[:, first : first + COLS] + received[:, first : first + COLS]).astype(BF16)
        queries, keys, values = heads(projection), projection[:, 384:512], projection[:, 512:640]
        scores = dot(queries, keys, ((1,), (1,))) * scale
        scores = jnp.where(allowed, scores, MASKED_SCORE)
        weights = jnp.exp(scores - jnp.max(scores, axis=1, keepdims=True))
        probs = weights / jnp.sum(weights, axis=1, keepdims=True)
        rounded = probs.astype(BF16)
        return queries, keys, values, probs, rounded, dot(rounded, values)

    out_ref = attend(0)[5]
    queries, keys, values, probs, rounded, out_policy = attend(COLS)
    weight = jnp.concatenate([advantage[...]] * 3, axis=0)
    grad_out = (weight * heads(upstream[...].astype(F32)) + KL_WEIGHT * (out_policy - out_ref)) * (12288**-0.5)
    high, low = two_parts(grad_out)
    grad_values = dot(rounded, high, ((0,), (0,))) + dot(rounded, low, ((0,), (0,)))
    grad_probs = dot(high, values, ((1,), (1,))) + dot(low, values, ((1,), (1,)))
    grad_scores = probs * (grad_probs - jnp.sum(grad_probs * probs, axis=1, keepdims=True))
    high, low = two_parts(grad_scores)
    grad_query = (dot(high, keys) + dot(low, keys)) * scale
    grad_keys = (dot(high, queries, ((0,), (0,))) + dot(low, queries, ((0,), (0,)))) * scale
    for i in range(3):
        out[:, 128 * i : 128 * (i + 1)] = grad_query[ROWS * i : ROWS * (i + 1)].astype(BF16)
    out[:, 384:512] = grad_keys.astype(BF16)
    out[:, 512:640] = grad_values.astype(BF16)


def attention(lengths, own, received, upstream, advantage):
    return pl.pallas_call(
        attention_kernel,
        out_shape=jax.ShapeDtypeStruct((ROWS, COLS), BF16),
        in_specs=[SMEM] + [VMEM] * 4,
        out_specs=VMEM,
        compiler_params=PARAMS,
        name="attention",
    )(lengths, own, received, upstream, advantage)


def gradient_kernel(moves, where, whole, own, other, *outs):
    grad = jnp.concatenate([own[...], other[...]], axis=0)
    y, x = where[0], where[1]
    half = CHUNK // 2
    for i, move in enumerate(moves):
        for part in range(2):
            rows = []
            for k in range(4):
                chunk = 4 * k + wrapped(x + move, 4) if part == 0 else 4 * wrapped(y + move, 4) + k
                rows.append(whole[pl.ds(pl.multiple_of(chunk * CHUNK + part * half, 16), half), :])
            outs[2 * i + part][...] = dot(jnp.concatenate(rows, axis=0), grad).astype(BF16)


def gradient_parts(where, whole, own, other, moves):
    shape = jax.ShapeDtypeStruct((4 * CHUNK // 2, COLS), BF16)

    def kernel(*refs):
        gradient_kernel(moves, *refs)

    count = 2 * len(moves)
    return pl.pallas_call(
        kernel,
        out_shape=(shape,) * count,
        in_specs=[SMEM] + [VMEM] * 3,
        out_specs=(VMEM,) * count,
        compiler_params=PARAMS,
        name="gradient",
    )(where, whole, own, other)


def middle_kernel(where, *refs):
    half = CHUNK // 2
    for part, me in ((0, where[0]), (1, where[1])):
        pieces, outs = refs[4 * part : 4 * part + 4], refs[8 + 4 * part : 12 + 4 * part]
        for move, out in zip((0, 1, -1, 2), outs):
            at = pl.ds(pl.multiple_of(wrapped(me + move, 4) * half, 16), half)
            total = (pieces[0][at, :].astype(F32) + pieces[1][at, :].astype(F32)) + (
                pieces[2][at, :].astype(F32) + pieces[3][at, :].astype(F32)
            )
            out[...] = total.astype(out.dtype)


def middle_sums(where, a, b):
    def shape(kind):
        return jax.ShapeDtypeStruct((CHUNK // 2, COLS), kind)

    return pl.pallas_call(
        middle_kernel,
        out_shape=(shape(F32), shape(BF16), shape(BF16), shape(BF16)) * 2,
        in_specs=[SMEM] + [VMEM] * 8,
        out_specs=(VMEM,) * 8,
        name="middle",
    )(where, *a, *b)


def final_kernel(*refs):
    half = CHUNK // 2
    for part in range(2):
        own, first, second, third = refs[4 * part : 4 * part + 4]
        refs[8][half * part : half * (part + 1), :] = (own[...] + first[...].astype(F32)) + (
            second[...].astype(F32) + third[...].astype(F32)
        )


def final_sums(a, b):
    return pl.pallas_call(
        final_kernel,
        out_shape=jax.ShapeDtypeStruct((CHUNK, COLS), F32),
        in_specs=[VMEM] * 8,
        out_specs=VMEM,
        name="final",
    )(*a, *b)


def body(
    tokens,
    dest_shard,
    dest_offset,
    seg_lengths,
    rewards,
    groups,
    reference_head_weight,
    policy_head_weight,
    upstream,
):
    where = jnp.stack([lax.axis_index(name).astype(I32) for name in ("y", "x", "c", "z")])

    outgoing = route(tokens, dest_shard, dest_offset, rewards, groups)
    arrived = lax.all_to_all(outgoing, ("y", "x", "c"), split_axis=0, concat_axis=0, tiled=True)
    block = place(arrived)

    notes = arrived[:, 0, 256:384]
    advantage = row_advantages(
        notes[:, NOTE_REWARD : NOTE_REWARD + 4],
        notes[:, NOTE_GROUP : NOTE_GROUP + 4],
        rewards,
        groups,
        seg_lengths,
    )

    ref_first = gather_ring(reference_head_weight.reshape(CHUNK, COLS), "x")
    policy_first = gather_ring(policy_head_weight.reshape(CHUNK, COLS), "y")
    ref_rows, policy_rows = first_assembly(where, ref_first, policy_first)
    ref_pieces = gather_ring(ref_rows, "y")
    policy_pieces = gather_ring(policy_rows, "x")

    pieces = [block]
    forward = backward = block
    for _ in range(3):
        forward = shift(forward, "z", 8, 1)
        backward = shift(backward, "z", 8, -1)
        pieces += [forward, backward]
    pieces += [shift(forward[:CHUNK], "z", 8, 1), shift(backward[CHUNK:], "z", 8, -1)]

    own, other, whole = project(where, pieces, ref_pieces, policy_pieces)
    received = lax.ppermute(other, "c", [(0, 1), (1, 0)])
    grad = attention(seg_lengths, own, received, upstream.reshape(ROWS, 3 * HEAD_WIDTH), advantage)
    grad_other = lax.ppermute(grad, "c", [(0, 1), (1, 0)])

    sent = gradient_parts(where, whole, grad, grad_other, (1, -1, 2))
    kept = gradient_parts(where, whole, grad, grad_other, (0,))
    a, b = [kept[0]], [kept[1]]
    for i, move in enumerate((1, -1, 2)):
        a.append(shift(sent[2 * i], "x", 4, move))
        b.append(shift(sent[2 * i + 1], "y", 4, move))
    sums = middle_sums(where, a, b)
    a, b = [sums[0]], [sums[4]]
    for i, move in enumerate((1, -1, 2)):
        a.append(shift(sums[1 + i], "y", 4, move))
        b.append(shift(sums[5 + i], "x", 4, move))
    return final_sums(a, b).reshape(CHUNK, 1, COLS)


def solution(mesh):
    split = Mesh(mesh.devices.reshape(4, 4, 2, 8), ("y", "x", "c", "z"))
    roll = ("y", "x", "c")
    in_specs = (
        P(roll, "z"),
        P(roll),
        P(roll),
        P(roll, None),
        P(roll),
        P(roll),
        P(roll, "z", None),
        P(roll, "z", None),
        P(roll, "z", None),
    )
    out_specs = P(roll, "z", None)
    return jax.shard_map(body, mesh=split, in_specs=in_specs, out_specs=out_specs, check_vma=False)
```

```python
import jax
import jax.numpy as jnp
from jax import lax
from jax.experimental import pallas as pl
from jax.experimental.pallas import tpu as pltpu
from jax.sharding import Mesh
from jax.sharding import PartitionSpec as P

HEAD_WIDTH = 128
KL_WEIGHT = 1.0
MASKED_SCORE = -1e30

ROWS = 384
CHAINS = 1
CAP = 24
MODEL_BLOCK = 640
COLS = 640
CHUNK = 160
HALF = 2 * CHUNK
LANES = 384
F32 = jnp.float32
BF16 = jnp.bfloat16
I32 = jnp.int32

REWARDS, GROUPS, LENGTHS = 4, 8, 12
NOTE_HIGH, NOTE_LOW, NOTE_REWARD, NOTE_GROUP = 64, 65, 66, 70

VMEM = pl.BlockSpec(memory_space=pltpu.VMEM)
SMEM = pl.BlockSpec(memory_space=pltpu.SMEM)
HBM = pl.BlockSpec(memory_space=pltpu.HBM)
PARAMS = pltpu.CompilerParams(vmem_limit_bytes=36 * 1024 * 1024)


def iota(shape, dim):
    return lax.broadcasted_iota(I32, shape, dim)


def dot(a, b, contract=((1,), (0,))):
    return lax.dot_general(a, b, (contract, ((), ())), preferred_element_type=F32)


def fetch(pairs, semaphores):
    copies = [pltpu.make_async_copy(source, to, semaphores.at[i]) for i, (source, to) in enumerate(pairs)]
    for copy in copies:
        copy.start()
    return copies


def shift(value, axis, size, by):
    return lax.ppermute(value, axis, [(i, (i + by) % size) for i in range(size)])


def turned(value, first, by):
    pairs = []
    for y in range(4):
        for x in range(4):
            for c in range(2):
                to_y, to_x = (y, (x + by) % 4) if (c == 0) == first else ((y + by) % 4, x)
                pairs.append((8 * y + 2 * x + c, 8 * to_y + 2 * to_x + c))
    return lax.ppermute(value, ("y", "x", "c"), pairs)


def turned_place(where):
    y, x, odd = where[0], where[1], where[2]
    first = jnp.where(odd == 0, x, y)
    second = jnp.where(odd == 0, y, x)
    stride = jnp.where(odd == 0, 1, 4)
    return first, second, stride, 5 - stride


def wrapped(index, size):
    return lax.rem(index + size, size)


def route_kernel(small, keys, tokens, out, landed, semaphores):
    copy = fetch([(tokens, landed)], semaphores)[0]
    shard_row = keys[0:1, :]
    offset_row = keys[1:2, :]
    table = iota((32, ROWS), 0) == shard_row
    before = (iota((ROWS, ROWS), 0) < iota((ROWS, ROWS), 1)).astype(BF16)
    counts = dot(table.astype(BF16), before)
    rank = jnp.sum(jnp.where(table, counts, 0.0), axis=0, keepdims=True).astype(I32)
    slot = shard_row * CAP + rank
    hot = iota((32 * CAP, ROWS), 0) == slot
    lane = iota((MODEL_BLOCK, 2 * LANES), 1)
    half = (lane >= LANES).astype(I32)
    within = lane - half * LANES
    source = jnp.where(within < CHUNK, within, within + CHUNK) + CHUNK * half
    pick = (iota((MODEL_BLOCK, 2 * LANES), 0) == source) & (within < HALF)
    copy.wait()
    ordered = dot(landed[...], pick.astype(BF16)).astype(BF16)
    gathered = dot(hot.astype(BF16), ordered)
    odd = shard_row & 1
    note_lane = iota((1, 128), 1)
    common = jnp.zeros((1, 128), F32)
    for i in range(4):
        common = jnp.where(note_lane == NOTE_REWARD + i, small[REWARDS + i].astype(F32), common)
        common = jnp.where(note_lane == NOTE_GROUP + i, small[GROUPS + i].astype(F32), common)
    for core in range(2):
        place = offset_row + 1 + ROWS * (odd ^ core)
        mark = jnp.sum(jnp.where(hot, place, 0), axis=1, keepdims=True)
        high = (mark >> 4).astype(F32)
        low = (mark & 15).astype(F32)
        notes = jnp.where(note_lane == NOTE_HIGH, high, jnp.where(note_lane == NOTE_LOW, low, common))
        first = LANES * core
        plain = gathered[:, first : first + 256].astype(BF16)
        last = (gathered[:, first + 256 : first + 384] + notes).astype(BF16)
        for chip in range(16):
            rows = slice(2 * CAP * chip, 2 * CAP * (chip + 1))
            out[2 * chip + core, :, 0:256] = plain[rows]
            out[2 * chip + core, :, 256:384] = last[rows]


def route(small, keys, tokens):
    return pl.pallas_call(
        route_kernel,
        out_shape=jax.ShapeDtypeStruct((32, 2 * CAP, LANES), BF16),
        in_specs=[SMEM, VMEM, HBM],
        out_specs=VMEM,
        scratch_shapes=[pltpu.VMEM((ROWS, MODEL_BLOCK), BF16), pltpu.SemaphoreType.DMA((1,))],
        compiler_params=PARAMS,
        name="route",
    )(small, keys, tokens)


def place_kernel(arrived, *refs):
    outs, (landed, semaphores) = refs[:-2], refs[-2:]
    fetch([(arrived, landed)], semaphores)[0].wait()
    rows = landed[...].reshape(32 * 2 * CAP, LANES)
    notes = rows[:, 256:384].astype(F32)
    note_lane = iota((1, 128), 1)
    weight = jnp.where(note_lane == NOTE_HIGH, 16.0, jnp.where(note_lane == NOTE_LOW, 1.0, 0.0))
    mark = jnp.sum(notes * weight, axis=1, keepdims=True).astype(I32) - 1
    hot = (mark == iota((32 * 2 * CAP, 2 * ROWS), 1)).astype(BF16)
    block = dot(rows, hot, ((0,), (0,))).astype(BF16)
    for i, out in enumerate(outs):
        out[...] = block[i * out.shape[0] : (i + 1) * out.shape[0]]


def place(arrived):
    return pl.pallas_call(
        place_kernel,
        out_shape=(jax.ShapeDtypeStruct((HALF // CHAINS, 2 * ROWS), BF16),) * CHAINS,
        in_specs=[HBM],
        out_specs=(VMEM,) * CHAINS,
        scratch_shapes=[pltpu.VMEM((32, 2 * CAP, LANES), BF16), pltpu.SemaphoreType.DMA((1,))],
        compiler_params=PARAMS,
        name="place",
    )(arrived)


def row_advantages(reward, group, small):
    position = iota((ROWS, 128), 0)
    result = jnp.zeros((ROWS, 128), F32)
    start = 0
    for i in range(4):
        member = group == small[GROUPS + i].astype(F32)
        count = jnp.sum(jnp.where(member, 1.0, 0.0), keepdims=True)
        total = jnp.sum(jnp.where(member, reward, 0.0), keepdims=True)
        square = jnp.sum(jnp.where(member, reward * reward, 0.0), keepdims=True)
        mean = total / count
        spread = jnp.maximum(jnp.sqrt(count * square - total * total) / count, 1.0)
        advantage = (small[REWARDS + i].astype(F32) - mean) / spread
        result = jnp.where(position >= start, advantage, result)
        start = start + small[LENGTHS + i]
    return result


def gather_four(block, first):
    return [block, turned(block, first, 1), turned(block, first, -1), turned(block, first, 2)]


STEPS = (-2, -1, 0, 1, 2, 3, -3, 4)


def slot_of(chunk, z):
    at = wrapped(lax.div(chunk, 2) - z + 2, 8)
    at = jnp.where(at == 6, 7, jnp.where(at == 7, 6, at))
    return pl.multiple_of((2 * at + lax.rem(chunk, 2)) * CHUNK, 16)


def stacked(pieces, whole):
    pairs, at = [], 0
    for piece in pieces:
        pairs.append((piece, whole.at[pl.ds(at, piece.shape[0]), :]))
        at += piece.shape[0]
    return pairs


def project_kernel(where, arrived, *refs):
    tokens, pieces = refs[:-12], refs[-12:-8]
    own, other, late, advantage, whole, weights, notes, semaphores = refs[-8:]
    first, second, first_stride, second_stride = turned_place(where)
    pairs = [(arrived.at[:, 0:16, 256:384], notes), *stacked(tokens, whole)]
    steps = (0, -1, 1, 2)
    for step, piece in zip(steps, pieces):
        for k in range(4):
            chunk = wrapped(first + steps[k], 4) * first_stride + wrapped(second + step, 4) * second_stride
            slot = slot_of(chunk, where[3])
            pairs.append((piece.at[pl.ds(k * CHUNK, CHUNK), :], weights.at[pl.ds(slot, CHUNK), :]))
    copies = fetch(pairs, semaphores)
    copies[0].wait()
    note = notes[:, 0, :].astype(F32)
    advantage[...] = row_advantages(
        note[:, NOTE_REWARD : NOTE_REWARD + 4], note[:, NOTE_GROUP : NOTE_GROUP + 4], where
    )
    for copy in copies[1:]:
        copy.wait()
    late[...] = weights[5 * HALF :, :]
    result = dot(whole[...], weights[: 5 * HALF, :], ((0,), (0,)))
    own[...] = result[:ROWS]
    other[...] = result[ROWS:]


def project(where, arrived, tokens, pieces):
    shape = jax.ShapeDtypeStruct((ROWS, 2 * COLS), F32)
    late = jax.ShapeDtypeStruct((3 * HALF, 2 * COLS), BF16)
    return pl.pallas_call(
        project_kernel,
        out_shape=(shape, shape, late, jax.ShapeDtypeStruct((ROWS, 128), F32)),
        in_specs=[SMEM] + [HBM] * (5 + len(tokens)),
        out_specs=(VMEM,) * 4,
        scratch_shapes=[
            pltpu.VMEM((5 * HALF, 2 * ROWS), BF16),
            pltpu.VMEM((16 * CHUNK, 2 * COLS), BF16),
            pltpu.VMEM((32, 16, 128), BF16),
            pltpu.SemaphoreType.DMA((17 + len(tokens),)),
        ],
        compiler_params=PARAMS,
        name="project",
    )(where, arrived, *tokens, *pieces)


def add_kernel(own, other, late, *refs):
    pieces, (own_out, other_out, tokens, semaphores) = refs[:-4], refs[-4:]
    for copy in fetch(stacked(pieces, tokens), semaphores):
        copy.wait()
    result = dot(tokens[...], late[: 2 * HALF, :], ((0,), (0,)))
    own_out[...] = own[...] + result[:ROWS]
    other_out[...] = other[...] + result[ROWS:]


def add_project(own, other, late, pieces):
    shape = jax.ShapeDtypeStruct((ROWS, 2 * COLS), F32)
    return pl.pallas_call(
        add_kernel,
        out_shape=(shape, shape),
        in_specs=[VMEM] * 3 + [HBM] * len(pieces),
        out_specs=(VMEM,) * 2,
        scratch_shapes=[pltpu.VMEM((2 * HALF, 2 * ROWS), BF16), pltpu.SemaphoreType.DMA((len(pieces),))],
        compiler_params=PARAMS,
        name="add",
    )(own, other, late, *pieces)


def late_kernel(begin, other, late, first, second, out, tokens, semaphores):
    pairs = [(first, tokens.at[pl.ds(0, CHUNK), :]), (second, tokens.at[pl.ds(CHUNK, CHUNK), :])]
    for copy in fetch(pairs, semaphores):
        copy.wait()
    columns = slice(begin, begin + COLS)
    out[...] = other[:, columns] + dot(tokens[:, ROWS:], late[2 * HALF :, columns], ((0,), (0,)))


def late_project(begin, other, late, first, second):
    def kernel(*refs):
        late_kernel(begin, *refs)

    return pl.pallas_call(
        kernel,
        out_shape=jax.ShapeDtypeStruct((ROWS, COLS), F32),
        in_specs=[VMEM] * 2 + [HBM] * 2,
        out_specs=VMEM,
        scratch_shapes=[pltpu.VMEM((HALF, 2 * ROWS), BF16), pltpu.SemaphoreType.DMA((2,))],
        compiler_params=PARAMS,
        name="late",
    )(other, late, first, second)


def collect_kernel(*refs):
    tokens, (whole, semaphores) = refs[:-2], refs[-2:]
    for copy in fetch(stacked(tokens, whole), semaphores):
        copy.wait()


def collect(tokens):
    return pl.pallas_call(
        collect_kernel,
        out_shape=jax.ShapeDtypeStruct((16 * CHUNK, 2 * ROWS), BF16),
        in_specs=[HBM] * len(tokens),
        out_specs=VMEM,
        scratch_shapes=[pltpu.SemaphoreType.DMA((len(tokens),))],
        compiler_params=PARAMS,
        name="collect",
    )(*tokens)


def two_parts(value):
    high = value.astype(BF16)
    return high, (value - high.astype(F32)).astype(BF16)


def heads(value):
    return jnp.concatenate([value[:, 128 * i : 128 * (i + 1)] for i in range(3)], axis=0)


def attend(small, projection):
    key_at = iota((ROWS, ROWS), 1)
    query_at = iota((ROWS, ROWS), 0)
    begin = jnp.zeros((ROWS, 1), I32)
    row_at = iota((ROWS, 1), 0)
    start = 0
    for i in range(4):
        begin = jnp.where(row_at >= start, start, begin)
        start = start + small[LENGTHS + i]
    allowed = (key_at <= query_at) & (key_at >= begin)
    allowed = jnp.concatenate([allowed] * 3, axis=0)
    queries, keys, values = heads(projection), projection[:, 384:512], projection[:, 512:640]
    scores = dot(queries, keys, ((1,), (1,))) * HEAD_WIDTH**-0.5
    scores = jnp.where(allowed, scores, MASKED_SCORE)
    weights = jnp.exp(scores - jnp.max(scores, axis=1, keepdims=True))
    probs = weights / jnp.sum(weights, axis=1, keepdims=True)
    rounded = probs.astype(BF16)
    return queries, keys, values, probs, rounded, dot(rounded, values)


def finish(begin, own, late, first, second, received, tokens, landed, semaphores):
    pairs = [
        (first, tokens.at[pl.ds(0, CHUNK), :]),
        (second, tokens.at[pl.ds(CHUNK, CHUNK), :]),
        (received, landed),
    ]
    copies = fetch(pairs, semaphores)
    copies[0].wait()
    copies[1].wait()
    columns = slice(begin, begin + COLS)
    result = own[:, columns] + dot(tokens[:, :ROWS], late[2 * HALF :, columns], ((0,), (0,)))
    copies[2].wait()
    return (result + landed[...]).astype(BF16)


FINISH = [
    pltpu.VMEM((HALF, 2 * ROWS), BF16),
    pltpu.VMEM((ROWS, COLS), F32),
    pltpu.SemaphoreType.DMA((3,)),
]


def ref_kernel(small, own, late, first, second, received, out, *scratch):
    projection = finish(0, own, late, first, second, received, *scratch)
    out[...] = attend(small, projection)[5]


def ref_attention(small, own, late, first, second, received):
    return pl.pallas_call(
        ref_kernel,
        out_shape=jax.ShapeDtypeStruct((3 * ROWS, HEAD_WIDTH), F32),
        in_specs=[SMEM] + [VMEM] * 2 + [HBM] * 3,
        out_specs=VMEM,
        scratch_shapes=FINISH,
        compiler_params=PARAMS,
        name="ref_attention",
    )(small, own, late, first, second, received)


def two_parts(value):
    high = value.astype(BF16)
    return high, (value - high.astype(F32)).astype(BF16)


def policy_kernel(small, own, late, first, second, received, out_ref, upstream, advantage, out, *scratch):
    scale = HEAD_WIDTH**-0.5
    projection = finish(COLS, own, late, first, second, received, *scratch)
    queries, keys, values, probs, rounded, out_policy = attend(small, projection)
    weight = jnp.concatenate([advantage[...]] * 3, axis=0)
    grad_out = weight * heads(upstream[...].astype(F32)) + KL_WEIGHT * (out_policy - out_ref[...])
    high, low = two_parts(grad_out * 12288**-0.5)
    grad_values = dot(rounded, high, ((0,), (0,))) + dot(rounded, low, ((0,), (0,)))
    grad_probs = dot(high, values, ((1,), (1,))) + dot(low, values, ((1,), (1,)))
    grad_scores = probs * (grad_probs - jnp.sum(grad_probs * probs, axis=1, keepdims=True))
    high, low = two_parts(grad_scores)
    grad_query = (dot(high, keys) + dot(low, keys)) * scale
    grad_keys = (dot(high, queries, ((0,), (0,))) + dot(low, queries, ((0,), (0,)))) * scale
    for i in range(3):
        out[:, 128 * i : 128 * (i + 1)] = grad_query[ROWS * i : ROWS * (i + 1)].astype(BF16)
    out[:, 384:512] = grad_keys.astype(BF16)
    out[:, 512:640] = grad_values.astype(BF16)


def policy_attention(small, own, late, first, second, received, out_ref, upstream, advantage):
    return pl.pallas_call(
        policy_kernel,
        out_shape=jax.ShapeDtypeStruct((ROWS, COLS), BF16),
        in_specs=[SMEM] + [VMEM] * 2 + [HBM] * 3 + [VMEM] * 3,
        out_specs=VMEM,
        scratch_shapes=FINISH,
        compiler_params=PARAMS,
        name="policy_attention",
    )(small, own, late, first, second, received, out_ref, upstream, advantage)


def gradient_dot(move, where, whole, grad):
    first, _, first_stride, second_stride = turned_place(where)
    rows = []
    for k in range(4):
        chunk = wrapped(first + move, 4) * first_stride + k * second_stride
        rows.append(whole[pl.ds(slot_of(chunk, where[3]), CHUNK), :])
    return dot(jnp.concatenate(rows, axis=0), grad).astype(BF16)


PART = jax.ShapeDtypeStruct((4 * CHUNK, COLS), BF16)


def first_gradient(where, whole, own, other, move):
    def kernel(where, whole, own, other, out, grad, semaphores):
        copy = fetch([(other, grad.at[pl.ds(ROWS, ROWS), :])], semaphores)[0]
        grad[0:ROWS, :] = own[...]
        copy.wait()
        out[...] = gradient_dot(move, where, whole, grad[...])

    return pl.pallas_call(
        kernel,
        out_shape=(PART, jax.ShapeDtypeStruct((2 * ROWS, COLS), BF16)),
        in_specs=[SMEM, VMEM, VMEM, HBM],
        out_specs=(VMEM, VMEM),
        scratch_shapes=[pltpu.SemaphoreType.DMA((1,))],
        compiler_params=PARAMS,
        name="gradient",
    )(where, whole, own, other)


def next_gradient(where, whole, grad, move):
    def kernel(where, whole, grad, out):
        out[...] = gradient_dot(move, where, whole, grad[...])

    return pl.pallas_call(
        kernel,
        out_shape=PART,
        in_specs=[SMEM, VMEM, VMEM],
        out_specs=VMEM,
        compiler_params=PARAMS,
        name="gradient",
    )(where, whole, grad)


def middle_kernel(where, own, *refs):
    pieces, outs, landed, semaphores = refs[:3], refs[3:7], refs[7], refs[8]
    second = turned_place(where)[1]
    copies = fetch([(piece, landed.at[i]) for i, piece in enumerate(pieces)], semaphores)
    for copy in copies:
        copy.wait()
    for move, out in zip((0, 1, -1, 2), outs):
        at = pl.ds(pl.multiple_of(wrapped(second + move, 4) * CHUNK, 16), CHUNK)
        total = (own[at, :].astype(F32) + landed[0, at, :].astype(F32)) + (
            landed[1, at, :].astype(F32) + landed[2, at, :].astype(F32)
        )
        out[...] = total.astype(out.dtype)


def middle_sums(where, own, pieces):
    def shape(kind):
        return jax.ShapeDtypeStruct((CHUNK, COLS), kind)

    return pl.pallas_call(
        middle_kernel,
        out_shape=(shape(F32), shape(BF16), shape(BF16), shape(BF16)),
        in_specs=[SMEM, VMEM] + [HBM] * 3,
        out_specs=(VMEM,) * 4,
        scratch_shapes=[pltpu.VMEM((3, 4 * CHUNK, COLS), BF16), pltpu.SemaphoreType.DMA((3,))],
        compiler_params=PARAMS,
        name="middle",
    )(where, own, *pieces)


def final_kernel(own, *refs):
    pieces, out, landed, semaphores = refs[:3], refs[3], refs[4], refs[5]
    for copy in fetch([(piece, landed.at[i]) for i, piece in enumerate(pieces)], semaphores):
        copy.wait()
    out[:, 0, :] = (own[...] + landed[0].astype(F32)) + (landed[1].astype(F32) + landed[2].astype(F32))


def final_sums(own, pieces):
    return pl.pallas_call(
        final_kernel,
        out_shape=jax.ShapeDtypeStruct((CHUNK, 1, COLS), F32),
        in_specs=[VMEM] + [HBM] * 3,
        out_specs=VMEM,
        scratch_shapes=[pltpu.VMEM((3, CHUNK, COLS), BF16), pltpu.SemaphoreType.DMA((3,))],
        compiler_params=PARAMS,
        name="final",
    )(own, *pieces)


def body(
    tokens,
    dest_shard,
    dest_offset,
    seg_lengths,
    rewards,
    groups,
    reference_head_weight,
    policy_head_weight,
    upstream,
):
    where = jnp.stack([lax.axis_index(name).astype(I32) for name in ("y", "x", "c", "z")])
    small = jnp.concatenate([where, rewards, groups, seg_lengths[0]])
    outgoing = route(small, jnp.stack([dest_shard, dest_offset]), tokens)
    outgoing, reference_head_weight, policy_head_weight = lax.optimization_barrier(
        (outgoing, reference_head_weight, policy_head_weight)
    )
    arrived = lax.all_to_all(outgoing, ("y", "x", "c"), split_axis=0, concat_axis=0, tiled=True)

    weights = jnp.concatenate([reference_head_weight[:, 0], policy_head_weight[:, 0]], axis=1)
    near = gather_four(weights, True)
    block = place(arrived)
    block, near = lax.optimization_barrier((block, near))
    weights = gather_four(jnp.concatenate(near, axis=0), False)

    forward, backward = [block], [block]
    for _ in range(3):
        forward.append([shift(piece, "z", 8, 1) for piece in forward[-1]])
        backward.append([shift(piece, "z", 8, -1) for piece in backward[-1]])
    if CHAINS == 1:
        first = shift(forward[3][0][:CHUNK], "z", 8, 1)
        second = shift(backward[3][0][CHUNK:], "z", 8, -1)
    else:
        first = shift(forward[3][0], "z", 8, 1)
        second = shift(backward[3][1], "z", 8, -1)

    near = [*forward[2], *forward[1], *forward[0], *backward[1], *backward[2]]
    far = [*backward[3], *forward[3]]
    own, other, late, advantage = project(small, arrived, near, weights)
    own, other = add_project(own, other, late, far)
    received = []
    for begin in (0, COLS):
        part = late_project(begin, other, late, first, second)
        received.append(lax.ppermute(part, "c", [(0, 1), (1, 0)]))
    whole = collect([*near, *far, first, second])
    out_ref = ref_attention(small, own, late, first, second, received[0])
    cotangent = upstream.reshape(ROWS, 3 * HEAD_WIDTH)
    grad = policy_attention(
        small, own, late, first, second, received[1], out_ref, cotangent, advantage
    )
    grad_other = lax.ppermute(grad, "c", [(0, 1), (1, 0)])

    part, grad = first_gradient(small, whole, grad, grad_other, 2)
    parts = [turned(part, True, 2)]
    for move in (1, -1):
        parts.append(turned(next_gradient(small, whole, grad, move), True, move))
    sums = middle_sums(small, next_gradient(small, whole, grad, 0), parts)
    parts = [turned(part, False, move) for move, part in zip((1, -1, 2), sums[1:])]
    return final_sums(sums[0], parts)


def solution(mesh):
    split = Mesh(mesh.devices.reshape(4, 4, 2, 8), ("y", "x", "c", "z"))
    roll = ("y", "x", "c")
    in_specs = (
        P(roll, "z"),
        P(roll),
        P(roll),
        P(roll, None),
        P(roll),
        P(roll),
        P(roll, "z", None),
        P(roll, "z", None),
        P(roll, "z", None),
    )
    out_specs = P(roll, "z", None)
    return jax.shard_map(body, mesh=split, in_specs=in_specs, out_specs=out_specs, check_vma=False)
```

```python
import jax
import jax.numpy as jnp
from jax import lax
from jax.experimental import pallas as pl
from jax.experimental.pallas import tpu as pltpu
from jax.sharding import Mesh
from jax.sharding import PartitionSpec as P

HEAD_WIDTH = 128
KL_WEIGHT = 1.0
MASKED_SCORE = -1e30

ROWS = 384
CAP = 24
MODEL_BLOCK = 640
COLS = 640
CHUNK = 160
HALF = 2 * CHUNK
LANES = 384
F32 = jnp.float32
BF16 = jnp.bfloat16
I32 = jnp.int32

REWARDS, GROUPS, LENGTHS = 4, 8, 12
NOTE_HIGH, NOTE_LOW, NOTE_REWARD, NOTE_GROUP = 64, 65, 66, 70

VMEM = pl.BlockSpec(memory_space=pltpu.VMEM)
SMEM = pl.BlockSpec(memory_space=pltpu.SMEM)
HBM = pl.BlockSpec(memory_space=pltpu.HBM)
ALONE = pltpu.CompilerParams(vmem_limit_bytes=60 * 1024 * 1024)
PARAMS = pltpu.CompilerParams(vmem_limit_bytes=36 * 1024 * 1024)


def iota(shape, dim):
    return lax.broadcasted_iota(I32, shape, dim)


def dot(a, b, contract=((1,), (0,))):
    return lax.dot_general(a, b, (contract, ((), ())), preferred_element_type=F32)


def fetch(pairs, semaphores):
    copies = [pltpu.make_async_copy(source, to, semaphores.at[i]) for i, (source, to) in enumerate(pairs)]
    for copy in copies:
        copy.start()
    return copies


def shift(value, axis, size, by):
    return lax.ppermute(value, axis, [(i, (i + by) % size) for i in range(size)])


def turned(value, first, by):
    pairs = []
    for y in range(4):
        for x in range(4):
            for c in range(2):
                to_y, to_x = (y, (x + by) % 4) if (c == 0) == first else ((y + by) % 4, x)
                pairs.append((8 * y + 2 * x + c, 8 * to_y + 2 * to_x + c))
    return lax.ppermute(value, ("y", "x", "c"), pairs)


def turned_place(where):
    y, x, odd = where[0], where[1], where[2]
    first = jnp.where(odd == 0, x, y)
    second = jnp.where(odd == 0, y, x)
    stride = jnp.where(odd == 0, 1, 4)
    return first, second, stride, 5 - stride


def wrapped(index, size):
    return lax.rem(index + size, size)


def route_kernel(rewards, groups, shard, offset, tokens, out, landed, semaphores):
    copy = fetch([(tokens, landed)], semaphores)[0]
    shard_row = shard[...].reshape(1, ROWS)
    offset_row = offset[...].reshape(1, ROWS)
    table = iota((32, ROWS), 0) == shard_row
    before = (iota((ROWS, ROWS), 0) < iota((ROWS, ROWS), 1)).astype(BF16)
    counts = dot(table.astype(BF16), before)
    rank = jnp.sum(jnp.where(table, counts, 0.0), axis=0, keepdims=True).astype(I32)
    slot = shard_row * CAP + rank
    hot = iota((32 * CAP, ROWS), 0) == slot
    lane = iota((MODEL_BLOCK, 2 * LANES), 1)
    half = (lane >= LANES).astype(I32)
    within = lane - half * LANES
    source = jnp.where(within < CHUNK, within, within + CHUNK) + CHUNK * half
    pick = (iota((MODEL_BLOCK, 2 * LANES), 0) == source) & (within < HALF)
    copy.wait()
    ordered = dot(landed[...], pick.astype(BF16)).astype(BF16)
    gathered = dot(hot.astype(BF16), ordered)
    odd = shard_row & 1
    note_lane = iota((1, 128), 1)
    common = jnp.zeros((1, 128), F32)
    for i in range(4):
        common = jnp.where(note_lane == NOTE_REWARD + i, rewards[i].astype(F32), common)
        common = jnp.where(note_lane == NOTE_GROUP + i, groups[i].astype(F32), common)
    for core in range(2):
        place = offset_row + 1 + ROWS * (odd ^ core)
        mark = jnp.sum(jnp.where(hot, place, 0), axis=1, keepdims=True)
        high = (mark >> 4).astype(F32)
        low = (mark & 15).astype(F32)
        notes = jnp.where(note_lane == NOTE_HIGH, high, jnp.where(note_lane == NOTE_LOW, low, common))
        first = LANES * core
        plain = gathered[:, first : first + 256].astype(BF16)
        last = (gathered[:, first + 256 : first + 384] + notes).astype(BF16)
        for chip in range(16):
            rows = slice(2 * CAP * chip, 2 * CAP * (chip + 1))
            out[2 * chip + core, :, 0:256] = plain[rows]
            out[2 * chip + core, :, 256:384] = last[rows]


def route(rewards, groups, shard, offset, tokens):
    return pl.pallas_call(
        route_kernel,
        out_shape=jax.ShapeDtypeStruct((32, 2 * CAP, LANES), BF16),
        in_specs=[SMEM, SMEM, VMEM, VMEM, HBM],
        out_specs=VMEM,
        scratch_shapes=[pltpu.VMEM((ROWS, MODEL_BLOCK), BF16), pltpu.SemaphoreType.DMA((1,))],
        compiler_params=ALONE,
        name="route",
    )(rewards, groups, shard, offset, tokens)


def place_kernel(arrived, out, landed, semaphores):
    fetch([(arrived, landed)], semaphores)[0].wait()
    rows = landed[...].reshape(32 * 2 * CAP, LANES)
    notes = rows[:, 256:384].astype(F32)
    note_lane = iota((1, 128), 1)
    weight = jnp.where(note_lane == NOTE_HIGH, 16.0, jnp.where(note_lane == NOTE_LOW, 1.0, 0.0))
    mark = jnp.sum(notes * weight, axis=1, keepdims=True).astype(I32) - 1
    hot = (mark == iota((32 * 2 * CAP, 2 * ROWS), 1)).astype(BF16)
    out[...] = dot(rows, hot, ((0,), (0,)))[:HALF].astype(BF16)


def place(arrived):
    return pl.pallas_call(
        place_kernel,
        out_shape=jax.ShapeDtypeStruct((HALF, 2 * ROWS), BF16),
        in_specs=[HBM],
        out_specs=VMEM,
        scratch_shapes=[pltpu.VMEM((32, 2 * CAP, LANES), BF16), pltpu.SemaphoreType.DMA((1,))],
        compiler_params=PARAMS,
        name="place",
    )(arrived)


def row_advantages(reward, group, small):
    position = iota((ROWS, 128), 0)
    result = jnp.zeros((ROWS, 128), F32)
    start = 0
    for i in range(4):
        member = group == small[GROUPS + i].astype(F32)
        count = jnp.sum(jnp.where(member, 1.0, 0.0), keepdims=True)
        total = jnp.sum(jnp.where(member, reward, 0.0), keepdims=True)
        square = jnp.sum(jnp.where(member, reward * reward, 0.0), keepdims=True)
        mean = total / count
        spread = jnp.maximum(jnp.sqrt(count * square - total * total) / count, 1.0)
        advantage = (small[REWARDS + i].astype(F32) - mean) / spread
        result = jnp.where(position >= start, advantage, result)
        start = start + small[LENGTHS + i]
    return result


def join_kernel(*refs):
    pieces, (out, semaphores) = refs[:4], refs[4:]
    for copy in fetch(stacked(pieces, out), semaphores):
        copy.wait()


def join(pieces):
    return pl.pallas_call(
        join_kernel,
        out_shape=jax.ShapeDtypeStruct((4 * CHUNK, 2 * COLS), BF16),
        in_specs=[HBM] * 4,
        out_specs=VMEM,
        scratch_shapes=[pltpu.SemaphoreType.DMA((4,))],
        compiler_params=PARAMS,
        name="join",
    )(*pieces)


STEPS = (-2, -1, 0, 1, 2, 3, -3, 4)


def slot_of(chunk, z):
    at = wrapped(lax.div(chunk, 2) - z + 2, 8)
    at = jnp.where(at == 6, 7, jnp.where(at == 7, 6, at))
    return pl.multiple_of((2 * at + lax.rem(chunk, 2)) * CHUNK, 16)


def stacked(pieces, whole):
    pairs, at = [], 0
    for piece in pieces:
        pairs.append((piece, whole.at[pl.ds(at, piece.shape[0]), :]))
        at += piece.shape[0]
    return pairs


def project_kernel(where, arrived, *refs):
    tokens, pieces = refs[:7], refs[7:11]
    own, other, late, advantage, whole, weights, notes, semaphores = refs[11:]
    first, second, first_stride, second_stride = turned_place(where)
    pairs = [(arrived.at[:, 0:16, 256:384], notes)]
    steps = (0, -1, 1, 2)
    for step, piece in zip(steps, pieces):
        for k in range(4):
            near = wrapped(first + steps[k], 4)
            chunk = near * first_stride + wrapped(second + step, 4) * second_stride
            slot = slot_of(chunk, where[3])
            pairs.append((piece.at[pl.ds(k * CHUNK, CHUNK), :], weights.at[pl.ds(slot, CHUNK), :]))
    copies = fetch(pairs + stacked(tokens, whole), semaphores)
    copies[0].wait()
    note = notes[:, 0, :].astype(F32)
    advantage[...] = row_advantages(
        note[:, NOTE_REWARD : NOTE_REWARD + 4], note[:, NOTE_GROUP : NOTE_GROUP + 4], where
    )
    for copy in copies[1:]:
        copy.wait()
    late[...] = weights[7 * HALF :, :]
    own[...] = dot(whole[:, :ROWS], weights[: 7 * HALF, :], ((0,), (0,)))
    other[...] = dot(whole[:, ROWS:], weights[: 7 * HALF, :], ((0,), (0,)))


def project(where, arrived, tokens, pieces):
    shape = jax.ShapeDtypeStruct((ROWS, 2 * COLS), F32)
    late = jax.ShapeDtypeStruct((HALF, 2 * COLS), BF16)
    whole = jax.ShapeDtypeStruct((7 * HALF, 2 * ROWS), BF16)
    return pl.pallas_call(
        project_kernel,
        out_shape=(shape, shape, late, jax.ShapeDtypeStruct((ROWS, 128), F32), whole),
        in_specs=[SMEM] + [HBM] * 12,
        out_specs=(VMEM,) * 5,
        scratch_shapes=[
            pltpu.VMEM((16 * CHUNK, 2 * COLS), BF16),
            pltpu.VMEM((32, 16, 128), BF16),
            pltpu.SemaphoreType.DMA((24,)),
        ],
        compiler_params=PARAMS,
        name="project",
    )(where, arrived, *tokens, *pieces)


def first_late(other, late, first, second):
    def kernel(other, late, first, second, out, tokens, semaphores):
        for copy in fetch(stacked([first, second], tokens), semaphores):
            copy.wait()
        out[...] = other[:, :COLS] + dot(tokens[:, ROWS:], late[:, :COLS], ((0,), (0,)))

    return pl.pallas_call(
        kernel,
        out_shape=(
            jax.ShapeDtypeStruct((ROWS, COLS), F32),
            jax.ShapeDtypeStruct((HALF, 2 * ROWS), BF16),
        ),
        in_specs=[VMEM] * 2 + [HBM] * 2,
        out_specs=(VMEM,) * 2,
        scratch_shapes=[pltpu.SemaphoreType.DMA((2,))],
        compiler_params=PARAMS,
        name="late",
    )(other, late, first, second)


def second_late(other, late, tokens):
    def kernel(other, late, tokens, out):
        out[...] = other[:, COLS:] + dot(tokens[:, ROWS:], late[:, COLS:], ((0,), (0,)))

    return pl.pallas_call(
        kernel,
        out_shape=jax.ShapeDtypeStruct((ROWS, COLS), F32),
        in_specs=[VMEM] * 3,
        out_specs=VMEM,
        compiler_params=PARAMS,
        name="late",
    )(other, late, tokens)


def heads(value):
    return jnp.concatenate([value[:, 128 * i : 128 * (i + 1)] for i in range(3)], axis=0)


def attend(small, projection, block):
    first, count = 128 * block, 128 * (block + 1)
    key_at = iota((128, count), 1)
    query_at = first + iota((128, count), 0)
    row_at = first + iota((128, 1), 0)
    begin = jnp.zeros((128, 1), I32)
    start = 0
    for i in range(4):
        begin = jnp.where(row_at >= start, start, begin)
        start = start + small[LENGTHS + i]
    allowed = (key_at <= query_at) & (key_at >= begin)
    allowed = jnp.concatenate([allowed] * 3, axis=0)
    queries = heads(projection[first:count, 0:384])
    keys, values = projection[:count, 384:512], projection[:count, 512:640]
    scores = dot(queries, keys, ((1,), (1,))) * HEAD_WIDTH**-0.5
    scores = jnp.where(allowed, scores, MASKED_SCORE)
    weights = jnp.exp(scores - jnp.max(scores, axis=1, keepdims=True))
    probs = weights / jnp.sum(weights, axis=1, keepdims=True)
    rounded = probs.astype(BF16)
    return queries, keys, values, probs, rounded, dot(rounded, values)


def finish(begin, own, late, tokens, received, landed, semaphores):
    copy = fetch([(received, landed)], semaphores)[0]
    columns = slice(begin, begin + COLS)
    result = own[:, columns] + dot(tokens[:, :ROWS], late[:, columns], ((0,), (0,)))
    copy.wait()
    return (result + landed[...]).astype(BF16)


FINISH = [pltpu.VMEM((ROWS, COLS), F32), pltpu.SemaphoreType.DMA((1,))]


def ref_kernel(small, own, late, tokens, received, out, *scratch):
    projection = finish(0, own, late, tokens, received, *scratch)
    for block in range(3):
        out[ROWS * block : ROWS * (block + 1), :] = attend(small, projection, block)[5]


def ref_attention(small, own, late, tokens, received):
    return pl.pallas_call(
        ref_kernel,
        out_shape=jax.ShapeDtypeStruct((3 * ROWS, HEAD_WIDTH), F32),
        in_specs=[SMEM] + [VMEM] * 3 + [HBM],
        out_specs=VMEM,
        scratch_shapes=FINISH,
        compiler_params=PARAMS,
        name="ref_attention",
    )(small, own, late, tokens, received)


def two_parts(value):
    high = value.astype(BF16)
    return high, (value - high.astype(F32)).astype(BF16)


def policy_kernel(small, own, late, last, received, out_ref, upstream, advantage, *refs):
    out, scratch = refs[0], refs[1:]
    scale = HEAD_WIDTH**-0.5
    projection = finish(COLS, own, late, last, received, *scratch)
    grad_keys, grad_values = [0.0] * 3, [0.0] * 3
    for block in range(3):
        rows = slice(128 * block, 128 * (block + 1))
        queries, keys, values, probs, rounded, out_policy = attend(small, projection, block)
        weight = jnp.concatenate([advantage[rows, :]] * 3, axis=0)
        grad_out = weight * heads(upstream[rows, :].astype(F32))
        grad_out = grad_out + KL_WEIGHT * (out_policy - out_ref[ROWS * block : ROWS * (block + 1), :])
        high, low = two_parts(grad_out * 12288**-0.5)
        grad_probs = dot(high, values, ((1,), (1,))) + dot(low, values, ((1,), (1,)))
        grad_scores = probs * (grad_probs - jnp.sum(grad_probs * probs, axis=1, keepdims=True))
        grad_scores = (grad_scores * scale).astype(BF16)
        grad_query = dot(grad_scores, keys)
        for i in range(3):
            out[rows, 128 * i : 128 * (i + 1)] = grad_query[128 * i : 128 * (i + 1)].astype(BF16)
        for_keys = dot(grad_scores, queries, ((0,), (0,)))
        for_values = dot(rounded, high, ((0,), (0,)))
        for k in range(block + 1):
            grad_keys[k] = grad_keys[k] + for_keys[128 * k : 128 * (k + 1)]
            grad_values[k] = grad_values[k] + for_values[128 * k : 128 * (k + 1)]
    for k in range(3):
        out[128 * k : 128 * (k + 1), 384:512] = grad_keys[k].astype(BF16)
        out[128 * k : 128 * (k + 1), 512:640] = grad_values[k].astype(BF16)


def policy_attention(small, own, late, last, received, out_ref, upstream, advantage):
    return pl.pallas_call(
        policy_kernel,
        out_shape=jax.ShapeDtypeStruct((ROWS, COLS), BF16),
        in_specs=[SMEM] + [VMEM] * 3 + [HBM] + [VMEM] * 3,
        out_specs=VMEM,
        scratch_shapes=FINISH,
        compiler_params=PARAMS,
        name="policy_attention",
    )(small, own, late, last, received, out_ref, upstream, advantage)


def gradient_dot(move, where, whole, last, grad):
    first, _, first_stride, second_stride = turned_place(where)
    rows = []
    for k in range(4):
        chunk = wrapped(first + move, 4) * first_stride + k * second_stride
        slot = slot_of(chunk, where[3])
        late = slot >= 7 * HALF
        early = whole[pl.ds(pl.multiple_of(jnp.where(late, 0, slot), 16), CHUNK), :]
        later = last[pl.ds(pl.multiple_of(lax.rem(chunk, 2) * CHUNK, 16), CHUNK), :]
        rows.append(jnp.where(late, later, early))
    return dot(jnp.concatenate(rows, axis=0), grad).astype(BF16)


PART = jax.ShapeDtypeStruct((4 * CHUNK, COLS), BF16)


def first_gradient(where, whole, last, own, other, move):
    def kernel(where, whole, last, own, other, out, grad, semaphores):
        copy = fetch([(other, grad.at[pl.ds(ROWS, ROWS), :])], semaphores)[0]
        grad[0:ROWS, :] = own[...]
        copy.wait()
        out[...] = gradient_dot(move, where, whole, last, grad[...])

    return pl.pallas_call(
        kernel,
        out_shape=(PART, jax.ShapeDtypeStruct((2 * ROWS, COLS), BF16)),
        in_specs=[SMEM, VMEM, VMEM, VMEM, HBM],
        out_specs=(VMEM, VMEM),
        scratch_shapes=[pltpu.SemaphoreType.DMA((1,))],
        compiler_params=PARAMS,
        name="gradient",
    )(where, whole, last, own, other)


def next_gradient(where, whole, last, grad, move):
    def kernel(where, whole, last, grad, out):
        out[...] = gradient_dot(move, where, whole, last, grad[...])

    return pl.pallas_call(
        kernel,
        out_shape=PART,
        in_specs=[SMEM, VMEM, VMEM, VMEM],
        out_specs=VMEM,
        compiler_params=PARAMS,
        name="gradient",
    )(where, whole, last, grad)


def middle_kernel(where, own, *refs):
    pieces, outs, landed, semaphores = refs[:3], refs[3:7], refs[7], refs[8]
    second = turned_place(where)[1]
    copies = fetch([(piece, landed.at[i]) for i, piece in enumerate(pieces)], semaphores)
    for copy in copies:
        copy.wait()
    for move, out in zip((0, 1, -1, 2), outs):
        at = pl.ds(pl.multiple_of(wrapped(second + move, 4) * CHUNK, 16), CHUNK)
        total = (own[at, :].astype(F32) + landed[0, at, :].astype(F32)) + (
            landed[1, at, :].astype(F32) + landed[2, at, :].astype(F32)
        )
        out[...] = total.astype(out.dtype)


def middle_sums(where, own, pieces):
    def shape(kind):
        return jax.ShapeDtypeStruct((CHUNK, COLS), kind)

    return pl.pallas_call(
        middle_kernel,
        out_shape=(shape(F32), shape(BF16), shape(BF16), shape(BF16)),
        in_specs=[SMEM, VMEM] + [HBM] * 3,
        out_specs=(VMEM,) * 4,
        scratch_shapes=[pltpu.VMEM((3, 4 * CHUNK, COLS), BF16), pltpu.SemaphoreType.DMA((3,))],
        compiler_params=PARAMS,
        name="middle",
    )(where, own, *pieces)


def final_kernel(own, *refs):
    pieces, out, landed, semaphores = refs[:3], refs[3], refs[4], refs[5]
    for copy in fetch([(piece, landed.at[i]) for i, piece in enumerate(pieces)], semaphores):
        copy.wait()
    out[:, 0, :] = (own[...] + landed[0].astype(F32)) + (landed[1].astype(F32) + landed[2].astype(F32))


def final_sums(own, pieces):
    return pl.pallas_call(
        final_kernel,
        out_shape=jax.ShapeDtypeStruct((CHUNK, 1, COLS), F32),
        in_specs=[VMEM] + [HBM] * 3,
        out_specs=VMEM,
        scratch_shapes=[pltpu.VMEM((3, CHUNK, COLS), BF16), pltpu.SemaphoreType.DMA((3,))],
        compiler_params=PARAMS,
        name="final",
    )(own, *pieces)


def body(
    tokens,
    dest_shard,
    dest_offset,
    seg_lengths,
    rewards,
    groups,
    reference_head_weight,
    policy_head_weight,
    upstream,
):
    where = jnp.stack([lax.axis_index(name).astype(I32) for name in ("y", "x", "c", "z")])
    small = jnp.concatenate([where, rewards, groups, seg_lengths[0]])
    outgoing = route(rewards, groups, dest_shard, dest_offset, tokens)
    arrived = lax.all_to_all(outgoing, ("y", "x", "c"), split_axis=0, concat_axis=0, tiled=True)
    arrived, small = lax.optimization_barrier((arrived, small))
    _, weights, policy_weights = lax.optimization_barrier(
        (outgoing, reference_head_weight[:, 0], policy_head_weight[:, 0])
    )
    weights = jnp.concatenate([weights, policy_weights], axis=1)
    near = [weights, *(turned(weights, True, by) for by in (1, -1, 2))]
    block = place(arrived)
    _, near = lax.optimization_barrier((block, near))
    rows = join(near)
    weights = [rows, *(turned(rows, False, by) for by in (1, -1, 2))]

    forward, backward = [block], [block]
    for _ in range(3):
        forward.append(shift(forward[-1], "z", 8, 1))
        backward.append(shift(backward[-1], "z", 8, -1))

    first = shift(forward[3][:CHUNK], "z", 8, 1)
    second = shift(backward[3][CHUNK:], "z", 8, -1)
    ring = [forward[2], forward[1], block, backward[1], backward[2], backward[3], forward[3]]
    own, other, late, advantage, whole = project(small, arrived, ring, weights)
    swap = [(0, 1), (1, 0)]
    part, last = first_late(other, late, first, second)
    received_ref = lax.ppermute(part, "c", swap)
    received_policy = lax.ppermute(second_late(other, late, last), "c", swap)
    out_ref = ref_attention(small, own, late, last, received_ref)
    cotangent = upstream.reshape(ROWS, 3 * HEAD_WIDTH)
    grad = policy_attention(small, own, late, last, received_policy, out_ref, cotangent, advantage)
    grad_other = lax.ppermute(grad, "c", swap)

    part, grad = first_gradient(small, whole, last, grad, grad_other, 2)
    parts = [turned(part, True, 2)]
    for move in (1, -1):
        parts.append(turned(next_gradient(small, whole, last, grad, move), True, move))
    sums = middle_sums(small, next_gradient(small, whole, last, grad, 0), parts)
    parts = [turned(part, False, move) for move, part in zip((1, -1, 2), sums[1:])]
    return final_sums(sums[0], parts)


def solution(mesh):
    split = Mesh(mesh.devices.reshape(4, 4, 2, 8), ("y", "x", "c", "z"))
    roll = ("y", "x", "c")
    in_specs = (
        P(roll, "z"),
        P(roll),
        P(roll),
        P(roll, None),
        P(roll),
        P(roll),
        P(roll, "z", None),
        P(roll, "z", None),
        P(roll, "z", None),
    )
    out_specs = P(roll, "z", None)
    return jax.shard_map(body, mesh=split, in_specs=in_specs, out_specs=out_specs, check_vma=False)
```

```python
import jax
import jax.numpy as jnp
from jax import lax
from jax.experimental import pallas as pl
from jax.experimental.pallas import tpu as pltpu
from jax.sharding import Mesh
from jax.sharding import PartitionSpec as P

HEAD_WIDTH = 128
KL_WEIGHT = 1.0
MASKED_SCORE = -1e30

ROWS = 384
CAP = 24
MODEL_BLOCK = 640
COLS = 640
CHUNK = 160
HALF = 2 * CHUNK
LANES = 384
F32 = jnp.float32
BF16 = jnp.bfloat16
I32 = jnp.int32

REWARDS, GROUPS, LENGTHS = 4, 8, 12
NOTE_HIGH, NOTE_LOW, NOTE_REWARD, NOTE_GROUP = 64, 65, 66, 70

VMEM = pl.BlockSpec(memory_space=pltpu.VMEM)
SMEM = pl.BlockSpec(memory_space=pltpu.SMEM)
HBM = pl.BlockSpec(memory_space=pltpu.HBM)
ALONE = pltpu.CompilerParams(vmem_limit_bytes=60 * 1024 * 1024)
PARAMS = pltpu.CompilerParams(vmem_limit_bytes=28 * 1024 * 1024)


def iota(shape, dim):
    return lax.broadcasted_iota(I32, shape, dim)


def dot(a, b, contract=((1,), (0,))):
    return lax.dot_general(a, b, (contract, ((), ())), preferred_element_type=F32)


def fetch(pairs, semaphores):
    copies = [pltpu.make_async_copy(source, to, semaphores.at[i]) for i, (source, to) in enumerate(pairs)]
    for copy in copies:
        copy.start()
    return copies


def shift(value, axis, size, by):
    return lax.ppermute(value, axis, [(i, (i + by) % size) for i in range(size)])


def turned(value, first, by):
    pairs = []
    for y in range(4):
        for x in range(4):
            for c in range(2):
                to_y, to_x = (y, (x + by) % 4) if (c == 0) == first else ((y + by) % 4, x)
                pairs.append((8 * y + 2 * x + c, 8 * to_y + 2 * to_x + c))
    return lax.ppermute(value, ("y", "x", "c"), pairs)


def turned_place(where):
    y, x, odd = where[0], where[1], where[2]
    first = jnp.where(odd == 0, x, y)
    second = jnp.where(odd == 0, y, x)
    stride = jnp.where(odd == 0, 1, 4)
    return first, second, stride, 5 - stride


def wrapped(index, size):
    return lax.rem(index + size, size)


def route_kernel(rewards, groups, shard, offset, tokens, out, landed, semaphores):
    copy = fetch([(tokens, landed)], semaphores)[0]
    shard_row = shard[...].reshape(1, ROWS)
    offset_row = offset[...].reshape(1, ROWS)
    table = iota((32, ROWS), 0) == shard_row
    before = (iota((ROWS, ROWS), 0) < iota((ROWS, ROWS), 1)).astype(BF16)
    counts = dot(table.astype(BF16), before)
    rank = jnp.sum(jnp.where(table, counts, 0.0), axis=0, keepdims=True).astype(I32)
    slot = shard_row * CAP + rank
    hot = iota((32 * CAP, ROWS), 0) == slot
    lane = iota((MODEL_BLOCK, 2 * LANES), 1)
    half = (lane >= LANES).astype(I32)
    within = lane - half * LANES
    source = jnp.where(within < CHUNK, within, within + CHUNK) + CHUNK * half
    pick = (iota((MODEL_BLOCK, 2 * LANES), 0) == source) & (within < HALF)
    copy.wait()
    ordered = dot(landed[...], pick.astype(BF16)).astype(BF16)
    gathered = dot(hot.astype(BF16), ordered)
    odd = shard_row & 1
    note_lane = iota((1, 128), 1)
    common = jnp.zeros((1, 128), F32)
    for i in range(4):
        common = jnp.where(note_lane == NOTE_REWARD + i, rewards[i].astype(F32), common)
        common = jnp.where(note_lane == NOTE_GROUP + i, groups[i].astype(F32), common)
    for core in range(2):
        place = offset_row + 1 + ROWS * (odd ^ core)
        mark = jnp.sum(jnp.where(hot, place, 0), axis=1, keepdims=True)
        high = (mark >> 4).astype(F32)
        low = (mark & 15).astype(F32)
        notes = jnp.where(note_lane == NOTE_HIGH, high, jnp.where(note_lane == NOTE_LOW, low, common))
        first = LANES * core
        plain = gathered[:, first : first + 256].astype(BF16)
        last = (gathered[:, first + 256 : first + 384] + notes).astype(BF16)
        for chip in range(16):
            rows = slice(2 * CAP * chip, 2 * CAP * (chip + 1))
            out[2 * chip + core, :, 0:256] = plain[rows]
            out[2 * chip + core, :, 256:384] = last[rows]


def route(rewards, groups, shard, offset, tokens):
    return pl.pallas_call(
        route_kernel,
        out_shape=jax.ShapeDtypeStruct((32, 2 * CAP, LANES), BF16),
        in_specs=[SMEM, SMEM, VMEM, VMEM, HBM],
        out_specs=VMEM,
        scratch_shapes=[pltpu.VMEM((ROWS, MODEL_BLOCK), BF16), pltpu.SemaphoreType.DMA((1,))],
        compiler_params=ALONE,
        name="route",
    )(rewards, groups, shard, offset, tokens)


def place_kernel(arrived, out, landed, semaphores):
    fetch([(arrived, landed)], semaphores)[0].wait()
    rows = landed[...].reshape(32 * 2 * CAP, LANES)
    notes = rows[:, 256:384].astype(F32)
    note_lane = iota((1, 128), 1)
    weight = jnp.where(note_lane == NOTE_HIGH, 16.0, jnp.where(note_lane == NOTE_LOW, 1.0, 0.0))
    mark = jnp.sum(notes * weight, axis=1, keepdims=True).astype(I32) - 1
    hot = (mark == iota((32 * 2 * CAP, 2 * ROWS), 1)).astype(BF16)
    out[...] = dot(rows, hot, ((0,), (0,)))[:HALF].astype(BF16)


def place(arrived):
    return pl.pallas_call(
        place_kernel,
        out_shape=jax.ShapeDtypeStruct((HALF, 2 * ROWS), BF16),
        in_specs=[HBM],
        out_specs=VMEM,
        scratch_shapes=[pltpu.VMEM((32, 2 * CAP, LANES), BF16), pltpu.SemaphoreType.DMA((1,))],
        compiler_params=PARAMS,
        name="place",
    )(arrived)


def row_advantages(reward, group, small):
    position = iota((ROWS, 128), 0)
    result = jnp.zeros((ROWS, 128), F32)
    start = 0
    for i in range(4):
        member = group == small[GROUPS + i].astype(F32)
        count = jnp.sum(jnp.where(member, 1.0, 0.0), keepdims=True)
        total = jnp.sum(jnp.where(member, reward, 0.0), keepdims=True)
        square = jnp.sum(jnp.where(member, reward * reward, 0.0), keepdims=True)
        mean = total / count
        spread = jnp.maximum(jnp.sqrt(count * square - total * total) / count, 1.0)
        advantage = (small[REWARDS + i].astype(F32) - mean) / spread
        result = jnp.where(position >= start, advantage, result)
        start = start + small[LENGTHS + i]
    return result


def join_kernel(*refs):
    pieces, (out, semaphores) = refs[:4], refs[4:]
    for copy in fetch(stacked(pieces, out), semaphores):
        copy.wait()


def join(pieces):
    return pl.pallas_call(
        join_kernel,
        out_shape=jax.ShapeDtypeStruct((4 * CHUNK, 2 * COLS), BF16),
        in_specs=[HBM] * 4,
        out_specs=VMEM,
        scratch_shapes=[pltpu.SemaphoreType.DMA((4,))],
        compiler_params=PARAMS,
        name="join",
    )(*pieces)


STEPS = (-2, -1, 0, 1, 2, 3, -3, 4)


def slot_of(chunk, z):
    at = wrapped(lax.div(chunk, 2) - z + 2, 8)
    at = jnp.where(at == 6, 7, jnp.where(at == 7, 6, at))
    return pl.multiple_of((2 * at + lax.rem(chunk, 2)) * CHUNK, 16)


def stacked(pieces, whole):
    pairs, at = [], 0
    for piece in pieces:
        pairs.append((piece, whole.at[pl.ds(at, piece.shape[0]), :]))
        at += piece.shape[0]
    return pairs


def chunk_rows(parts, slot):
    total = None
    for part, begin in parts:
        inside = (slot >= begin) & (slot < begin + part.shape[0])
        at = pl.multiple_of(jnp.where(inside, slot - begin, 0), 16)
        rows = part[pl.ds(at, CHUNK), :]
        rows = jnp.where(inside, rows, jnp.zeros_like(rows))
        total = rows if total is None else total + rows
    return total


def chunk_slots(where, step):
    first, second, first_stride, second_stride = turned_place(where)
    at = wrapped(second + step, 4) * second_stride
    return [slot_of(wrapped(first + near, 4) * first_stride + at, where[3]) for near in (0, -1, 1, 2)]


def keep_late(where, step, piece, late):
    for k, slot in enumerate(chunk_slots(where, step)):

        @pl.when(slot >= 7 * HALF)
        def _(k=k, slot=slot):
            at = pl.multiple_of(slot - 7 * HALF, 16)
            late[pl.ds(at, CHUNK), :] = piece[k * CHUNK : (k + 1) * CHUNK, :]


def project_kernel(where, arrived, *refs):
    tokens, piece = refs[:5], refs[5]
    own, other, late, advantage, whole, landed, notes, semaphores = refs[6:]
    pairs = [(arrived.at[:, 0:16, 256:384], notes), *stacked(tokens, whole), (piece, landed)]
    copies = fetch(pairs, semaphores)
    copies[0].wait()
    note = notes[:, 0, :].astype(F32)
    advantage[...] = row_advantages(
        note[:, NOTE_REWARD : NOTE_REWARD + 4], note[:, NOTE_GROUP : NOTE_GROUP + 4], where
    )
    for copy in copies[1:]:
        copy.wait()
    keep_late(where, 0, landed, late)
    rows = [chunk_rows([(whole, 0)], slot) for slot in chunk_slots(where, 0)]
    rows = jnp.concatenate(rows, axis=0)
    own[...] = dot(rows[:, :ROWS], landed[...], ((0,), (0,)))
    other[...] = dot(rows[:, ROWS:], landed[...], ((0,), (0,)))


SUMS = jax.ShapeDtypeStruct((ROWS, 2 * COLS), F32)
LATE = jax.ShapeDtypeStruct((HALF, 2 * COLS), BF16)


def project(where, arrived, tokens, piece):
    whole = jax.ShapeDtypeStruct((5 * HALF, 2 * ROWS), BF16)
    return pl.pallas_call(
        project_kernel,
        out_shape=(SUMS, SUMS, LATE, jax.ShapeDtypeStruct((ROWS, 128), F32), whole),
        in_specs=[SMEM] + [HBM] * 7,
        out_specs=(VMEM,) * 5,
        scratch_shapes=[
            pltpu.VMEM((4 * CHUNK, 2 * COLS), BF16),
            pltpu.VMEM((32, 16, 128), BF16),
            pltpu.SemaphoreType.DMA((7,)),
        ],
        compiler_params=PARAMS,
        name="project",
    )(where, arrived, *tokens, piece)


def far_kernel(where, own, other, *refs):
    tokens, piece = refs[:2], refs[2]
    own_out, other_out, far, landed, semaphores = refs[3:]
    for copy in fetch([*stacked(tokens, far), (piece, landed)], semaphores):
        copy.wait()
    rows = [chunk_rows([(far, 5 * HALF)], slot) for slot in chunk_slots(where, 0)]
    rows = jnp.concatenate(rows, axis=0)
    own_out[...] = own[...] + dot(rows[:, :ROWS], landed[...], ((0,), (0,)))
    other_out[...] = other[...] + dot(rows[:, ROWS:], landed[...], ((0,), (0,)))


def project_far(where, own, other, tokens, piece):
    far = jax.ShapeDtypeStruct((2 * HALF, 2 * ROWS), BF16)
    return pl.pallas_call(
        far_kernel,
        out_shape=(SUMS, SUMS, far),
        in_specs=[SMEM] + [VMEM] * 2 + [HBM] * 3,
        out_specs=(VMEM,) * 3,
        scratch_shapes=[pltpu.VMEM((4 * CHUNK, 2 * COLS), BF16), pltpu.SemaphoreType.DMA((3,))],
        compiler_params=PARAMS,
        name="far",
    )(where, own, other, *tokens, piece)


def across_kernel(where, own, other, late, whole, far, *refs):
    pieces, (own_out, other_out, late_out, landed, semaphores) = refs[:3], refs[3:]
    pairs = [(piece, landed.at[pl.ds(4 * CHUNK * i, 4 * CHUNK), :]) for i, piece in enumerate(pieces)]
    copies = fetch(pairs, semaphores)
    late_out[...] = late[...]
    rows, steps = [], (-1, 1, 2)
    for step in steps:
        rows += [chunk_rows([(whole, 0), (far, 5 * HALF)], slot) for slot in chunk_slots(where, step)]
    for i, end in ((0, 1), (1, 3)):
        for k in range(i, end):
            copies[k].wait()
            keep_late(where, steps[k], landed.at[pl.ds(4 * CHUNK * k, 4 * CHUNK), :], late_out)
        some = jnp.concatenate(rows[4 * i : 4 * end], axis=0)
        weights = landed[4 * CHUNK * i : 4 * CHUNK * end, :]
        for columns, source, out in ((slice(0, ROWS), own, own_out), (slice(ROWS, 2 * ROWS), other, other_out)):
            before = source if i == 0 else out
            out[...] = before[...] + dot(some[:, columns], weights, ((0,), (0,)))


def project_across(where, own, other, late, whole, far, pieces):
    return pl.pallas_call(
        across_kernel,
        out_shape=(SUMS, SUMS, LATE),
        in_specs=[SMEM] + [VMEM] * 5 + [HBM] * 3,
        out_specs=(VMEM,) * 3,
        scratch_shapes=[pltpu.VMEM((12 * CHUNK, 2 * COLS), BF16), pltpu.SemaphoreType.DMA((3,))],
        compiler_params=PARAMS,
        name="across",
    )(where, own, other, late, whole, far, *pieces)


def first_late(other, late, first, second):
    def kernel(other, late, first, second, out, tokens, semaphores):
        for copy in fetch(stacked([first, second], tokens), semaphores):
            copy.wait()
        out[...] = other[:, :COLS] + dot(tokens[:, ROWS:], late[:, :COLS], ((0,), (0,)))

    return pl.pallas_call(
        kernel,
        out_shape=(
            jax.ShapeDtypeStruct((ROWS, COLS), F32),
            jax.ShapeDtypeStruct((HALF, 2 * ROWS), BF16),
        ),
        in_specs=[VMEM] * 2 + [HBM] * 2,
        out_specs=(VMEM,) * 2,
        scratch_shapes=[pltpu.SemaphoreType.DMA((2,))],
        compiler_params=PARAMS,
        name="late",
    )(other, late, first, second)


def second_late(other, late, tokens):
    def kernel(other, late, tokens, out):
        out[...] = other[:, COLS:] + dot(tokens[:, ROWS:], late[:, COLS:], ((0,), (0,)))

    return pl.pallas_call(
        kernel,
        out_shape=jax.ShapeDtypeStruct((ROWS, COLS), F32),
        in_specs=[VMEM] * 3,
        out_specs=VMEM,
        compiler_params=PARAMS,
        name="late",
    )(other, late, tokens)


def heads(value):
    return jnp.concatenate([value[:, 128 * i : 128 * (i + 1)] for i in range(3)], axis=0)


def attend(small, projection, block):
    first, count = 128 * block, 128 * (block + 1)
    key_at = iota((128, count), 1)
    query_at = first + iota((128, count), 0)
    row_at = first + iota((128, 1), 0)
    begin = jnp.zeros((128, 1), I32)
    start = 0
    for i in range(4):
        begin = jnp.where(row_at >= start, start, begin)
        start = start + small[LENGTHS + i]
    allowed = (key_at <= query_at) & (key_at >= begin)
    allowed = jnp.concatenate([allowed] * 3, axis=0)
    queries = heads(projection[first:count, 0:384])
    keys, values = projection[:count, 384:512], projection[:count, 512:640]
    scores = dot(queries, keys, ((1,), (1,))) * HEAD_WIDTH**-0.5
    scores = jnp.where(allowed, scores, MASKED_SCORE)
    weights = jnp.exp(scores - jnp.max(scores, axis=1, keepdims=True))
    probs = weights / jnp.sum(weights, axis=1, keepdims=True)
    rounded = probs.astype(BF16)
    return queries, keys, values, probs, rounded, dot(rounded, values)


def finish(begin, own, late, tokens, received, landed, semaphores):
    copy = fetch([(received, landed)], semaphores)[0]
    columns = slice(begin, begin + COLS)
    result = own[:, columns] + dot(tokens[:, :ROWS], late[:, columns], ((0,), (0,)))
    copy.wait()
    return (result + landed[...]).astype(BF16)


FINISH = [pltpu.VMEM((ROWS, COLS), F32), pltpu.SemaphoreType.DMA((1,))]


def ref_kernel(small, own, late, tokens, received, out, *scratch):
    projection = finish(0, own, late, tokens, received, *scratch)
    for block in range(3):
        out[ROWS * block : ROWS * (block + 1), :] = attend(small, projection, block)[5]


def ref_attention(small, own, late, tokens, received):
    return pl.pallas_call(
        ref_kernel,
        out_shape=jax.ShapeDtypeStruct((3 * ROWS, HEAD_WIDTH), F32),
        in_specs=[SMEM] + [VMEM] * 3 + [HBM],
        out_specs=VMEM,
        scratch_shapes=FINISH,
        compiler_params=PARAMS,
        name="ref_attention",
    )(small, own, late, tokens, received)


def two_parts(value):
    high = value.astype(BF16)
    return high, (value - high.astype(F32)).astype(BF16)


def policy_kernel(small, own, late, last, received, out_ref, upstream, advantage, *refs):
    out, scratch = refs[0], refs[1:]
    scale = HEAD_WIDTH**-0.5
    projection = finish(COLS, own, late, last, received, *scratch)
    grad_keys, grad_values = [0.0] * 3, [0.0] * 3
    for block in range(3):
        rows = slice(128 * block, 128 * (block + 1))
        queries, keys, values, probs, rounded, out_policy = attend(small, projection, block)
        weight = jnp.concatenate([advantage[rows, :]] * 3, axis=0)
        grad_out = weight * heads(upstream[rows, :].astype(F32))
        grad_out = grad_out + KL_WEIGHT * (out_policy - out_ref[ROWS * block : ROWS * (block + 1), :])
        high, low = two_parts(grad_out * 12288**-0.5)
        grad_probs = dot(high, values, ((1,), (1,))) + dot(low, values, ((1,), (1,)))
        grad_scores = probs * (grad_probs - jnp.sum(grad_probs * probs, axis=1, keepdims=True))
        grad_scores = (grad_scores * scale).astype(BF16)
        grad_query = dot(grad_scores, keys)
        for i in range(3):
            out[rows, 128 * i : 128 * (i + 1)] = grad_query[128 * i : 128 * (i + 1)].astype(BF16)
        for_keys = dot(grad_scores, queries, ((0,), (0,)))
        for_values = dot(rounded, high, ((0,), (0,)))
        for k in range(block + 1):
            grad_keys[k] = grad_keys[k] + for_keys[128 * k : 128 * (k + 1)]
            grad_values[k] = grad_values[k] + for_values[128 * k : 128 * (k + 1)]
    for k in range(3):
        out[128 * k : 128 * (k + 1), 384:512] = grad_keys[k].astype(BF16)
        out[128 * k : 128 * (k + 1), 512:640] = grad_values[k].astype(BF16)


def policy_attention(small, own, late, last, received, out_ref, upstream, advantage):
    return pl.pallas_call(
        policy_kernel,
        out_shape=jax.ShapeDtypeStruct((ROWS, COLS), BF16),
        in_specs=[SMEM] + [VMEM] * 3 + [HBM] + [VMEM] * 3,
        out_specs=VMEM,
        scratch_shapes=FINISH,
        compiler_params=PARAMS,
        name="policy_attention",
    )(small, own, late, last, received, out_ref, upstream, advantage)


def gradient_dot(move, where, whole, far, last, grad):
    first, _, first_stride, second_stride = turned_place(where)
    parts = [(whole, 0), (far, 5 * HALF), (last, 7 * HALF)]
    rows = []
    for k in range(4):
        chunk = wrapped(first + move, 4) * first_stride + k * second_stride
        rows.append(chunk_rows(parts, slot_of(chunk, where[3])))
    return dot(jnp.concatenate(rows, axis=0), grad).astype(BF16)


PART = jax.ShapeDtypeStruct((4 * CHUNK, COLS), BF16)


def gradient_part(where, whole, far, last, own, other, move):
    def kernel(where, whole, far, last, own, other, out, grad, semaphores):
        copy = fetch([(other, grad.at[pl.ds(ROWS, ROWS), :])], semaphores)[0]
        grad[0:ROWS, :] = own[...]
        copy.wait()
        out[...] = gradient_dot(move, where, whole, far, last, grad[...])

    return pl.pallas_call(
        kernel,
        out_shape=PART,
        in_specs=[SMEM] + [VMEM] * 4 + [HBM],
        out_specs=VMEM,
        scratch_shapes=[pltpu.VMEM((2 * ROWS, COLS), BF16), pltpu.SemaphoreType.DMA((1,))],
        compiler_params=PARAMS,
        name="gradient",
    )(where, whole, far, last, own, other)


def middle_kernel(where, own, *refs):
    pieces, outs, landed, semaphores = refs[:3], refs[3:7], refs[7], refs[8]
    second = turned_place(where)[1]
    copies = fetch([(piece, landed.at[i]) for i, piece in enumerate(pieces)], semaphores)
    for copy in copies:
        copy.wait()
    for move, out in zip((0, 1, -1, 2), outs):
        at = pl.ds(pl.multiple_of(wrapped(second + move, 4) * CHUNK, 16), CHUNK)
        total = (own[at, :].astype(F32) + landed[0, at, :].astype(F32)) + (
            landed[1, at, :].astype(F32) + landed[2, at, :].astype(F32)
        )
        out[...] = total.astype(out.dtype)


def middle_sums(where, own, pieces):
    def shape(kind):
        return jax.ShapeDtypeStruct((CHUNK, COLS), kind)

    return pl.pallas_call(
        middle_kernel,
        out_shape=(shape(F32), shape(BF16), shape(BF16), shape(BF16)),
        in_specs=[SMEM, VMEM] + [HBM] * 3,
        out_specs=(VMEM,) * 4,
        scratch_shapes=[pltpu.VMEM((3, 4 * CHUNK, COLS), BF16), pltpu.SemaphoreType.DMA((3,))],
        compiler_params=PARAMS,
        name="middle",
    )(where, own, *pieces)


def final_kernel(own, *refs):
    pieces, out, landed, semaphores = refs[:3], refs[3], refs[4], refs[5]
    for copy in fetch([(piece, landed.at[i]) for i, piece in enumerate(pieces)], semaphores):
        copy.wait()
    out[:, 0, :] = (own[...] + landed[0].astype(F32)) + (landed[1].astype(F32) + landed[2].astype(F32))


def final_sums(own, pieces):
    return pl.pallas_call(
        final_kernel,
        out_shape=jax.ShapeDtypeStruct((CHUNK, 1, COLS), F32),
        in_specs=[VMEM] + [HBM] * 3,
        out_specs=VMEM,
        scratch_shapes=[pltpu.VMEM((3, CHUNK, COLS), BF16), pltpu.SemaphoreType.DMA((3,))],
        compiler_params=PARAMS,
        name="final",
    )(own, *pieces)


def body(
    tokens,
    dest_shard,
    dest_offset,
    seg_lengths,
    rewards,
    groups,
    reference_head_weight,
    policy_head_weight,
    upstream,
):
    where = jnp.stack([lax.axis_index(name).astype(I32) for name in ("y", "x", "c", "z")])
    small = jnp.concatenate([where, rewards, groups, seg_lengths[0]])
    outgoing = route(rewards, groups, dest_shard, dest_offset, tokens)
    arrived = lax.all_to_all(outgoing, ("y", "x", "c"), split_axis=0, concat_axis=0, tiled=True)
    arrived, small = lax.optimization_barrier((arrived, small))
    _, weights, policy_weights = lax.optimization_barrier(
        (outgoing, reference_head_weight[:, 0], policy_head_weight[:, 0])
    )
    weights = jnp.concatenate([weights, policy_weights], axis=1)
    near = [weights, *(turned(weights, True, by) for by in (1, -1, 2))]
    block = place(arrived)
    _, near = lax.optimization_barrier((block, near))
    rows = join(near)
    weights = [turned(rows, False, by) for by in (1, -1, 2)]

    forward, backward = [block], [block]
    for _ in range(3):
        forward.append(shift(forward[-1], "z", 8, 1))
        backward.append(shift(backward[-1], "z", 8, -1))

    near = [forward[2], forward[1], block, backward[1], backward[2]]
    own, other, late, advantage, whole = project(small, arrived, near, rows)
    far = [backward[3], forward[3]]
    behind, ahead, own = lax.optimization_barrier((*far, own))
    first = shift(ahead[:CHUNK], "z", 8, 1)
    second = shift(behind[CHUNK:], "z", 8, -1)
    own, other, far = project_far(small, own, other, far, rows)
    own, other, late = project_across(small, own, other, late, whole, far, weights)
    swap = [(0, 1), (1, 0)]
    part, last = first_late(other, late, first, second)
    received_ref = lax.ppermute(part, "c", swap)
    received_policy = lax.ppermute(second_late(other, late, last), "c", swap)
    out_ref = ref_attention(small, own, late, last, received_ref)
    cotangent = upstream.reshape(ROWS, 3 * HEAD_WIDTH)
    grad = policy_attention(small, own, late, last, received_policy, out_ref, cotangent, advantage)
    grad_other = lax.ppermute(grad, "c", swap)

    parts = []
    for move in (-1, 1, 2, 0):
        part = gradient_part(small, whole, far, last, grad, grad_other, move)
        parts.append(turned(part, True, move) if move else part)
    sums = middle_sums(small, parts[3], parts[:3])
    parts = [turned(part, False, move) for move, part in zip((1, -1, 2), sums[1:])]
    return final_sums(sums[0], parts)


def solution(mesh):
    split = Mesh(mesh.devices.reshape(4, 4, 2, 8), ("y", "x", "c", "z"))
    roll = ("y", "x", "c")
    in_specs = (
        P(roll, "z"),
        P(roll),
        P(roll),
        P(roll, None),
        P(roll),
        P(roll),
        P(roll, "z", None),
        P(roll, "z", None),
        P(roll, "z", None),
    )
    out_specs = P(roll, "z", None)
    return jax.shard_map(body, mesh=split, in_specs=in_specs, out_specs=out_specs, check_vma=False)
```

```python
import jax
import jax.numpy as jnp
from jax import lax
from jax.experimental import pallas as pl
from jax.experimental.pallas import tpu as pltpu
from jax.sharding import Mesh
from jax.sharding import PartitionSpec as P

HEAD_WIDTH = 128
KL_WEIGHT = 1.0
MASKED_SCORE = -1e30

ROWS = 384
CAP = 24
MODEL_BLOCK = 640
COLS = 640
CHUNK = 160
HALF = 2 * CHUNK
LANES = 384
F32 = jnp.float32
BF16 = jnp.bfloat16
I32 = jnp.int32

REWARDS, GROUPS, LENGTHS = 4, 8, 12
NOTE_HIGH, NOTE_LOW, NOTE_REWARD, NOTE_GROUP = 64, 65, 66, 70

VMEM = pl.BlockSpec(memory_space=pltpu.VMEM)
SMEM = pl.BlockSpec(memory_space=pltpu.SMEM)
HBM = pl.BlockSpec(memory_space=pltpu.HBM)
ALONE = pltpu.CompilerParams(vmem_limit_bytes=60 * 1024 * 1024)
PARAMS = pltpu.CompilerParams(vmem_limit_bytes=28 * 1024 * 1024)


def iota(shape, dim):
    return lax.broadcasted_iota(I32, shape, dim)


def dot(a, b, contract=((1,), (0,))):
    return lax.dot_general(a, b, (contract, ((), ())), preferred_element_type=F32)


def fetch(pairs, semaphores):
    copies = [pltpu.make_async_copy(source, to, semaphores.at[i]) for i, (source, to) in enumerate(pairs)]
    for copy in copies:
        copy.start()
    return copies


def shift(value, axis, size, by):
    return lax.ppermute(value, axis, [(i, (i + by) % size) for i in range(size)])


def turned(value, first, by):
    pairs = []
    for y in range(4):
        for x in range(4):
            for c in range(2):
                to_y, to_x = (y, (x + by) % 4) if (c == 0) == first else ((y + by) % 4, x)
                pairs.append((8 * y + 2 * x + c, 8 * to_y + 2 * to_x + c))
    return lax.ppermute(value, ("y", "x", "c"), pairs)


def turned_place(where):
    y, x, odd = where[0], where[1], where[2]
    first = jnp.where(odd == 0, x, y)
    second = jnp.where(odd == 0, y, x)
    stride = jnp.where(odd == 0, 1, 4)
    return first, second, stride, 5 - stride


def wrapped(index, size):
    return lax.rem(index + size, size)


def route_kernel(rewards, groups, shard, offset, tokens, out, landed, semaphores):
    copy = fetch([(tokens, landed)], semaphores)[0]
    shard_row = shard[...].reshape(1, ROWS)
    offset_row = offset[...].reshape(1, ROWS)
    table = iota((32, ROWS), 0) == shard_row
    before = (iota((ROWS, ROWS), 0) < iota((ROWS, ROWS), 1)).astype(BF16)
    counts = dot(table.astype(BF16), before)
    rank = jnp.sum(jnp.where(table, counts, 0.0), axis=0, keepdims=True).astype(I32)
    slot = shard_row * CAP + rank
    hot = iota((32 * CAP, ROWS), 0) == slot
    lane = iota((MODEL_BLOCK, 2 * LANES), 1)
    half = (lane >= LANES).astype(I32)
    within = lane - half * LANES
    source = jnp.where(within < CHUNK, within, within + CHUNK) + CHUNK * half
    pick = (iota((MODEL_BLOCK, 2 * LANES), 0) == source) & (within < HALF)
    copy.wait()
    ordered = dot(landed[...], pick.astype(BF16)).astype(BF16)
    gathered = dot(hot.astype(BF16), ordered)
    odd = shard_row & 1
    note_lane = iota((1, 128), 1)
    common = jnp.zeros((1, 128), F32)
    for i in range(4):
        common = jnp.where(note_lane == NOTE_REWARD + i, rewards[i].astype(F32), common)
        common = jnp.where(note_lane == NOTE_GROUP + i, groups[i].astype(F32), common)
    for core in range(2):
        place = offset_row + 1 + ROWS * (odd ^ core)
        mark = jnp.sum(jnp.where(hot, place, 0), axis=1, keepdims=True)
        high = (mark >> 4).astype(F32)
        low = (mark & 15).astype(F32)
        notes = jnp.where(note_lane == NOTE_HIGH, high, jnp.where(note_lane == NOTE_LOW, low, common))
        first = LANES * core
        plain = gathered[:, first : first + 256].astype(BF16)
        last = (gathered[:, first + 256 : first + 384] + notes).astype(BF16)
        for chip in range(16):
            rows = slice(2 * CAP * chip, 2 * CAP * (chip + 1))
            out[2 * chip + core, :, 0:256] = plain[rows]
            out[2 * chip + core, :, 256:384] = last[rows]


def route(rewards, groups, shard, offset, tokens):
    return pl.pallas_call(
        route_kernel,
        out_shape=jax.ShapeDtypeStruct((32, 2 * CAP, LANES), BF16),
        in_specs=[SMEM, SMEM, VMEM, VMEM, HBM],
        out_specs=VMEM,
        scratch_shapes=[pltpu.VMEM((ROWS, MODEL_BLOCK), BF16), pltpu.SemaphoreType.DMA((1,))],
        compiler_params=ALONE,
        name="route",
    )(rewards, groups, shard, offset, tokens)


def place_kernel(arrived, out, landed, semaphores):
    fetch([(arrived, landed)], semaphores)[0].wait()
    rows = landed[...].reshape(32 * 2 * CAP, LANES)
    notes = rows[:, 256:384].astype(F32)
    note_lane = iota((1, 128), 1)
    weight = jnp.where(note_lane == NOTE_HIGH, 16.0, jnp.where(note_lane == NOTE_LOW, 1.0, 0.0))
    mark = jnp.sum(notes * weight, axis=1, keepdims=True).astype(I32) - 1
    hot = (mark == iota((32 * 2 * CAP, 2 * ROWS), 1)).astype(BF16)
    out[...] = dot(rows, hot, ((0,), (0,)))[:HALF].astype(BF16)


def place(arrived):
    return pl.pallas_call(
        place_kernel,
        out_shape=jax.ShapeDtypeStruct((HALF, 2 * ROWS), BF16),
        in_specs=[HBM],
        out_specs=VMEM,
        scratch_shapes=[pltpu.VMEM((32, 2 * CAP, LANES), BF16), pltpu.SemaphoreType.DMA((1,))],
        compiler_params=PARAMS,
        name="place",
    )(arrived)


def row_advantages(reward, group, small):
    position = iota((ROWS, 128), 0)
    result = jnp.zeros((ROWS, 128), F32)
    start = 0
    for i in range(4):
        member = group == small[GROUPS + i].astype(F32)
        count = jnp.sum(jnp.where(member, 1.0, 0.0), keepdims=True)
        total = jnp.sum(jnp.where(member, reward, 0.0), keepdims=True)
        square = jnp.sum(jnp.where(member, reward * reward, 0.0), keepdims=True)
        mean = total / count
        spread = jnp.maximum(jnp.sqrt(count * square - total * total) / count, 1.0)
        advantage = (small[REWARDS + i].astype(F32) - mean) / spread
        result = jnp.where(position >= start, advantage, result)
        start = start + small[LENGTHS + i]
    return result


def join_kernel(*refs):
    pieces, (out, semaphores) = refs[:4], refs[4:]
    for copy in fetch(stacked(pieces, out), semaphores):
        copy.wait()


def join(pieces):
    return pl.pallas_call(
        join_kernel,
        out_shape=jax.ShapeDtypeStruct((4 * CHUNK, 2 * COLS), BF16),
        in_specs=[HBM] * 4,
        out_specs=VMEM,
        scratch_shapes=[pltpu.SemaphoreType.DMA((4,))],
        compiler_params=PARAMS,
        name="join",
    )(*pieces)


STEPS = (-2, -1, 0, 1, 2, 3, -3, 4)


def slot_of(chunk, z):
    at = wrapped(lax.div(chunk, 2) - z + 2, 8)
    at = jnp.where(at == 6, 7, jnp.where(at == 7, 6, at))
    return pl.multiple_of((2 * at + lax.rem(chunk, 2)) * CHUNK, 16)


def stacked(pieces, whole):
    pairs, at = [], 0
    for piece in pieces:
        pairs.append((piece, whole.at[pl.ds(at, piece.shape[0]), :]))
        at += piece.shape[0]
    return pairs


def chunk_rows(parts, slot):
    total = None
    for part, begin in parts:
        inside = (slot >= begin) & (slot < begin + part.shape[0])
        at = pl.multiple_of(jnp.where(inside, slot - begin, 0), 16)
        rows = part[pl.ds(at, CHUNK), :]
        rows = jnp.where(inside, rows, jnp.zeros_like(rows))
        total = rows if total is None else total + rows
    return total


def chunk_slots(where, step):
    first, second, first_stride, second_stride = turned_place(where)
    at = wrapped(second + step, 4) * second_stride
    return [slot_of(wrapped(first + near, 4) * first_stride + at, where[3]) for near in (0, -1, 1, 2)]


def keep_late(where, step, piece, late):
    for k, slot in enumerate(chunk_slots(where, step)):

        @pl.when(slot >= 7 * HALF)
        def _(k=k, slot=slot):
            at = pl.multiple_of(slot - 7 * HALF, 16)
            late[pl.ds(at, CHUNK), :] = piece[k * CHUNK : (k + 1) * CHUNK, :]


def project_kernel(where, arrived, *refs):
    tokens, piece = refs[:5], refs[5]
    own, other, late, advantage, whole, landed, notes, semaphores = refs[6:]
    pairs = [(arrived.at[:, 0:16, 256:384], notes), *stacked(tokens, whole), (piece, landed)]
    copies = fetch(pairs, semaphores)
    copies[0].wait()
    note = notes[:, 0, :].astype(F32)
    advantage[...] = row_advantages(
        note[:, NOTE_REWARD : NOTE_REWARD + 4], note[:, NOTE_GROUP : NOTE_GROUP + 4], where
    )
    for copy in copies[1:]:
        copy.wait()
    keep_late(where, 0, landed, late)
    rows = [chunk_rows([(whole, 0)], slot) for slot in chunk_slots(where, 0)]
    rows = jnp.concatenate(rows, axis=0)
    own[...] = dot(rows[:, :ROWS], landed[...], ((0,), (0,)))
    other[...] = dot(rows[:, ROWS:], landed[...], ((0,), (0,)))


SUMS = jax.ShapeDtypeStruct((ROWS, 2 * COLS), F32)
LATE = jax.ShapeDtypeStruct((HALF, 2 * COLS), BF16)


def project(where, arrived, tokens, piece):
    whole = jax.ShapeDtypeStruct((5 * HALF, 2 * ROWS), BF16)
    return pl.pallas_call(
        project_kernel,
        out_shape=(SUMS, SUMS, LATE, jax.ShapeDtypeStruct((ROWS, 128), F32), whole),
        in_specs=[SMEM] + [HBM] * 7,
        out_specs=(VMEM,) * 5,
        scratch_shapes=[
            pltpu.VMEM((4 * CHUNK, 2 * COLS), BF16),
            pltpu.VMEM((32, 16, 128), BF16),
            pltpu.SemaphoreType.DMA((7,)),
        ],
        compiler_params=PARAMS,
        name="project",
    )(where, arrived, *tokens, piece)


def far_kernel(where, own, other, *refs):
    tokens, piece = refs[:2], refs[2]
    own_out, other_out, far, landed, semaphores = refs[3:]
    for copy in fetch([*stacked(tokens, far), (piece, landed)], semaphores):
        copy.wait()
    rows = [chunk_rows([(far, 5 * HALF)], slot) for slot in chunk_slots(where, 0)]
    rows = jnp.concatenate(rows, axis=0)
    own_out[...] = own[...] + dot(rows[:, :ROWS], landed[...], ((0,), (0,)))
    other_out[...] = other[...] + dot(rows[:, ROWS:], landed[...], ((0,), (0,)))


def project_far(where, own, other, tokens, piece):
    far = jax.ShapeDtypeStruct((2 * HALF, 2 * ROWS), BF16)
    return pl.pallas_call(
        far_kernel,
        out_shape=(SUMS, SUMS, far),
        in_specs=[SMEM] + [VMEM] * 2 + [HBM] * 3,
        out_specs=(VMEM,) * 3,
        scratch_shapes=[pltpu.VMEM((4 * CHUNK, 2 * COLS), BF16), pltpu.SemaphoreType.DMA((3,))],
        compiler_params=PARAMS,
        name="far",
    )(where, own, other, *tokens, piece)


def across_kernel(where, own, other, late, whole, far, *refs):
    pieces, (own_out, other_out, late_out, landed, semaphores) = refs[:3], refs[3:]
    pairs = [(piece, landed.at[pl.ds(4 * CHUNK * i, 4 * CHUNK), :]) for i, piece in enumerate(pieces)]
    copies = fetch(pairs, semaphores)
    late_out[...] = late[...]
    rows, steps = [], (-1, 1, 2)
    for step in steps:
        rows += [chunk_rows([(whole, 0), (far, 5 * HALF)], slot) for slot in chunk_slots(where, step)]
    for i, end in ((0, 1), (1, 3)):
        for k in range(i, end):
            copies[k].wait()
            keep_late(where, steps[k], landed.at[pl.ds(4 * CHUNK * k, 4 * CHUNK), :], late_out)
        some = jnp.concatenate(rows[4 * i : 4 * end], axis=0)
        weights = landed[4 * CHUNK * i : 4 * CHUNK * end, :]
        for columns, source, out in ((slice(0, ROWS), own, own_out), (slice(ROWS, 2 * ROWS), other, other_out)):
            before = source if i == 0 else out
            out[...] = before[...] + dot(some[:, columns], weights, ((0,), (0,)))


def project_across(where, own, other, late, whole, far, pieces):
    return pl.pallas_call(
        across_kernel,
        out_shape=(SUMS, SUMS, LATE),
        in_specs=[SMEM] + [VMEM] * 5 + [HBM] * 3,
        out_specs=(VMEM,) * 3,
        scratch_shapes=[pltpu.VMEM((12 * CHUNK, 2 * COLS), BF16), pltpu.SemaphoreType.DMA((3,))],
        compiler_params=PARAMS,
        name="across",
    )(where, own, other, late, whole, far, *pieces)


def late_other(other, late, first, second):
    def kernel(other, late, first, second, out, tokens, semaphores):
        for copy in fetch(stacked([first, second], tokens), semaphores):
            copy.wait()
        out[...] = other[...] + dot(tokens[:, ROWS:], late[...], ((0,), (0,)))

    return pl.pallas_call(
        kernel,
        out_shape=(SUMS, jax.ShapeDtypeStruct((HALF, 2 * ROWS), BF16)),
        in_specs=[VMEM] * 2 + [HBM] * 2,
        out_specs=(VMEM,) * 2,
        scratch_shapes=[pltpu.SemaphoreType.DMA((2,))],
        compiler_params=PARAMS,
        name="late",
    )(other, late, first, second)


def late_own(own, late, tokens):
    def kernel(own, late, tokens, out):
        out[...] = own[...] + dot(tokens[:, :ROWS], late[...], ((0,), (0,)))

    return pl.pallas_call(
        kernel,
        out_shape=SUMS,
        in_specs=[VMEM] * 3,
        out_specs=VMEM,
        compiler_params=PARAMS,
        name="own",
    )(own, late, tokens)


def heads(value):
    return jnp.concatenate([value[:, 128 * i : 128 * (i + 1)] for i in range(3)], axis=0)


def attend(small, projection, block):
    first, count = 128 * block, 128 * (block + 1)
    key_at = iota((128, count), 1)
    query_at = first + iota((128, count), 0)
    row_at = first + iota((128, 1), 0)
    begin = jnp.zeros((128, 1), I32)
    start = 0
    for i in range(4):
        begin = jnp.where(row_at >= start, start, begin)
        start = start + small[LENGTHS + i]
    allowed = (key_at <= query_at) & (key_at >= begin)
    allowed = jnp.concatenate([allowed] * 3, axis=0)
    queries = heads(projection[first:count, 0:384])
    keys, values = projection[:count, 384:512], projection[:count, 512:640]
    scores = dot(queries, keys, ((1,), (1,))) * HEAD_WIDTH**-0.5
    scores = jnp.where(allowed, scores, MASKED_SCORE)
    weights = jnp.exp(scores - jnp.max(scores, axis=1, keepdims=True))
    probs = weights / jnp.sum(weights, axis=1, keepdims=True)
    rounded = probs.astype(BF16)
    return queries, keys, values, probs, rounded, dot(rounded, values)


def two_parts(value):
    high = value.astype(BF16)
    return high, (value - high.astype(F32)).astype(BF16)


def attention_kernel(small, own, received, upstream, advantage, out, landed, semaphores):
    fetch([(received, landed)], semaphores)[0].wait()
    scale = HEAD_WIDTH**-0.5
    projection = (own[...] + landed[...]).astype(BF16)
    ref_projection, projection = projection[:, :COLS], projection[:, COLS:]
    grad_keys, grad_values = [0.0] * 3, [0.0] * 3
    for block in range(3):
        rows = slice(128 * block, 128 * (block + 1))
        out_ref = attend(small, ref_projection, block)[5]
        queries, keys, values, probs, rounded, out_policy = attend(small, projection, block)
        weight = jnp.concatenate([advantage[rows, :]] * 3, axis=0)
        grad_out = weight * heads(upstream[rows, :].astype(F32))
        grad_out = grad_out + KL_WEIGHT * (out_policy - out_ref)
        high, low = two_parts(grad_out * 12288**-0.5)
        grad_probs = dot(high, values, ((1,), (1,))) + dot(low, values, ((1,), (1,)))
        grad_scores = probs * (grad_probs - jnp.sum(grad_probs * probs, axis=1, keepdims=True))
        grad_scores = (grad_scores * scale).astype(BF16)
        grad_query = dot(grad_scores, keys)
        for i in range(3):
            out[rows, 128 * i : 128 * (i + 1)] = grad_query[128 * i : 128 * (i + 1)].astype(BF16)
        for_keys = dot(grad_scores, queries, ((0,), (0,)))
        for_values = dot(rounded, high, ((0,), (0,)))
        for k in range(block + 1):
            grad_keys[k] = grad_keys[k] + for_keys[128 * k : 128 * (k + 1)]
            grad_values[k] = grad_values[k] + for_values[128 * k : 128 * (k + 1)]
    for k in range(3):
        out[128 * k : 128 * (k + 1), 384:512] = grad_keys[k].astype(BF16)
        out[128 * k : 128 * (k + 1), 512:640] = grad_values[k].astype(BF16)


def attention(small, own, received, upstream, advantage):
    return pl.pallas_call(
        attention_kernel,
        out_shape=jax.ShapeDtypeStruct((ROWS, COLS), BF16),
        in_specs=[SMEM, VMEM, HBM, VMEM, VMEM],
        out_specs=VMEM,
        scratch_shapes=[pltpu.VMEM((ROWS, 2 * COLS), F32), pltpu.SemaphoreType.DMA((1,))],
        compiler_params=PARAMS,
        name="attention",
    )(small, own, received, upstream, advantage)


def gradient_dot(move, where, whole, far, last, grad):
    first, _, first_stride, second_stride = turned_place(where)
    parts = [(whole, 0), (far, 5 * HALF), (last, 7 * HALF)]
    rows = []
    for k in range(4):
        chunk = wrapped(first + move, 4) * first_stride + k * second_stride
        rows.append(chunk_rows(parts, slot_of(chunk, where[3])))
    return dot(jnp.concatenate(rows, axis=0), grad).astype(BF16)


PART = jax.ShapeDtypeStruct((4 * CHUNK, COLS), BF16)


def gradient_part(where, whole, far, last, own, other, move):
    def kernel(where, whole, far, last, own, other, out, grad, semaphores):
        copy = fetch([(other, grad.at[pl.ds(ROWS, ROWS), :])], semaphores)[0]
        grad[0:ROWS, :] = own[...]
        copy.wait()
        out[...] = gradient_dot(move, where, whole, far, last, grad[...])

    return pl.pallas_call(
        kernel,
        out_shape=PART,
        in_specs=[SMEM] + [VMEM] * 4 + [HBM],
        out_specs=VMEM,
        scratch_shapes=[pltpu.VMEM((2 * ROWS, COLS), BF16), pltpu.SemaphoreType.DMA((1,))],
        compiler_params=PARAMS,
        name="gradient",
    )(where, whole, far, last, own, other)


def middle_kernel(where, own, *refs):
    pieces, outs, landed, semaphores = refs[:3], refs[3:7], refs[7], refs[8]
    second = turned_place(where)[1]
    copies = fetch([(piece, landed.at[i]) for i, piece in enumerate(pieces)], semaphores)
    for copy in copies:
        copy.wait()
    for move, out in zip((0, 1, -1, 2), outs):
        at = pl.ds(pl.multiple_of(wrapped(second + move, 4) * CHUNK, 16), CHUNK)
        total = (own[at, :].astype(F32) + landed[0, at, :].astype(F32)) + (
            landed[1, at, :].astype(F32) + landed[2, at, :].astype(F32)
        )
        out[...] = total.astype(out.dtype)


def middle_sums(where, own, pieces):
    def shape(kind):
        return jax.ShapeDtypeStruct((CHUNK, COLS), kind)

    return pl.pallas_call(
        middle_kernel,
        out_shape=(shape(F32), shape(BF16), shape(BF16), shape(BF16)),
        in_specs=[SMEM, VMEM] + [HBM] * 3,
        out_specs=(VMEM,) * 4,
        scratch_shapes=[pltpu.VMEM((3, 4 * CHUNK, COLS), BF16), pltpu.SemaphoreType.DMA((3,))],
        compiler_params=PARAMS,
        name="middle",
    )(where, own, *pieces)


def final_kernel(own, *refs):
    pieces, out, landed, semaphores = refs[:3], refs[3], refs[4], refs[5]
    for copy in fetch([(piece, landed.at[i]) for i, piece in enumerate(pieces)], semaphores):
        copy.wait()
    out[:, 0, :] = (own[...] + landed[0].astype(F32)) + (landed[1].astype(F32) + landed[2].astype(F32))


def final_sums(own, pieces):
    return pl.pallas_call(
        final_kernel,
        out_shape=jax.ShapeDtypeStruct((CHUNK, 1, COLS), F32),
        in_specs=[VMEM] + [HBM] * 3,
        out_specs=VMEM,
        scratch_shapes=[pltpu.VMEM((3, CHUNK, COLS), BF16), pltpu.SemaphoreType.DMA((3,))],
        compiler_params=PARAMS,
        name="final",
    )(own, *pieces)


def body(
    tokens,
    dest_shard,
    dest_offset,
    seg_lengths,
    rewards,
    groups,
    reference_head_weight,
    policy_head_weight,
    upstream,
):
    where = jnp.stack([lax.axis_index(name).astype(I32) for name in ("y", "x", "c", "z")])
    small = jnp.concatenate([where, rewards, groups, seg_lengths[0]])
    outgoing = route(rewards, groups, dest_shard, dest_offset, tokens)
    arrived = lax.all_to_all(outgoing, ("y", "x", "c"), split_axis=0, concat_axis=0, tiled=True)
    arrived, small = lax.optimization_barrier((arrived, small))
    _, weights, policy_weights = lax.optimization_barrier(
        (outgoing, reference_head_weight[:, 0], policy_head_weight[:, 0])
    )
    weights = jnp.concatenate([weights, policy_weights], axis=1)
    near = [weights, *(turned(weights, True, by) for by in (1, -1, 2))]
    block = place(arrived)
    _, near = lax.optimization_barrier((block, near))
    rows = join(near)
    weights = [turned(rows, False, by) for by in (1, -1, 2)]

    forward, backward = [block], [block]
    for _ in range(3):
        forward.append(shift(forward[-1], "z", 8, 1))
        backward.append(shift(backward[-1], "z", 8, -1))

    near = [forward[2], forward[1], block, backward[1], backward[2]]
    own, other, late, advantage, whole = project(small, arrived, near, rows)
    far = [backward[3], forward[3]]
    behind, ahead, own = lax.optimization_barrier((*far, own))
    first = shift(ahead[:CHUNK], "z", 8, 1)
    second = shift(behind[CHUNK:], "z", 8, -1)
    own, other, far = project_far(small, own, other, far, rows)
    own, other, late = project_across(small, own, other, late, whole, far, weights)
    swap = [(0, 1), (1, 0)]
    other, last = late_other(other, late, first, second)
    received = lax.ppermute(other, "c", swap)
    own = late_own(own, late, last)
    cotangent = upstream.reshape(ROWS, 3 * HEAD_WIDTH)
    grad = attention(small, own, received, cotangent, advantage)
    grad_other = lax.ppermute(grad, "c", swap)

    parts = []
    for move in (-1, 1, 2, 0):
        part = gradient_part(small, whole, far, last, grad, grad_other, move)
        parts.append(turned(part, True, move) if move else part)
    sums = middle_sums(small, parts[3], parts[:3])
    parts = [turned(part, False, move) for move, part in zip((1, -1, 2), sums[1:])]
    return final_sums(sums[0], parts)


def solution(mesh):
    split = Mesh(mesh.devices.reshape(4, 4, 2, 8), ("y", "x", "c", "z"))
    roll = ("y", "x", "c")
    in_specs = (
        P(roll, "z"),
        P(roll),
        P(roll),
        P(roll, None),
        P(roll),
        P(roll),
        P(roll, "z", None),
        P(roll, "z", None),
        P(roll, "z", None),
    )
    out_specs = P(roll, "z", None)
    return jax.shard_map(body, mesh=split, in_specs=in_specs, out_specs=out_specs, check_vma=False)
```

```python
import jax
import jax.numpy as jnp
from jax import lax
from jax.experimental import pallas as pl
from jax.experimental.pallas import tpu as pltpu
from jax.sharding import Mesh
from jax.sharding import PartitionSpec as P

HEAD_WIDTH = 128
KL_WEIGHT = 1.0
MASKED_SCORE = -1e30

ROWS = 384
CAP = 24
MODEL_BLOCK = 640
COLS = 640
CHUNK = 160
HALF = 2 * CHUNK
LANES = 384
F32 = jnp.float32
BF16 = jnp.bfloat16
I32 = jnp.int32

REWARDS, GROUPS, LENGTHS = 4, 8, 12
NOTE_HIGH, NOTE_LOW, NOTE_REWARD, NOTE_GROUP = 64, 65, 66, 70

VMEM = pl.BlockSpec(memory_space=pltpu.VMEM)
SMEM = pl.BlockSpec(memory_space=pltpu.SMEM)
HBM = pl.BlockSpec(memory_space=pltpu.HBM)
ALONE = pltpu.CompilerParams(vmem_limit_bytes=60 * 1024 * 1024)
PARAMS = pltpu.CompilerParams(vmem_limit_bytes=28 * 1024 * 1024)


def iota(shape, dim):
    return lax.broadcasted_iota(I32, shape, dim)


def dot(a, b, contract=((1,), (0,))):
    return lax.dot_general(a, b, (contract, ((), ())), preferred_element_type=F32)


def fetch(pairs, semaphores):
    copies = [pltpu.make_async_copy(source, to, semaphores.at[i]) for i, (source, to) in enumerate(pairs)]
    for copy in copies:
        copy.start()
    return copies


def shift(value, axis, size, by):
    return lax.ppermute(value, axis, [(i, (i + by) % size) for i in range(size)])


def turned(value, first, by):
    pairs = []
    for y in range(4):
        for x in range(4):
            for c in range(2):
                to_y, to_x = (y, (x + by) % 4) if (c == 0) == first else ((y + by) % 4, x)
                pairs.append((8 * y + 2 * x + c, 8 * to_y + 2 * to_x + c))
    return lax.ppermute(value, ("y", "x", "c"), pairs)


def turned_place(where):
    y, x, odd = where[0], where[1], where[2]
    first = jnp.where(odd == 0, x, y)
    second = jnp.where(odd == 0, y, x)
    stride = jnp.where(odd == 0, 1, 4)
    return first, second, stride, 5 - stride


def wrapped(index, size):
    return lax.rem(index + size, size)


def route_kernel(rewards, groups, shard, offset, tokens, out, landed, semaphores):
    copy = fetch([(tokens, landed)], semaphores)[0]
    shard_row = shard[...].reshape(1, ROWS)
    offset_row = offset[...].reshape(1, ROWS)
    table = iota((32, ROWS), 0) == shard_row
    before = (iota((ROWS, ROWS), 0) < iota((ROWS, ROWS), 1)).astype(BF16)
    counts = dot(table.astype(BF16), before)
    rank = jnp.sum(jnp.where(table, counts, 0.0), axis=0, keepdims=True).astype(I32)
    slot = shard_row * CAP + rank
    hot = iota((32 * CAP, ROWS), 0) == slot
    lane = iota((MODEL_BLOCK, 2 * LANES), 1)
    half = (lane >= LANES).astype(I32)
    within = lane - half * LANES
    source = jnp.where(within < CHUNK, within, within + CHUNK) + CHUNK * half
    pick = (iota((MODEL_BLOCK, 2 * LANES), 0) == source) & (within < HALF)
    copy.wait()
    ordered = dot(landed[...], pick.astype(BF16)).astype(BF16)
    gathered = dot(hot.astype(BF16), ordered)
    odd = shard_row & 1
    note_lane = iota((1, 128), 1)
    common = jnp.zeros((1, 128), F32)
    for i in range(4):
        common = jnp.where(note_lane == NOTE_REWARD + i, rewards[i].astype(F32), common)
        common = jnp.where(note_lane == NOTE_GROUP + i, groups[i].astype(F32), common)
    for core in range(2):
        place = offset_row + 1 + ROWS * (odd ^ core)
        mark = jnp.sum(jnp.where(hot, place, 0), axis=1, keepdims=True)
        high = (mark >> 4).astype(F32)
        low = (mark & 15).astype(F32)
        notes = jnp.where(note_lane == NOTE_HIGH, high, jnp.where(note_lane == NOTE_LOW, low, common))
        first = LANES * core
        plain = gathered[:, first : first + 256].astype(BF16)
        last = (gathered[:, first + 256 : first + 384] + notes).astype(BF16)
        for chip in range(16):
            rows = slice(2 * CAP * chip, 2 * CAP * (chip + 1))
            out[2 * chip + core, :, 0:256] = plain[rows]
            out[2 * chip + core, :, 256:384] = last[rows]


def route(rewards, groups, shard, offset, tokens):
    return pl.pallas_call(
        route_kernel,
        out_shape=jax.ShapeDtypeStruct((32, 2 * CAP, LANES), BF16),
        in_specs=[SMEM, SMEM, VMEM, VMEM, HBM],
        out_specs=VMEM,
        scratch_shapes=[pltpu.VMEM((ROWS, MODEL_BLOCK), BF16), pltpu.SemaphoreType.DMA((1,))],
        compiler_params=ALONE,
        name="route",
    )(rewards, groups, shard, offset, tokens)


def place_kernel(arrived, out):
    rows = arrived[...].reshape(32 * 2 * CAP, LANES)
    notes = rows[:, 256:384].astype(F32)
    note_lane = iota((1, 128), 1)
    weight = jnp.where(note_lane == NOTE_HIGH, 16.0, jnp.where(note_lane == NOTE_LOW, 1.0, 0.0))
    mark = jnp.sum(notes * weight, axis=1, keepdims=True).astype(I32) - 1
    hot = (mark == iota((32 * 2 * CAP, 2 * ROWS), 1)).astype(BF16)
    out[...] = dot(rows, hot, ((0,), (0,)))[:HALF].astype(BF16)


def place(arrived):
    return pl.pallas_call(
        place_kernel,
        out_shape=jax.ShapeDtypeStruct((HALF, 2 * ROWS), BF16),
        in_specs=[VMEM],
        out_specs=VMEM,
        compiler_params=PARAMS,
        name="place",
    )(arrived)


def row_advantages(reward, group, small):
    position = iota((ROWS, 128), 0)
    result = jnp.zeros((ROWS, 128), F32)
    start = 0
    for i in range(4):
        member = group == small[GROUPS + i].astype(F32)
        count = jnp.sum(jnp.where(member, 1.0, 0.0), keepdims=True)
        total = jnp.sum(jnp.where(member, reward, 0.0), keepdims=True)
        square = jnp.sum(jnp.where(member, reward * reward, 0.0), keepdims=True)
        mean = total / count
        spread = jnp.maximum(jnp.sqrt(count * square - total * total) / count, 1.0)
        advantage = (small[REWARDS + i].astype(F32) - mean) / spread
        result = jnp.where(position >= start, advantage, result)
        start = start + small[LENGTHS + i]
    return result


def stack(pieces, out):
    at = 0
    for piece in pieces:
        out[at : at + piece.shape[0], :] = piece[...]
        at += piece.shape[0]


def join_kernel(*refs):
    stack(refs[:-1], refs[-1])


def join(pieces):
    return pl.pallas_call(
        join_kernel,
        out_shape=jax.ShapeDtypeStruct((4 * CHUNK, 2 * COLS), BF16),
        in_specs=[VMEM] * 4,
        out_specs=VMEM,
        compiler_params=PARAMS,
        name="join",
    )(*pieces)


STEPS = (-2, -1, 0, 1, 2, 3, -3, 4)


def slot_of(chunk, z):
    at = wrapped(lax.div(chunk, 2) - z + 2, 8)
    at = jnp.where(at == 6, 7, jnp.where(at == 7, 6, at))
    return pl.multiple_of((2 * at + lax.rem(chunk, 2)) * CHUNK, 16)


def chunk_rows(parts, slot):
    total = None
    for part, begin in parts:
        inside = (slot >= begin) & (slot < begin + part.shape[0])
        at = pl.multiple_of(jnp.where(inside, slot - begin, 0), 16)
        rows = part[pl.ds(at, CHUNK), :]
        rows = jnp.where(inside, rows, jnp.zeros_like(rows))
        total = rows if total is None else total + rows
    return total


def chunk_slots(where, step):
    first, second, first_stride, second_stride = turned_place(where)
    at = wrapped(second + step, 4) * second_stride
    return [slot_of(wrapped(first + near, 4) * first_stride + at, where[3]) for near in (0, -1, 1, 2)]


def keep_late(where, step, piece, late):
    for k, slot in enumerate(chunk_slots(where, step)):

        @pl.when(slot >= 7 * HALF)
        def _(k=k, slot=slot):
            at = pl.multiple_of(slot - 7 * HALF, 16)
            late[pl.ds(at, CHUNK), :] = piece[k * CHUNK : (k + 1) * CHUNK, :]


def project_kernel(where, arrived, *refs):
    tokens, piece = refs[:5], refs[5]
    own, other, late, advantage, whole = refs[6:]
    note = arrived[:, 0:16, 256:384][:, 0, :].astype(F32)
    advantage[...] = row_advantages(
        note[:, NOTE_REWARD : NOTE_REWARD + 4], note[:, NOTE_GROUP : NOTE_GROUP + 4], where
    )
    stack(tokens, whole)
    keep_late(where, 0, piece, late)
    rows = [chunk_rows([(whole, 0)], slot) for slot in chunk_slots(where, 0)]
    rows = jnp.concatenate(rows, axis=0)
    own[...] = dot(rows[:, :ROWS], piece[...], ((0,), (0,)))
    other[...] = dot(rows[:, ROWS:], piece[...], ((0,), (0,)))


SUMS = jax.ShapeDtypeStruct((ROWS, 2 * COLS), F32)
LATE = jax.ShapeDtypeStruct((HALF, 2 * COLS), BF16)


def project(where, arrived, tokens, piece):
    whole = jax.ShapeDtypeStruct((5 * HALF, 2 * ROWS), BF16)
    return pl.pallas_call(
        project_kernel,
        out_shape=(SUMS, SUMS, LATE, jax.ShapeDtypeStruct((ROWS, 128), F32), whole),
        in_specs=[SMEM] + [VMEM] * 7,
        out_specs=(VMEM,) * 5,
        compiler_params=PARAMS,
        name="project",
    )(where, arrived, *tokens, piece)


def far_kernel(where, own, other, *refs):
    tokens, piece = refs[:2], refs[2]
    own_out, other_out, far = refs[3:]
    stack(tokens, far)
    rows = [chunk_rows([(far, 5 * HALF)], slot) for slot in chunk_slots(where, 0)]
    rows = jnp.concatenate(rows, axis=0)
    own_out[...] = own[...] + dot(rows[:, :ROWS], piece[...], ((0,), (0,)))
    other_out[...] = other[...] + dot(rows[:, ROWS:], piece[...], ((0,), (0,)))


def project_far(where, own, other, tokens, piece):
    far = jax.ShapeDtypeStruct((2 * HALF, 2 * ROWS), BF16)
    return pl.pallas_call(
        far_kernel,
        out_shape=(SUMS, SUMS, far),
        in_specs=[SMEM] + [VMEM] * 5,
        out_specs=(VMEM,) * 3,
        compiler_params=PARAMS,
        name="far",
    )(where, own, other, *tokens, piece)


def across_sum(where, columns, whole, far, pieces):
    total = None
    for piece, step in zip(pieces, (-1, 1, 2)):
        parts = [(whole.at[:, columns], 0), (far.at[:, columns], 5 * HALF)]
        rows = jnp.concatenate([chunk_rows(parts, slot) for slot in chunk_slots(where, step)], axis=0)
        result = dot(rows, piece[...], ((0,), (0,)))
        total = result if total is None else total + result
    return total


def across_other(where, other, late, whole, far, pieces):
    def kernel(where, other, late, whole, far, *refs):
        pieces, (out, late_out) = refs[:3], refs[3:]
        late_out[...] = late[...]
        for piece, step in zip(pieces, (-1, 1, 2)):
            keep_late(where, step, piece, late_out)
        out[...] = other[...] + across_sum(where, pl.ds(ROWS, ROWS), whole, far, pieces)

    return pl.pallas_call(
        kernel,
        out_shape=(SUMS, LATE),
        in_specs=[SMEM] + [VMEM] * 7,
        out_specs=(VMEM,) * 2,
        compiler_params=PARAMS,
        name="across_other",
    )(where, other, late, whole, far, *pieces)


def late_other(other, late, first, second):
    def kernel(other, late, first, second, out, tokens):
        stack([first, second], tokens)
        out[...] = other[...] + dot(tokens[:, ROWS:], late[...], ((0,), (0,)))

    return pl.pallas_call(
        kernel,
        out_shape=(SUMS, jax.ShapeDtypeStruct((HALF, 2 * ROWS), BF16)),
        in_specs=[VMEM] * 4,
        out_specs=(VMEM,) * 2,
        compiler_params=PARAMS,
        name="late",
    )(other, late, first, second)


def across_own(where, own, late, whole, far, last, pieces):
    def kernel(where, own, late, whole, far, last, *refs):
        pieces, out = refs[:3], refs[3]
        total = across_sum(where, pl.ds(0, ROWS), whole, far, pieces)
        out[...] = own[...] + total + dot(last[:, :ROWS], late[...], ((0,), (0,)))

    return pl.pallas_call(
        kernel,
        out_shape=SUMS,
        in_specs=[SMEM] + [VMEM] * 8,
        out_specs=VMEM,
        compiler_params=PARAMS,
        name="across_own",
    )(where, own, late, whole, far, last, *pieces)


def heads(value):
    return jnp.concatenate([value[:, 128 * i : 128 * (i + 1)] for i in range(3)], axis=0)


def attend(small, projection, block):
    first, count = 128 * block, 128 * (block + 1)
    key_at = iota((128, count), 1)
    query_at = first + iota((128, count), 0)
    row_at = first + iota((128, 1), 0)
    begin = jnp.zeros((128, 1), I32)
    start = 0
    for i in range(4):
        begin = jnp.where(row_at >= start, start, begin)
        start = start + small[LENGTHS + i]
    allowed = (key_at <= query_at) & (key_at >= begin)
    allowed = jnp.concatenate([allowed] * 3, axis=0)
    queries = heads(projection[first:count, 0:384])
    keys, values = projection[:count, 384:512], projection[:count, 512:640]
    scores = dot(queries, keys, ((1,), (1,))) * HEAD_WIDTH**-0.5
    scores = jnp.where(allowed, scores, MASKED_SCORE)
    weights = jnp.exp(scores - jnp.max(scores, axis=1, keepdims=True))
    probs = weights / jnp.sum(weights, axis=1, keepdims=True)
    rounded = probs.astype(BF16)
    return queries, keys, values, probs, rounded, dot(rounded, values)


def two_parts(value):
    high = value.astype(BF16)
    return high, (value - high.astype(F32)).astype(BF16)


def attention_kernel(small, own, received, upstream, advantage, out):
    scale = HEAD_WIDTH**-0.5
    projection = (own[...] + received[...]).astype(BF16)
    ref_projection, projection = projection[:, :COLS], projection[:, COLS:]
    grad_keys, grad_values = [0.0] * 3, [0.0] * 3
    for block in range(3):
        rows = slice(128 * block, 128 * (block + 1))
        out_ref = attend(small, ref_projection, block)[5]
        queries, keys, values, probs, rounded, out_policy = attend(small, projection, block)
        weight = jnp.concatenate([advantage[rows, :]] * 3, axis=0)
        grad_out = weight * heads(upstream[rows, :].astype(F32))
        grad_out = grad_out + KL_WEIGHT * (out_policy - out_ref)
        high, low = two_parts(grad_out * 12288**-0.5)
        grad_probs = dot(high, values, ((1,), (1,))) + dot(low, values, ((1,), (1,)))
        grad_scores = probs * (grad_probs - jnp.sum(grad_probs * probs, axis=1, keepdims=True))
        grad_scores = (grad_scores * scale).astype(BF16)
        grad_query = dot(grad_scores, keys)
        for i in range(3):
            out[rows, 128 * i : 128 * (i + 1)] = grad_query[128 * i : 128 * (i + 1)].astype(BF16)
        for_keys = dot(grad_scores, queries, ((0,), (0,)))
        for_values = dot(rounded, high, ((0,), (0,)))
        for k in range(block + 1):
            grad_keys[k] = grad_keys[k] + for_keys[128 * k : 128 * (k + 1)]
            grad_values[k] = grad_values[k] + for_values[128 * k : 128 * (k + 1)]
    for k in range(3):
        out[128 * k : 128 * (k + 1), 384:512] = grad_keys[k].astype(BF16)
        out[128 * k : 128 * (k + 1), 512:640] = grad_values[k].astype(BF16)


def attention(small, own, received, upstream, advantage):
    return pl.pallas_call(
        attention_kernel,
        out_shape=jax.ShapeDtypeStruct((ROWS, COLS), BF16),
        in_specs=[SMEM] + [VMEM] * 4,
        out_specs=VMEM,
        compiler_params=PARAMS,
        name="attention",
    )(small, own, received, upstream, advantage)


def gradient_dot(move, where, whole, far, last, grad):
    first, _, first_stride, second_stride = turned_place(where)
    parts = [(whole, 0), (far, 5 * HALF), (last, 7 * HALF)]
    rows = []
    for k in range(4):
        chunk = wrapped(first + move, 4) * first_stride + k * second_stride
        rows.append(chunk_rows(parts, slot_of(chunk, where[3])))
    return dot(jnp.concatenate(rows, axis=0), grad).astype(BF16)


PART = jax.ShapeDtypeStruct((4 * CHUNK, COLS), BF16)


def gradient_part(where, whole, far, last, own, other, move):
    def kernel(where, whole, far, last, own, other, out):
        grad = jnp.concatenate([own[...], other[...]], axis=0)
        out[...] = gradient_dot(move, where, whole, far, last, grad)

    return pl.pallas_call(
        kernel,
        out_shape=PART,
        in_specs=[SMEM] + [VMEM] * 5,
        out_specs=VMEM,
        compiler_params=PARAMS,
        name="gradient",
    )(where, whole, far, last, own, other)


def middle_kernel(where, own, *refs):
    pieces, outs = refs[:3], refs[3:]
    second = turned_place(where)[1]
    for move, out in zip((0, 1, -1, 2), outs):
        at = pl.ds(pl.multiple_of(wrapped(second + move, 4) * CHUNK, 16), CHUNK)
        total = (own[at, :].astype(F32) + pieces[0][at, :].astype(F32)) + (
            pieces[1][at, :].astype(F32) + pieces[2][at, :].astype(F32)
        )
        out[...] = total.astype(out.dtype)


def middle_sums(where, own, pieces):
    def shape(kind):
        return jax.ShapeDtypeStruct((CHUNK, COLS), kind)

    return pl.pallas_call(
        middle_kernel,
        out_shape=(shape(F32), shape(BF16), shape(BF16), shape(BF16)),
        in_specs=[SMEM] + [VMEM] * 4,
        out_specs=(VMEM,) * 4,
        compiler_params=PARAMS,
        name="middle",
    )(where, own, *pieces)


def final_kernel(own, first, second, third, out):
    out[:, 0, :] = (own[...] + first[...].astype(F32)) + (second[...].astype(F32) + third[...].astype(F32))


def final_sums(own, pieces):
    return pl.pallas_call(
        final_kernel,
        out_shape=jax.ShapeDtypeStruct((CHUNK, 1, COLS), F32),
        in_specs=[VMEM] * 4,
        out_specs=VMEM,
        compiler_params=PARAMS,
        name="final",
    )(own, *pieces)


def body(
    tokens,
    dest_shard,
    dest_offset,
    seg_lengths,
    rewards,
    groups,
    reference_head_weight,
    policy_head_weight,
    upstream,
):
    where = jnp.stack([lax.axis_index(name).astype(I32) for name in ("y", "x", "c", "z")])
    small = jnp.concatenate([where, rewards, groups, seg_lengths[0]])
    outgoing = route(rewards, groups, dest_shard, dest_offset, tokens)
    arrived = lax.all_to_all(outgoing, ("y", "x", "c"), split_axis=0, concat_axis=0, tiled=True)
    arrived, small = lax.optimization_barrier((arrived, small))
    _, weights, policy_weights = lax.optimization_barrier(
        (outgoing, reference_head_weight[:, 0], policy_head_weight[:, 0])
    )
    weights = jnp.concatenate([weights, policy_weights], axis=1)
    near = [weights, *(turned(weights, True, by) for by in (1, -1, 2))]
    block = place(arrived)
    _, near = lax.optimization_barrier((block, near))
    rows = join(near)
    weights = [turned(rows, False, by) for by in (1, -1, 2)]

    forward, backward = [block], [block]
    for _ in range(3):
        forward.append(shift(forward[-1], "z", 8, 1))
        backward.append(shift(backward[-1], "z", 8, -1))

    near = [forward[2], forward[1], block, backward[1], backward[2]]
    own, other, late, advantage, whole = project(small, arrived, near, rows)
    far = [backward[3], forward[3]]
    behind, ahead, own = lax.optimization_barrier((*far, own))
    first = shift(ahead[:CHUNK], "z", 8, 1)
    second = shift(behind[CHUNK:], "z", 8, -1)
    own, other, far = project_far(small, own, other, far, rows)
    swap = [(0, 1), (1, 0)]
    other, late = across_other(small, other, late, whole, far, weights)
    other, last = late_other(other, late, first, second)
    received = lax.ppermute(other, "c", swap)
    own = across_own(small, own, late, whole, far, last, weights)
    cotangent = upstream.reshape(ROWS, 3 * HEAD_WIDTH)
    grad = attention(small, own, received, cotangent, advantage)
    grad_other = lax.ppermute(grad, "c", swap)

    parts = []
    for move in (-1, 1, 2, 0):
        part = gradient_part(small, whole, far, last, grad, grad_other, move)
        parts.append(turned(part, True, move) if move else part)
    sums = middle_sums(small, parts[3], parts[:3])
    parts = [turned(part, False, move) for move, part in zip((1, -1, 2), sums[1:])]
    return final_sums(sums[0], parts)


def solution(mesh):
    split = Mesh(mesh.devices.reshape(4, 4, 2, 8), ("y", "x", "c", "z"))
    roll = ("y", "x", "c")
    in_specs = (
        P(roll, "z"),
        P(roll),
        P(roll),
        P(roll, None),
        P(roll),
        P(roll),
        P(roll, "z", None),
        P(roll, "z", None),
        P(roll, "z", None),
    )
    out_specs = P(roll, "z", None)
    return jax.shard_map(body, mesh=split, in_specs=in_specs, out_specs=out_specs, check_vma=False)
```

```python
import jax
import jax.numpy as jnp
from jax import lax
from jax.experimental import pallas as pl
from jax.experimental.pallas import tpu as pltpu
from jax.sharding import Mesh
from jax.sharding import PartitionSpec as P

HEAD_WIDTH = 128
KL_WEIGHT = 1.0
MASKED_SCORE = -1e30

ROWS = 384
CAP = 24
MODEL_BLOCK = 640
COLS = 640
CHUNK = 160
HALF = 2 * CHUNK
LANES = 384
F32 = jnp.float32
BF16 = jnp.bfloat16
I32 = jnp.int32

REWARDS, GROUPS, LENGTHS = 4, 8, 12
NOTE_HIGH, NOTE_LOW, NOTE_REWARD, NOTE_GROUP = 64, 65, 66, 70

VMEM = pl.BlockSpec(memory_space=pltpu.VMEM)
SMEM = pl.BlockSpec(memory_space=pltpu.SMEM)
HBM = pl.BlockSpec(memory_space=pltpu.HBM)
ALONE = pltpu.CompilerParams(vmem_limit_bytes=60 * 1024 * 1024)
PARAMS = pltpu.CompilerParams(vmem_limit_bytes=28 * 1024 * 1024)


def iota(shape, dim):
    return lax.broadcasted_iota(I32, shape, dim)


def dot(a, b, contract=((1,), (0,))):
    return lax.dot_general(a, b, (contract, ((), ())), preferred_element_type=F32)


def fetch(pairs, semaphores):
    copies = [pltpu.make_async_copy(source, to, semaphores.at[i]) for i, (source, to) in enumerate(pairs)]
    for copy in copies:
        copy.start()
    return copies


def shift(value, axis, size, by):
    return lax.ppermute(value, axis, [(i, (i + by) % size) for i in range(size)])


def turned(value, first, by):
    pairs = []
    for y in range(4):
        for x in range(4):
            for c in range(2):
                to_y, to_x = (y, (x + by) % 4) if (c == 0) == first else ((y + by) % 4, x)
                pairs.append((8 * y + 2 * x + c, 8 * to_y + 2 * to_x + c))
    return lax.ppermute(value, ("y", "x", "c"), pairs)


def turned_place(where):
    y, x, odd = where[0], where[1], where[2]
    first = jnp.where(odd == 0, x, y)
    second = jnp.where(odd == 0, y, x)
    stride = jnp.where(odd == 0, 1, 4)
    return first, second, stride, 5 - stride


def wrapped(index, size):
    return lax.rem(index + size, size)


def route_kernel(rewards, groups, shard, offset, tokens, out, landed, semaphores):
    copy = fetch([(tokens, landed)], semaphores)[0]
    shard_row = shard[...].reshape(1, ROWS)
    offset_row = offset[...].reshape(1, ROWS)
    table = iota((32, ROWS), 0) == shard_row
    before = (iota((ROWS, ROWS), 0) < iota((ROWS, ROWS), 1)).astype(BF16)
    counts = dot(table.astype(BF16), before)
    rank = jnp.sum(jnp.where(table, counts, 0.0), axis=0, keepdims=True).astype(I32)
    slot = shard_row * CAP + rank
    hot = iota((32 * CAP, ROWS), 0) == slot
    lane = iota((MODEL_BLOCK, 2 * LANES), 1)
    half = (lane >= LANES).astype(I32)
    within = lane - half * LANES
    source = jnp.where(within < CHUNK, within, within + CHUNK) + CHUNK * half
    pick = (iota((MODEL_BLOCK, 2 * LANES), 0) == source) & (within < HALF)
    copy.wait()
    ordered = dot(landed[...], pick.astype(BF16)).astype(BF16)
    gathered = dot(hot.astype(BF16), ordered)
    odd = shard_row & 1
    note_lane = iota((1, 128), 1)
    common = jnp.zeros((1, 128), F32)
    for i in range(4):
        common = jnp.where(note_lane == NOTE_REWARD + i, rewards[i].astype(F32), common)
        common = jnp.where(note_lane == NOTE_GROUP + i, groups[i].astype(F32), common)
    for core in range(2):
        place = offset_row + 1 + ROWS * (odd ^ core)
        mark = jnp.sum(jnp.where(hot, place, 0), axis=1, keepdims=True)
        high = (mark >> 4).astype(F32)
        low = (mark & 15).astype(F32)
        notes = jnp.where(note_lane == NOTE_HIGH, high, jnp.where(note_lane == NOTE_LOW, low, common))
        first = LANES * core
        plain = gathered[:, first : first + 256].astype(BF16)
        last = (gathered[:, first + 256 : first + 384] + notes).astype(BF16)
        for chip in range(16):
            rows = slice(2 * CAP * chip, 2 * CAP * (chip + 1))
            out[2 * chip + core, :, 0:256] = plain[rows]
            out[2 * chip + core, :, 256:384] = last[rows]


def route(rewards, groups, shard, offset, tokens):
    return pl.pallas_call(
        route_kernel,
        out_shape=jax.ShapeDtypeStruct((32, 2 * CAP, LANES), BF16),
        in_specs=[SMEM, SMEM, VMEM, VMEM, HBM],
        out_specs=VMEM,
        scratch_shapes=[pltpu.VMEM((ROWS, MODEL_BLOCK), BF16), pltpu.SemaphoreType.DMA((1,))],
        compiler_params=ALONE,
        name="route",
    )(rewards, groups, shard, offset, tokens)


def place_kernel(arrived, out):
    rows = arrived[...].reshape(32 * 2 * CAP, LANES)
    notes = rows[:, 256:384].astype(F32)
    note_lane = iota((1, 128), 1)
    weight = jnp.where(note_lane == NOTE_HIGH, 16.0, jnp.where(note_lane == NOTE_LOW, 1.0, 0.0))
    mark = jnp.sum(notes * weight, axis=1, keepdims=True).astype(I32) - 1
    hot = (mark == iota((32 * 2 * CAP, 2 * ROWS), 1)).astype(BF16)
    out[...] = dot(rows, hot, ((0,), (0,)))[:HALF].astype(BF16)


def place(arrived):
    return pl.pallas_call(
        place_kernel,
        out_shape=jax.ShapeDtypeStruct((HALF, 2 * ROWS), BF16),
        in_specs=[VMEM],
        out_specs=VMEM,
        compiler_params=PARAMS,
        name="place",
    )(arrived)


def row_advantages(reward, group, small):
    position = iota((ROWS, 128), 0)
    result = jnp.zeros((ROWS, 128), F32)
    start = 0
    for i in range(4):
        member = group == small[GROUPS + i].astype(F32)
        count = jnp.sum(jnp.where(member, 1.0, 0.0), keepdims=True)
        total = jnp.sum(jnp.where(member, reward, 0.0), keepdims=True)
        square = jnp.sum(jnp.where(member, reward * reward, 0.0), keepdims=True)
        mean = total / count
        spread = jnp.maximum(jnp.sqrt(count * square - total * total) / count, 1.0)
        advantage = (small[REWARDS + i].astype(F32) - mean) / spread
        result = jnp.where(position >= start, advantage, result)
        start = start + small[LENGTHS + i]
    return result


def stack(pieces, out):
    at = 0
    for piece in pieces:
        out[at : at + piece.shape[0], :] = piece[...]
        at += piece.shape[0]


def join_kernel(*refs):
    stack(refs[:-1], refs[-1])


def join(pieces):
    return pl.pallas_call(
        join_kernel,
        out_shape=jax.ShapeDtypeStruct((4 * CHUNK, 2 * COLS), BF16),
        in_specs=[VMEM] * 4,
        out_specs=VMEM,
        compiler_params=PARAMS,
        name="join",
    )(*pieces)


STEPS = (-2, -1, 0, 1, 2, 3, -3, 4)


def slot_of(chunk, z):
    at = wrapped(lax.div(chunk, 2) - z + 2, 8)
    at = jnp.where(at == 6, 7, jnp.where(at == 7, 6, at))
    return pl.multiple_of((2 * at + lax.rem(chunk, 2)) * CHUNK, 16)


def chunk_rows(parts, slot):
    total = None
    for part, begin in parts:
        inside = (slot >= begin) & (slot < begin + part.shape[0])
        at = pl.multiple_of(jnp.where(inside, slot - begin, 0), 16)
        rows = part[pl.ds(at, CHUNK), :]
        rows = jnp.where(inside, rows, jnp.zeros_like(rows))
        total = rows if total is None else total + rows
    return total


def chunk_slots(where, step):
    first, second, first_stride, second_stride = turned_place(where)
    at = wrapped(second + step, 4) * second_stride
    return [slot_of(wrapped(first + near, 4) * first_stride + at, where[3]) for near in (0, -1, 1, 2)]


def keep_late(where, step, piece, late):
    for k, slot in enumerate(chunk_slots(where, step)):

        @pl.when(slot >= 7 * HALF)
        def _(k=k, slot=slot):
            at = pl.multiple_of(slot - 7 * HALF, 16)
            late[pl.ds(at, CHUNK), :] = piece[k * CHUNK : (k + 1) * CHUNK, :]


def project_kernel(where, arrived, *refs):
    tokens, piece = refs[:5], refs[5]
    own, other, late, advantage, whole = refs[6:]
    note = arrived[:, 0:16, 256:384][:, 0, :].astype(F32)
    advantage[...] = row_advantages(
        note[:, NOTE_REWARD : NOTE_REWARD + 4], note[:, NOTE_GROUP : NOTE_GROUP + 4], where
    )
    stack(tokens, whole)
    keep_late(where, 0, piece, late)
    rows = [chunk_rows([(whole, 0)], slot) for slot in chunk_slots(where, 0)]
    rows = jnp.concatenate(rows, axis=0)
    own[...] = dot(rows[:, :ROWS], piece[...], ((0,), (0,)))
    other[...] = dot(rows[:, ROWS:], piece[...], ((0,), (0,)))


SUMS = jax.ShapeDtypeStruct((ROWS, 2 * COLS), F32)
LATE = jax.ShapeDtypeStruct((HALF, 2 * COLS), BF16)


def project(where, arrived, tokens, piece):
    whole = jax.ShapeDtypeStruct((5 * HALF, 2 * ROWS), BF16)
    return pl.pallas_call(
        project_kernel,
        out_shape=(SUMS, SUMS, LATE, jax.ShapeDtypeStruct((ROWS, 128), F32), whole),
        in_specs=[SMEM] + [VMEM] * 7,
        out_specs=(VMEM,) * 5,
        compiler_params=PARAMS,
        name="project",
    )(where, arrived, *tokens, piece)


def far_kernel(where, own, other, *refs):
    tokens, piece = refs[:2], refs[2]
    own_out, other_out, far = refs[3:]
    stack(tokens, far)
    own_out[...] = own[...]
    other_out[...] = other[...]
    for k, slot in enumerate(chunk_slots(where, 0)):

        @pl.when((slot >= 5 * HALF) & (slot < 7 * HALF))
        def _(k=k, slot=slot):
            at = pl.multiple_of(slot - 5 * HALF, 16)
            rows, weights = far[pl.ds(at, CHUNK), :], piece[k * CHUNK : (k + 1) * CHUNK, :]
            own_out[...] += dot(rows[:, :ROWS], weights, ((0,), (0,)))
            other_out[...] += dot(rows[:, ROWS:], weights, ((0,), (0,)))


def project_far(where, own, other, tokens, piece):
    far = jax.ShapeDtypeStruct((2 * HALF, 2 * ROWS), BF16)
    return pl.pallas_call(
        far_kernel,
        out_shape=(SUMS, SUMS, far),
        in_specs=[SMEM] + [VMEM] * 5,
        out_specs=(VMEM,) * 3,
        compiler_params=PARAMS,
        name="far",
    )(where, own, other, *tokens, piece)


def across_sum(where, columns, whole, far, pieces):
    total = None
    for piece, step in zip(pieces, (-1, 1, 2)):
        parts = [(whole.at[:, columns], 0), (far.at[:, columns], 5 * HALF)]
        rows = jnp.concatenate([chunk_rows(parts, slot) for slot in chunk_slots(where, step)], axis=0)
        result = dot(rows, piece[...], ((0,), (0,)))
        total = result if total is None else total + result
    return total


def across_other(where, other, late, whole, far, pieces):
    def kernel(where, other, late, whole, far, *refs):
        pieces, (out, late_out) = refs[:3], refs[3:]
        late_out[...] = late[...]
        for piece, step in zip(pieces, (-1, 1, 2)):
            keep_late(where, step, piece, late_out)
        out[...] = other[...] + across_sum(where, pl.ds(ROWS, ROWS), whole, far, pieces)

    return pl.pallas_call(
        kernel,
        out_shape=(SUMS, LATE),
        in_specs=[SMEM] + [VMEM] * 7,
        out_specs=(VMEM,) * 2,
        compiler_params=PARAMS,
        name="across_other",
    )(where, other, late, whole, far, *pieces)


def late_other(other, late, first, second):
    def kernel(other, late, first, second, out, tokens):
        stack([first, second], tokens)
        out[...] = other[...] + dot(tokens[:, ROWS:], late[...], ((0,), (0,)))

    return pl.pallas_call(
        kernel,
        out_shape=(SUMS, jax.ShapeDtypeStruct((HALF, 2 * ROWS), BF16)),
        in_specs=[VMEM] * 4,
        out_specs=(VMEM,) * 2,
        compiler_params=PARAMS,
        name="late",
    )(other, late, first, second)


def across_own(where, own, late, whole, far, last, pieces):
    def kernel(where, own, late, whole, far, last, *refs):
        pieces, out = refs[:3], refs[3]
        total = across_sum(where, pl.ds(0, ROWS), whole, far, pieces)
        out[...] = own[...] + total + dot(last[:, :ROWS], late[...], ((0,), (0,)))

    return pl.pallas_call(
        kernel,
        out_shape=SUMS,
        in_specs=[SMEM] + [VMEM] * 8,
        out_specs=VMEM,
        compiler_params=PARAMS,
        name="across_own",
    )(where, own, late, whole, far, last, *pieces)


def heads(value):
    return jnp.concatenate([value[:, 128 * i : 128 * (i + 1)] for i in range(3)], axis=0)


def attend(small, projection, block):
    first, count = 128 * block, 128 * (block + 1)
    key_at = iota((128, count), 1)
    query_at = first + iota((128, count), 0)
    row_at = first + iota((128, 1), 0)
    begin = jnp.zeros((128, 1), I32)
    start = 0
    for i in range(4):
        begin = jnp.where(row_at >= start, start, begin)
        start = start + small[LENGTHS + i]
    allowed = (key_at <= query_at) & (key_at >= begin)
    allowed = jnp.concatenate([allowed] * 3, axis=0)
    queries = heads(projection[first:count, 0:384])
    keys, values = projection[:count, 384:512], projection[:count, 512:640]
    scores = dot(queries, keys, ((1,), (1,))) * HEAD_WIDTH**-0.5
    scores = jnp.where(allowed, scores, MASKED_SCORE)
    weights = jnp.exp(scores - jnp.max(scores, axis=1, keepdims=True))
    probs = weights / jnp.sum(weights, axis=1, keepdims=True)
    rounded = probs.astype(BF16)
    return queries, keys, values, probs, rounded, dot(rounded, values)


def two_parts(value):
    high = value.astype(BF16)
    return high, (value - high.astype(F32)).astype(BF16)


def attention_kernel(small, own, received, upstream, advantage, out):
    scale = HEAD_WIDTH**-0.5
    projection = (own[...] + received[...]).astype(BF16)
    ref_projection, projection = projection[:, :COLS], projection[:, COLS:]
    grad_keys, grad_values = [0.0] * 3, [0.0] * 3
    for block in range(3):
        rows = slice(128 * block, 128 * (block + 1))
        out_ref = attend(small, ref_projection, block)[5]
        queries, keys, values, probs, rounded, out_policy = attend(small, projection, block)
        weight = jnp.concatenate([advantage[rows, :]] * 3, axis=0)
        grad_out = weight * heads(upstream[rows, :].astype(F32))
        grad_out = grad_out + KL_WEIGHT * (out_policy - out_ref)
        high, low = two_parts(grad_out * 12288**-0.5)
        grad_probs = dot(high, values, ((1,), (1,))) + dot(low, values, ((1,), (1,)))
        grad_scores = probs * (grad_probs - jnp.sum(grad_probs * probs, axis=1, keepdims=True))
        grad_scores = (grad_scores * scale).astype(BF16)
        grad_query = dot(grad_scores, keys)
        for i in range(3):
            out[rows, 128 * i : 128 * (i + 1)] = grad_query[128 * i : 128 * (i + 1)].astype(BF16)
        for_keys = dot(grad_scores, queries, ((0,), (0,)))
        for_values = dot(rounded, high, ((0,), (0,)))
        for k in range(block + 1):
            grad_keys[k] = grad_keys[k] + for_keys[128 * k : 128 * (k + 1)]
            grad_values[k] = grad_values[k] + for_values[128 * k : 128 * (k + 1)]
    for k in range(3):
        out[128 * k : 128 * (k + 1), 384:512] = grad_keys[k].astype(BF16)
        out[128 * k : 128 * (k + 1), 512:640] = grad_values[k].astype(BF16)


def attention(small, own, received, upstream, advantage):
    return pl.pallas_call(
        attention_kernel,
        out_shape=jax.ShapeDtypeStruct((ROWS, COLS), BF16),
        in_specs=[SMEM] + [VMEM] * 4,
        out_specs=VMEM,
        compiler_params=PARAMS,
        name="attention",
    )(small, own, received, upstream, advantage)


def gradient_dot(move, where, whole, far, last, grad):
    first, _, first_stride, second_stride = turned_place(where)
    parts = [(whole, 0), (far, 5 * HALF), (last, 7 * HALF)]
    rows = []
    for k in range(4):
        chunk = wrapped(first + move, 4) * first_stride + k * second_stride
        rows.append(chunk_rows(parts, slot_of(chunk, where[3])))
    return dot(jnp.concatenate(rows, axis=0), grad).astype(BF16)


PART = jax.ShapeDtypeStruct((4 * CHUNK, COLS), BF16)


def gradient_part(where, whole, far, last, own, other, move):
    def kernel(where, whole, far, last, own, other, out):
        grad = jnp.concatenate([own[...], other[...]], axis=0)
        out[...] = gradient_dot(move, where, whole, far, last, grad)

    return pl.pallas_call(
        kernel,
        out_shape=PART,
        in_specs=[SMEM] + [VMEM] * 5,
        out_specs=VMEM,
        compiler_params=PARAMS,
        name="gradient",
    )(where, whole, far, last, own, other)


def middle_kernel(where, own, *refs):
    pieces, outs = refs[:3], refs[3:]
    second = turned_place(where)[1]
    for move, out in zip((0, 1, -1, 2), outs):
        at = pl.ds(pl.multiple_of(wrapped(second + move, 4) * CHUNK, 16), CHUNK)
        total = (own[at, :].astype(F32) + pieces[0][at, :].astype(F32)) + (
            pieces[1][at, :].astype(F32) + pieces[2][at, :].astype(F32)
        )
        out[...] = total.astype(out.dtype)


def middle_sums(where, own, pieces):
    def shape(kind):
        return jax.ShapeDtypeStruct((CHUNK, COLS), kind)

    return pl.pallas_call(
        middle_kernel,
        out_shape=(shape(F32), shape(BF16), shape(BF16), shape(BF16)),
        in_specs=[SMEM] + [VMEM] * 4,
        out_specs=(VMEM,) * 4,
        compiler_params=PARAMS,
        name="middle",
    )(where, own, *pieces)


def final_kernel(own, first, second, third, out):
    out[:, 0, :] = (own[...] + first[...].astype(F32)) + (second[...].astype(F32) + third[...].astype(F32))


def final_sums(own, pieces):
    return pl.pallas_call(
        final_kernel,
        out_shape=jax.ShapeDtypeStruct((CHUNK, 1, COLS), F32),
        in_specs=[VMEM] * 4,
        out_specs=VMEM,
        compiler_params=PARAMS,
        name="final",
    )(own, *pieces)


def body(
    tokens,
    dest_shard,
    dest_offset,
    seg_lengths,
    rewards,
    groups,
    reference_head_weight,
    policy_head_weight,
    upstream,
):
    where = jnp.stack([lax.axis_index(name).astype(I32) for name in ("y", "x", "c", "z")])
    small = jnp.concatenate([where, rewards, groups, seg_lengths[0]])
    outgoing = route(rewards, groups, dest_shard, dest_offset, tokens)
    arrived = lax.all_to_all(outgoing, ("y", "x", "c"), split_axis=0, concat_axis=0, tiled=True)
    arrived, small = lax.optimization_barrier((arrived, small))
    _, weights, policy_weights = lax.optimization_barrier(
        (outgoing, reference_head_weight[:, 0], policy_head_weight[:, 0])
    )
    weights = jnp.concatenate([weights, policy_weights], axis=1)
    near = [weights, *(turned(weights, True, by) for by in (1, -1, 2))]
    block = place(arrived)
    _, near = lax.optimization_barrier((block, near))
    rows = join(near)
    across, right, left = (turned(rows, False, by) for by in (2, 1, -1))
    weights = [right, left, across]

    forward, backward = [block], [block]
    for _ in range(3):
        forward.append(shift(forward[-1], "z", 8, 1))
        backward.append(shift(backward[-1], "z", 8, -1))

    near = [forward[2], forward[1], block, backward[1], backward[2]]
    own, other, late, advantage, whole = project(small, arrived, near, rows)
    far = [backward[3], forward[3]]
    behind, ahead, own = lax.optimization_barrier((*far, own))
    first = shift(ahead[:CHUNK], "z", 8, 1)
    second = shift(behind[CHUNK:], "z", 8, -1)
    own, other, far = project_far(small, own, other, far, rows)
    swap = [(0, 1), (1, 0)]
    other, late = across_other(small, other, late, whole, far, weights)
    other, last = late_other(other, late, first, second)
    received = lax.ppermute(other, "c", swap)
    own = across_own(small, own, late, whole, far, last, weights)
    cotangent = upstream.reshape(ROWS, 3 * HEAD_WIDTH)
    grad = attention(small, own, received, cotangent, advantage)
    grad_other = lax.ppermute(grad, "c", swap)

    parts = []
    for move in (-1, 1, 2, 0):
        part = gradient_part(small, whole, far, last, grad, grad_other, move)
        parts.append(turned(part, True, move) if move else part)
    sums = middle_sums(small, parts[3], parts[:3])
    parts = [turned(part, False, move) for move, part in zip((1, -1, 2), sums[1:])]
    return final_sums(sums[0], parts)


def solution(mesh):
    split = Mesh(mesh.devices.reshape(4, 4, 2, 8), ("y", "x", "c", "z"))
    roll = ("y", "x", "c")
    in_specs = (
        P(roll, "z"),
        P(roll),
        P(roll),
        P(roll, None),
        P(roll),
        P(roll),
        P(roll, "z", None),
        P(roll, "z", None),
        P(roll, "z", None),
    )
    out_specs = P(roll, "z", None)
    return jax.shard_map(body, mesh=split, in_specs=in_specs, out_specs=out_specs, check_vma=False)
```

```python
import jax
import jax.numpy as jnp
from jax import lax
from jax.experimental import pallas as pl
from jax.experimental.pallas import tpu as pltpu
from jax.sharding import Mesh
from jax.sharding import PartitionSpec as P

HEAD_WIDTH = 128
KL_WEIGHT = 1.0
MASKED_SCORE = -1e30

ROWS = 384
CAP = 24
MODEL_BLOCK = 640
COLS = 640
CHUNK = 160
HALF = 2 * CHUNK
LANES = 384
F32 = jnp.float32
BF16 = jnp.bfloat16
I32 = jnp.int32

REWARDS, GROUPS, LENGTHS = 4, 8, 12
NOTE_HIGH, NOTE_LOW, NOTE_REWARD, NOTE_GROUP = 64, 65, 66, 70

VMEM = pl.BlockSpec(memory_space=pltpu.VMEM)
SMEM = pl.BlockSpec(memory_space=pltpu.SMEM)
HBM = pl.BlockSpec(memory_space=pltpu.HBM)
ALONE = pltpu.CompilerParams(vmem_limit_bytes=60 * 1024 * 1024)
PARAMS = pltpu.CompilerParams(vmem_limit_bytes=28 * 1024 * 1024)


def iota(shape, dim):
    return lax.broadcasted_iota(I32, shape, dim)


def dot(a, b, contract=((1,), (0,))):
    return lax.dot_general(a, b, (contract, ((), ())), preferred_element_type=F32)


def fetch(pairs, semaphores):
    copies = [pltpu.make_async_copy(source, to, semaphores.at[i]) for i, (source, to) in enumerate(pairs)]
    for copy in copies:
        copy.start()
    return copies


def shift(value, axis, size, by):
    return lax.ppermute(value, axis, [(i, (i + by) % size) for i in range(size)])


def turned(value, first, by):
    pairs = []
    for y in range(4):
        for x in range(4):
            for c in range(2):
                to_y, to_x = (y, (x + by) % 4) if (c == 0) == first else ((y + by) % 4, x)
                pairs.append((8 * y + 2 * x + c, 8 * to_y + 2 * to_x + c))
    return lax.ppermute(value, ("y", "x", "c"), pairs)


def turned_place(where):
    y, x, odd = where[0], where[1], where[2]
    first = jnp.where(odd == 0, x, y)
    second = jnp.where(odd == 0, y, x)
    stride = jnp.where(odd == 0, 1, 4)
    return first, second, stride, 5 - stride


def wrapped(index, size):
    return lax.rem(index + size, size)


def route_kernel(rewards, groups, shard, offset, tokens, out, landed, semaphores):
    copy = fetch([(tokens, landed)], semaphores)[0]
    shard_row = shard[...].reshape(1, ROWS)
    offset_row = offset[...].reshape(1, ROWS)
    table = iota((32, ROWS), 0) == shard_row
    before = (iota((ROWS, ROWS), 0) < iota((ROWS, ROWS), 1)).astype(BF16)
    counts = dot(table.astype(BF16), before)
    rank = jnp.sum(jnp.where(table, counts, 0.0), axis=0, keepdims=True).astype(I32)
    slot = shard_row * CAP + rank
    hot = iota((32 * CAP, ROWS), 0) == slot
    lane = iota((MODEL_BLOCK, 2 * LANES), 1)
    half = (lane >= LANES).astype(I32)
    within = lane - half * LANES
    source = jnp.where(within < CHUNK, within, within + CHUNK) + CHUNK * half
    pick = (iota((MODEL_BLOCK, 2 * LANES), 0) == source) & (within < HALF)
    copy.wait()
    ordered = dot(landed[...], pick.astype(BF16)).astype(BF16)
    gathered = dot(hot.astype(BF16), ordered)
    odd = shard_row & 1
    note_lane = iota((1, 128), 1)
    common = jnp.zeros((1, 128), F32)
    for i in range(4):
        common = jnp.where(note_lane == NOTE_REWARD + i, rewards[i].astype(F32), common)
        common = jnp.where(note_lane == NOTE_GROUP + i, groups[i].astype(F32), common)
    for core in range(2):
        place = offset_row + 1 + ROWS * (odd ^ core)
        mark = jnp.sum(jnp.where(hot, place, 0), axis=1, keepdims=True)
        high = (mark >> 4).astype(F32)
        low = (mark & 15).astype(F32)
        notes = jnp.where(note_lane == NOTE_HIGH, high, jnp.where(note_lane == NOTE_LOW, low, common))
        first = LANES * core
        plain = gathered[:, first : first + 256].astype(BF16)
        last = (gathered[:, first + 256 : first + 384] + notes).astype(BF16)
        for chip in range(16):
            rows = slice(2 * CAP * chip, 2 * CAP * (chip + 1))
            out[2 * chip + core, :, 0:256] = plain[rows]
            out[2 * chip + core, :, 256:384] = last[rows]


def route(rewards, groups, shard, offset, tokens):
    return pl.pallas_call(
        route_kernel,
        out_shape=jax.ShapeDtypeStruct((32, 2 * CAP, LANES), BF16),
        in_specs=[SMEM, SMEM, VMEM, VMEM, HBM],
        out_specs=VMEM,
        scratch_shapes=[pltpu.VMEM((ROWS, MODEL_BLOCK), BF16), pltpu.SemaphoreType.DMA((1,))],
        compiler_params=ALONE,
        name="route",
    )(rewards, groups, shard, offset, tokens)


def place_kernel(arrived, out):
    rows = arrived[...].reshape(32 * 2 * CAP, LANES)
    notes = rows[:, 256:384].astype(F32)
    note_lane = iota((1, 128), 1)
    weight = jnp.where(note_lane == NOTE_HIGH, 16.0, jnp.where(note_lane == NOTE_LOW, 1.0, 0.0))
    mark = jnp.sum(notes * weight, axis=1, keepdims=True).astype(I32) - 1
    hot = (mark == iota((32 * 2 * CAP, 2 * ROWS), 1)).astype(BF16)
    out[...] = dot(rows, hot, ((0,), (0,)))[:HALF].astype(BF16)


def place(arrived):
    return pl.pallas_call(
        place_kernel,
        out_shape=jax.ShapeDtypeStruct((HALF, 2 * ROWS), BF16),
        in_specs=[VMEM],
        out_specs=VMEM,
        compiler_params=PARAMS,
        name="place",
    )(arrived)


def row_advantages(reward, group, small):
    position = iota((ROWS, 128), 0)
    result = jnp.zeros((ROWS, 128), F32)
    start = 0
    for i in range(4):
        member = group == small[GROUPS + i].astype(F32)
        count = jnp.sum(jnp.where(member, 1.0, 0.0), keepdims=True)
        total = jnp.sum(jnp.where(member, reward, 0.0), keepdims=True)
        square = jnp.sum(jnp.where(member, reward * reward, 0.0), keepdims=True)
        mean = total / count
        spread = jnp.maximum(jnp.sqrt(count * square - total * total) / count, 1.0)
        advantage = (small[REWARDS + i].astype(F32) - mean) / spread
        result = jnp.where(position >= start, advantage, result)
        start = start + small[LENGTHS + i]
    return result


def stack(pieces, out):
    at = 0
    for piece in pieces:
        out[at : at + piece.shape[0], :] = piece[...]
        at += piece.shape[0]


def join_kernel(*refs):
    stack(refs[:-1], refs[-1])


def join(pieces):
    return pl.pallas_call(
        join_kernel,
        out_shape=jax.ShapeDtypeStruct((4 * CHUNK, 2 * COLS), BF16),
        in_specs=[VMEM] * 4,
        out_specs=VMEM,
        compiler_params=PARAMS,
        name="join",
    )(*pieces)


STEPS = (-2, -1, 0, 1, 2, 3, -3, 4)


def slot_of(chunk, z):
    at = wrapped(lax.div(chunk, 2) - z + 2, 8)
    at = jnp.where(at == 6, 7, jnp.where(at == 7, 6, at))
    return pl.multiple_of((2 * at + lax.rem(chunk, 2)) * CHUNK, 16)


def chunk_rows(parts, slot):
    total = None
    for part, begin in parts:
        inside = (slot >= begin) & (slot < begin + part.shape[0])
        at = pl.multiple_of(jnp.where(inside, slot - begin, 0), 16)
        rows = part[pl.ds(at, CHUNK), :]
        rows = jnp.where(inside, rows, jnp.zeros_like(rows))
        total = rows if total is None else total + rows
    return total


def chunk_slots(where, step):
    first, second, first_stride, second_stride = turned_place(where)
    at = wrapped(second + step, 4) * second_stride
    return [slot_of(wrapped(first + near, 4) * first_stride + at, where[3]) for near in (0, -1, 1, 2)]


def chunk_slot(where, step, k):
    first, second, first_stride, second_stride = turned_place(where)
    near = jnp.where(k == 0, 0, jnp.where(k == 1, -1, k - 1))
    chunk = wrapped(first + near, 4) * first_stride + wrapped(second + step, 4) * second_stride
    return slot_of(chunk, where[3])


def keep_late(where, step, piece, late):
    def keep(k, carry):
        slot = chunk_slot(where, step, k)

        @pl.when(slot >= 7 * HALF)
        def _():
            at = pl.ds(pl.multiple_of(slot - 7 * HALF, 16), CHUNK)
            late[at, :] = piece[pl.ds(pl.multiple_of(k * CHUNK, 16), CHUNK), :]

        return carry

    lax.fori_loop(0, 4, keep, 0)


def project_kernel(where, arrived, *refs):
    tokens, piece = refs[:5], refs[5]
    own, other, late, advantage, whole = refs[6:]
    note = arrived[:, 0:16, 256:384][:, 0, :].astype(F32)
    advantage[...] = row_advantages(
        note[:, NOTE_REWARD : NOTE_REWARD + 4], note[:, NOTE_GROUP : NOTE_GROUP + 4], where
    )
    stack(tokens, whole)
    keep_late(where, 0, piece, late)
    rows = [chunk_rows([(whole, 0)], slot) for slot in chunk_slots(where, 0)]
    rows = jnp.concatenate(rows, axis=0)
    own[...] = dot(rows[:, :ROWS], piece[...], ((0,), (0,)))
    other[...] = dot(rows[:, ROWS:], piece[...], ((0,), (0,)))


SUMS = jax.ShapeDtypeStruct((ROWS, 2 * COLS), F32)
LATE = jax.ShapeDtypeStruct((HALF, 2 * COLS), BF16)


def project(where, arrived, tokens, piece):
    whole = jax.ShapeDtypeStruct((5 * HALF, 2 * ROWS), BF16)
    return pl.pallas_call(
        project_kernel,
        out_shape=(SUMS, SUMS, LATE, jax.ShapeDtypeStruct((ROWS, 128), F32), whole),
        in_specs=[SMEM] + [VMEM] * 7,
        out_specs=(VMEM,) * 5,
        compiler_params=PARAMS,
        name="project",
    )(where, arrived, *tokens, piece)


def far_kernel(where, own, other, *refs):
    tokens, piece = refs[:2], refs[2]
    own_out, other_out, far = refs[3:]
    stack(tokens, far)
    own_out[...] = own[...]
    other_out[...] = other[...]

    def add(k, carry):
        slot = chunk_slot(where, 0, k)

        @pl.when((slot >= 5 * HALF) & (slot < 7 * HALF))
        def _():
            at = pl.ds(pl.multiple_of(slot - 5 * HALF, 16), CHUNK)
            weights = piece[pl.ds(pl.multiple_of(k * CHUNK, 16), CHUNK), :]
            own_out[...] += dot(far[at, :ROWS], weights, ((0,), (0,)))
            other_out[...] += dot(far[at, ROWS:], weights, ((0,), (0,)))

        return carry

    lax.fori_loop(0, 4, add, 0)


def project_far(where, own, other, tokens, piece):
    far = jax.ShapeDtypeStruct((2 * HALF, 2 * ROWS), BF16)
    return pl.pallas_call(
        far_kernel,
        out_shape=(SUMS, SUMS, far),
        in_specs=[SMEM] + [VMEM] * 5,
        out_specs=(VMEM,) * 3,
        compiler_params=PARAMS,
        name="far",
    )(where, own, other, *tokens, piece)


def across_sum(where, columns, whole, far, pieces):
    total = None
    for piece, step in zip(pieces, (-1, 1, 2)):
        parts = [(whole.at[:, columns], 0), (far.at[:, columns], 5 * HALF)]
        rows = jnp.concatenate([chunk_rows(parts, slot) for slot in chunk_slots(where, step)], axis=0)
        result = dot(rows, piece[...], ((0,), (0,)))
        total = result if total is None else total + result
    return total


def across_other(where, other, late, whole, far, pieces):
    def kernel(where, other, late, whole, far, *refs):
        pieces, (out, late_out) = refs[:3], refs[3:]
        late_out[...] = late[...]
        for piece, step in zip(pieces, (-1, 1, 2)):
            keep_late(where, step, piece, late_out)
        out[...] = other[...] + across_sum(where, pl.ds(ROWS, ROWS), whole, far, pieces)

    return pl.pallas_call(
        kernel,
        out_shape=(SUMS, LATE),
        in_specs=[SMEM] + [VMEM] * 7,
        out_specs=(VMEM,) * 2,
        compiler_params=PARAMS,
        name="across_other",
    )(where, other, late, whole, far, *pieces)


def late_other(other, late, first, second):
    def kernel(other, late, first, second, out, tokens):
        stack([first, second], tokens)
        out[...] = other[...] + dot(tokens[:, ROWS:], late[...], ((0,), (0,)))

    return pl.pallas_call(
        kernel,
        out_shape=(SUMS, jax.ShapeDtypeStruct((HALF, 2 * ROWS), BF16)),
        in_specs=[VMEM] * 4,
        out_specs=(VMEM,) * 2,
        compiler_params=PARAMS,
        name="late",
    )(other, late, first, second)


def across_own(where, own, late, whole, far, last, pieces):
    def kernel(where, own, late, whole, far, last, *refs):
        pieces, out = refs[:3], refs[3]
        total = across_sum(where, pl.ds(0, ROWS), whole, far, pieces)
        out[...] = own[...] + total + dot(last[:, :ROWS], late[...], ((0,), (0,)))

    return pl.pallas_call(
        kernel,
        out_shape=SUMS,
        in_specs=[SMEM] + [VMEM] * 8,
        out_specs=VMEM,
        compiler_params=PARAMS,
        name="across_own",
    )(where, own, late, whole, far, last, *pieces)


def heads(value):
    return jnp.concatenate([value[:, 128 * i : 128 * (i + 1)] for i in range(3)], axis=0)


def attend(small, projection, block):
    first, count = 128 * block, 128 * (block + 1)
    key_at = iota((128, count), 1)
    query_at = first + iota((128, count), 0)
    row_at = first + iota((128, 1), 0)
    begin = jnp.zeros((128, 1), I32)
    start = 0
    for i in range(4):
        begin = jnp.where(row_at >= start, start, begin)
        start = start + small[LENGTHS + i]
    allowed = (key_at <= query_at) & (key_at >= begin)
    allowed = jnp.concatenate([allowed] * 3, axis=0)
    queries = heads(projection[first:count, 0:384])
    keys, values = projection[:count, 384:512], projection[:count, 512:640]
    scores = dot(queries, keys, ((1,), (1,))) * HEAD_WIDTH**-0.5
    scores = jnp.where(allowed, scores, MASKED_SCORE)
    weights = jnp.exp(scores - jnp.max(scores, axis=1, keepdims=True))
    probs = weights / jnp.sum(weights, axis=1, keepdims=True)
    rounded = probs.astype(BF16)
    return queries, keys, values, probs, rounded, dot(rounded, values)


def two_parts(value):
    high = value.astype(BF16)
    return high, (value - high.astype(F32)).astype(BF16)


def attention_kernel(small, own, received, upstream, advantage, out):
    scale = HEAD_WIDTH**-0.5
    projection = (own[...] + received[...]).astype(BF16)
    ref_projection, projection = projection[:, :COLS], projection[:, COLS:]
    grad_keys, grad_values = [0.0] * 3, [0.0] * 3
    for block in range(3):
        rows = slice(128 * block, 128 * (block + 1))
        out_ref = attend(small, ref_projection, block)[5]
        queries, keys, values, probs, rounded, out_policy = attend(small, projection, block)
        weight = jnp.concatenate([advantage[rows, :]] * 3, axis=0)
        grad_out = weight * heads(upstream[rows, :].astype(F32))
        grad_out = grad_out + KL_WEIGHT * (out_policy - out_ref)
        high, low = two_parts(grad_out * 12288**-0.5)
        grad_probs = dot(high, values, ((1,), (1,))) + dot(low, values, ((1,), (1,)))
        grad_scores = probs * (grad_probs - jnp.sum(grad_probs * probs, axis=1, keepdims=True))
        grad_scores = (grad_scores * scale).astype(BF16)
        grad_query = dot(grad_scores, keys)
        for i in range(3):
            out[rows, 128 * i : 128 * (i + 1)] = grad_query[128 * i : 128 * (i + 1)].astype(BF16)
        for_keys = dot(grad_scores, queries, ((0,), (0,)))
        for_values = dot(rounded, high, ((0,), (0,)))
        for k in range(block + 1):
            grad_keys[k] = grad_keys[k] + for_keys[128 * k : 128 * (k + 1)]
            grad_values[k] = grad_values[k] + for_values[128 * k : 128 * (k + 1)]
    for k in range(3):
        out[128 * k : 128 * (k + 1), 384:512] = grad_keys[k].astype(BF16)
        out[128 * k : 128 * (k + 1), 512:640] = grad_values[k].astype(BF16)


def attention(small, own, received, upstream, advantage):
    return pl.pallas_call(
        attention_kernel,
        out_shape=jax.ShapeDtypeStruct((ROWS, COLS), BF16),
        in_specs=[SMEM] + [VMEM] * 4,
        out_specs=VMEM,
        compiler_params=PARAMS,
        name="attention",
    )(small, own, received, upstream, advantage)


def gradient_dot(move, where, whole, far, last, grad):
    first, _, first_stride, second_stride = turned_place(where)
    parts = [(whole, 0), (far, 5 * HALF), (last, 7 * HALF)]
    rows = []
    for k in range(4):
        chunk = wrapped(first + move, 4) * first_stride + k * second_stride
        rows.append(chunk_rows(parts, slot_of(chunk, where[3])))
    return dot(jnp.concatenate(rows, axis=0), grad).astype(BF16)


PART = jax.ShapeDtypeStruct((4 * CHUNK, COLS), BF16)


def gradient_part(where, whole, far, last, own, other, move):
    def kernel(where, whole, far, last, own, other, out):
        grad = jnp.concatenate([own[...], other[...]], axis=0)
        out[...] = gradient_dot(move, where, whole, far, last, grad)

    return pl.pallas_call(
        kernel,
        out_shape=PART,
        in_specs=[SMEM] + [VMEM] * 5,
        out_specs=VMEM,
        compiler_params=PARAMS,
        name="gradient",
    )(where, whole, far, last, own, other)


def middle_kernel(where, own, *refs):
    pieces, outs = refs[:3], refs[3:]
    second = turned_place(where)[1]
    for move, out in zip((0, 1, -1, 2), outs):
        at = pl.ds(pl.multiple_of(wrapped(second + move, 4) * CHUNK, 16), CHUNK)
        total = (own[at, :].astype(F32) + pieces[0][at, :].astype(F32)) + (
            pieces[1][at, :].astype(F32) + pieces[2][at, :].astype(F32)
        )
        out[...] = total.astype(out.dtype)


def middle_sums(where, own, pieces):
    def shape(kind):
        return jax.ShapeDtypeStruct((CHUNK, COLS), kind)

    return pl.pallas_call(
        middle_kernel,
        out_shape=(shape(F32), shape(BF16), shape(BF16), shape(BF16)),
        in_specs=[SMEM] + [VMEM] * 4,
        out_specs=(VMEM,) * 4,
        compiler_params=PARAMS,
        name="middle",
    )(where, own, *pieces)


def final_kernel(own, first, second, third, out):
    out[:, 0, :] = (own[...] + first[...].astype(F32)) + (second[...].astype(F32) + third[...].astype(F32))


def final_sums(own, pieces):
    return pl.pallas_call(
        final_kernel,
        out_shape=jax.ShapeDtypeStruct((CHUNK, 1, COLS), F32),
        in_specs=[VMEM] * 4,
        out_specs=VMEM,
        compiler_params=PARAMS,
        name="final",
    )(own, *pieces)


def body(
    tokens,
    dest_shard,
    dest_offset,
    seg_lengths,
    rewards,
    groups,
    reference_head_weight,
    policy_head_weight,
    upstream,
):
    where = jnp.stack([lax.axis_index(name).astype(I32) for name in ("y", "x", "c", "z")])
    small = jnp.concatenate([where, rewards, groups, seg_lengths[0]])
    outgoing = route(rewards, groups, dest_shard, dest_offset, tokens)
    arrived = lax.all_to_all(outgoing, ("y", "x", "c"), split_axis=0, concat_axis=0, tiled=True)
    arrived, small = lax.optimization_barrier((arrived, small))
    _, weights, policy_weights = lax.optimization_barrier(
        (outgoing, reference_head_weight[:, 0], policy_head_weight[:, 0])
    )
    weights = jnp.concatenate([weights, policy_weights], axis=1)
    near = [weights, *(turned(weights, True, by) for by in (1, -1, 2))]
    block = place(arrived)
    _, near = lax.optimization_barrier((block, near))
    rows = join(near)
    across, right, left = (turned(rows, False, by) for by in (2, 1, -1))
    weights = [right, left, across]

    forward, backward = [block], [block]
    for _ in range(3):
        forward.append(shift(forward[-1], "z", 8, 1))
        backward.append(shift(backward[-1], "z", 8, -1))

    near = [forward[2], forward[1], block, backward[1], backward[2]]
    own, other, late, advantage, whole = project(small, arrived, near, rows)
    far = [backward[3], forward[3]]
    behind, ahead, own = lax.optimization_barrier((*far, own))
    first = shift(ahead[:CHUNK], "z", 8, 1)
    second = shift(behind[CHUNK:], "z", 8, -1)
    own, other, far = project_far(small, own, other, far, rows)
    swap = [(0, 1), (1, 0)]
    other, late = across_other(small, other, late, whole, far, weights)
    other, last = late_other(other, late, first, second)
    received = lax.ppermute(other, "c", swap)
    own = across_own(small, own, late, whole, far, last, weights)
    cotangent = upstream.reshape(ROWS, 3 * HEAD_WIDTH)
    grad = attention(small, own, received, cotangent, advantage)
    grad_other = lax.ppermute(grad, "c", swap)

    parts = []
    for move in (-1, 1, 2, 0):
        part = gradient_part(small, whole, far, last, grad, grad_other, move)
        parts.append(turned(part, True, move) if move else part)
    sums = middle_sums(small, parts[3], parts[:3])
    parts = [turned(part, False, move) for move, part in zip((1, -1, 2), sums[1:])]
    return final_sums(sums[0], parts)


def solution(mesh):
    split = Mesh(mesh.devices.reshape(4, 4, 2, 8), ("y", "x", "c", "z"))
    roll = ("y", "x", "c")
    in_specs = (
        P(roll, "z"),
        P(roll),
        P(roll),
        P(roll, None),
        P(roll),
        P(roll),
        P(roll, "z", None),
        P(roll, "z", None),
        P(roll, "z", None),
    )
    out_specs = P(roll, "z", None)
    return jax.shard_map(body, mesh=split, in_specs=in_specs, out_specs=out_specs, check_vma=False)
```

```python
import jax
import jax.numpy as jnp
from jax import lax
from jax.experimental import pallas as pl
from jax.experimental.pallas import tpu as pltpu
from jax.sharding import Mesh
from jax.sharding import PartitionSpec as P

HEAD_WIDTH = 128
KL_WEIGHT = 1.0
MASKED_SCORE = -1e30

ROWS = 384
CAP = 24
MODEL_BLOCK = 640
COLS = 640
CHUNK = 160
HALF = 2 * CHUNK
LANES = 384
F32 = jnp.float32
BF16 = jnp.bfloat16
I32 = jnp.int32

REWARDS, GROUPS, LENGTHS = 4, 8, 12
NOTE_HIGH, NOTE_LOW, NOTE_REWARD, NOTE_GROUP = 64, 65, 66, 70

VMEM = pl.BlockSpec(memory_space=pltpu.VMEM)
SMEM = pl.BlockSpec(memory_space=pltpu.SMEM)
HBM = pl.BlockSpec(memory_space=pltpu.HBM)
ALONE = pltpu.CompilerParams(vmem_limit_bytes=60 * 1024 * 1024)
PARAMS = pltpu.CompilerParams(vmem_limit_bytes=28 * 1024 * 1024)


def iota(shape, dim):
    return lax.broadcasted_iota(I32, shape, dim)


def dot(a, b, contract=((1,), (0,))):
    return lax.dot_general(a, b, (contract, ((), ())), preferred_element_type=F32)


def fetch(pairs, semaphores):
    copies = [pltpu.make_async_copy(source, to, semaphores.at[i]) for i, (source, to) in enumerate(pairs)]
    for copy in copies:
        copy.start()
    return copies


def shift(value, axis, size, by):
    return lax.ppermute(value, axis, [(i, (i + by) % size) for i in range(size)])


def turned(value, first, by):
    pairs = []
    for y in range(4):
        for x in range(4):
            for c in range(2):
                to_y, to_x = (y, (x + by) % 4) if (c == 0) == first else ((y + by) % 4, x)
                pairs.append((8 * y + 2 * x + c, 8 * to_y + 2 * to_x + c))
    return lax.ppermute(value, ("y", "x", "c"), pairs)


def turned_place(where):
    y, x, odd = where[0], where[1], where[2]
    first = jnp.where(odd == 0, x, y)
    second = jnp.where(odd == 0, y, x)
    stride = jnp.where(odd == 0, 1, 4)
    return first, second, stride, 5 - stride


def wrapped(index, size):
    return lax.rem(index + size, size)


def route_kernel(rewards, groups, shard, offset, tokens, out, landed, semaphores):
    copy = fetch([(tokens, landed)], semaphores)[0]
    shard_row = shard[...].reshape(1, ROWS)
    offset_row = offset[...].reshape(1, ROWS)
    table = iota((32, ROWS), 0) == shard_row
    before = (iota((ROWS, ROWS), 0) < iota((ROWS, ROWS), 1)).astype(BF16)
    counts = dot(table.astype(BF16), before)
    rank = jnp.sum(jnp.where(table, counts, 0.0), axis=0, keepdims=True).astype(I32)
    slot = shard_row * CAP + rank
    hot = iota((32 * CAP, ROWS), 0) == slot
    lane = iota((MODEL_BLOCK, 2 * LANES), 1)
    half = (lane >= LANES).astype(I32)
    within = lane - half * LANES
    source = jnp.where(within < CHUNK, within, within + CHUNK) + CHUNK * half
    pick = (iota((MODEL_BLOCK, 2 * LANES), 0) == source) & (within < HALF)
    copy.wait()
    ordered = dot(landed[...], pick.astype(BF16)).astype(BF16)
    gathered = dot(hot.astype(BF16), ordered)
    odd = shard_row & 1
    note_lane = iota((1, 128), 1)
    common = jnp.zeros((1, 128), F32)
    for i in range(4):
        common = jnp.where(note_lane == NOTE_REWARD + i, rewards[i].astype(F32), common)
        common = jnp.where(note_lane == NOTE_GROUP + i, groups[i].astype(F32), common)
    for core in range(2):
        place = offset_row + 1 + ROWS * (odd ^ core)
        mark = jnp.sum(jnp.where(hot, place, 0), axis=1, keepdims=True)
        high = (mark >> 4).astype(F32)
        low = (mark & 15).astype(F32)
        notes = jnp.where(note_lane == NOTE_HIGH, high, jnp.where(note_lane == NOTE_LOW, low, common))
        first = LANES * core
        plain = gathered[:, first : first + 256].astype(BF16)
        last = (gathered[:, first + 256 : first + 384] + notes).astype(BF16)
        for chip in range(16):
            rows = slice(2 * CAP * chip, 2 * CAP * (chip + 1))
            out[2 * chip + core, :, 0:256] = plain[rows]
            out[2 * chip + core, :, 256:384] = last[rows]


def route(rewards, groups, shard, offset, tokens):
    return pl.pallas_call(
        route_kernel,
        out_shape=jax.ShapeDtypeStruct((32, 2 * CAP, LANES), BF16),
        in_specs=[SMEM, SMEM, VMEM, VMEM, HBM],
        out_specs=VMEM,
        scratch_shapes=[pltpu.VMEM((ROWS, MODEL_BLOCK), BF16), pltpu.SemaphoreType.DMA((1,))],
        compiler_params=ALONE,
        name="route",
    )(rewards, groups, shard, offset, tokens)


def place_kernel(arrived, out):
    rows = arrived[...].reshape(32 * 2 * CAP, LANES)
    notes = rows[:, 256:384].astype(F32)
    note_lane = iota((1, 128), 1)
    weight = jnp.where(note_lane == NOTE_HIGH, 16.0, jnp.where(note_lane == NOTE_LOW, 1.0, 0.0))
    mark = jnp.sum(notes * weight, axis=1, keepdims=True).astype(I32) - 1
    hot = (mark == iota((32 * 2 * CAP, 2 * ROWS), 1)).astype(BF16)
    out[...] = dot(rows, hot, ((0,), (0,)))[:HALF].astype(BF16)


def place(arrived):
    return pl.pallas_call(
        place_kernel,
        out_shape=jax.ShapeDtypeStruct((HALF, 2 * ROWS), BF16),
        in_specs=[VMEM],
        out_specs=VMEM,
        compiler_params=PARAMS,
        name="place",
    )(arrived)


def row_advantages(reward, group, small):
    position = iota((ROWS, 128), 0)
    result = jnp.zeros((ROWS, 128), F32)
    start = 0
    for i in range(4):
        member = group == small[GROUPS + i].astype(F32)
        count = jnp.sum(jnp.where(member, 1.0, 0.0), keepdims=True)
        total = jnp.sum(jnp.where(member, reward, 0.0), keepdims=True)
        square = jnp.sum(jnp.where(member, reward * reward, 0.0), keepdims=True)
        mean = total / count
        spread = jnp.maximum(jnp.sqrt(count * square - total * total) / count, 1.0)
        advantage = (small[REWARDS + i].astype(F32) - mean) / spread
        result = jnp.where(position >= start, advantage, result)
        start = start + small[LENGTHS + i]
    return result


def stack(pieces, out):
    at = 0
    for piece in pieces:
        out[at : at + piece.shape[0], :] = piece[...]
        at += piece.shape[0]


def join_kernel(*refs):
    stack(refs[:-1], refs[-1])


def join(pieces):
    return pl.pallas_call(
        join_kernel,
        out_shape=jax.ShapeDtypeStruct((4 * CHUNK, 2 * COLS), BF16),
        in_specs=[VMEM] * 4,
        out_specs=VMEM,
        compiler_params=PARAMS,
        name="join",
    )(*pieces)


STEPS = (-2, -1, 0, 1, 2, 3, -3, 4)


def slot_of(chunk, z):
    at = wrapped(lax.div(chunk, 2) - z + 2, 8)
    at = jnp.where(at == 6, 7, jnp.where(at == 7, 6, at))
    return pl.multiple_of((2 * at + lax.rem(chunk, 2)) * CHUNK, 16)


def chunk_rows(parts, slot):
    total = None
    for part, begin in parts:
        inside = (slot >= begin) & (slot < begin + part.shape[0])
        at = pl.multiple_of(jnp.where(inside, slot - begin, 0), 16)
        rows = part[pl.ds(at, CHUNK), :]
        rows = jnp.where(inside, rows, jnp.zeros_like(rows))
        total = rows if total is None else total + rows
    return total


def chunk_slots(where, step):
    first, second, first_stride, second_stride = turned_place(where)
    at = wrapped(second + step, 4) * second_stride
    return [slot_of(wrapped(first + near, 4) * first_stride + at, where[3]) for near in (0, -1, 1, 2)]


def chunk_slot(where, step, k):
    first, second, first_stride, second_stride = turned_place(where)
    near = jnp.where(k == 0, 0, jnp.where(k == 1, -1, k - 1))
    chunk = wrapped(first + near, 4) * first_stride + wrapped(second + step, 4) * second_stride
    return slot_of(chunk, where[3])


def keep_late(where, step, piece, late):
    def keep(k, carry):
        slot = chunk_slot(where, step, k)

        @pl.when(slot >= 7 * HALF)
        def _():
            at = pl.ds(pl.multiple_of(slot - 7 * HALF, 16), CHUNK)
            late[at, :] = piece[pl.ds(pl.multiple_of(k * CHUNK, 16), CHUNK), :]

        return carry

    lax.fori_loop(0, 4, keep, 0)


def project_kernel(where, arrived, *refs):
    tokens, piece = refs[:5], refs[5]
    own, other, late, advantage, whole = refs[6:]
    note = arrived[:, 0:16, 256:384][:, 0, :].astype(F32)
    advantage[...] = row_advantages(
        note[:, NOTE_REWARD : NOTE_REWARD + 4], note[:, NOTE_GROUP : NOTE_GROUP + 4], where
    )
    stack(tokens, whole)
    keep_late(where, 0, piece, late)
    rows = [chunk_rows([(whole, 0)], slot) for slot in chunk_slots(where, 0)]
    rows = jnp.concatenate(rows, axis=0)
    own[...] = dot(rows[:, :ROWS], piece[...], ((0,), (0,)))
    other[...] = dot(rows[:, ROWS:], piece[...], ((0,), (0,)))


SUMS = jax.ShapeDtypeStruct((ROWS, 2 * COLS), F32)
LATE = jax.ShapeDtypeStruct((HALF, 2 * COLS), BF16)


def project(where, arrived, tokens, piece):
    whole = jax.ShapeDtypeStruct((5 * HALF, 2 * ROWS), BF16)
    return pl.pallas_call(
        project_kernel,
        out_shape=(SUMS, SUMS, LATE, jax.ShapeDtypeStruct((ROWS, 128), F32), whole),
        in_specs=[SMEM] + [VMEM] * 7,
        out_specs=(VMEM,) * 5,
        compiler_params=PARAMS,
        name="project",
    )(where, arrived, *tokens, piece)


def far_kernel(where, own, other, *refs):
    tokens, piece = refs[:2], refs[2]
    own_out, other_out, far = refs[3:]
    stack(tokens, far)
    own_out[...] = own[...]
    other_out[...] = other[...]

    def add(k, carry):
        slot = chunk_slot(where, 0, k)

        @pl.when((slot >= 5 * HALF) & (slot < 7 * HALF))
        def _():
            at = pl.ds(pl.multiple_of(slot - 5 * HALF, 16), CHUNK)
            weights = piece[pl.ds(pl.multiple_of(k * CHUNK, 16), CHUNK), :]
            own_out[...] += dot(far[at, :ROWS], weights, ((0,), (0,)))
            other_out[...] += dot(far[at, ROWS:], weights, ((0,), (0,)))

        return carry

    lax.fori_loop(0, 4, add, 0)


def project_far(where, own, other, tokens, piece):
    far = jax.ShapeDtypeStruct((2 * HALF, 2 * ROWS), BF16)
    return pl.pallas_call(
        far_kernel,
        out_shape=(SUMS, SUMS, far),
        in_specs=[SMEM] + [VMEM] * 5,
        out_specs=(VMEM,) * 3,
        compiler_params=PARAMS,
        name="far",
    )(where, own, other, *tokens, piece)


def across_sum(where, columns, whole, far, pieces):
    total = None
    for piece, step in zip(pieces, (-1, 1, 2)):
        parts = [(whole.at[:, columns], 0), (far.at[:, columns], 5 * HALF)]
        rows = jnp.concatenate([chunk_rows(parts, slot) for slot in chunk_slots(where, step)], axis=0)
        result = dot(rows, piece[...], ((0,), (0,)))
        total = result if total is None else total + result
    return total


def across_other(where, other, late, whole, far, pieces):
    def kernel(where, other, late, whole, far, *refs):
        pieces, (out, late_out) = refs[:3], refs[3:]
        late_out[...] = late[...]
        for piece, step in zip(pieces, (-1, 1, 2)):
            keep_late(where, step, piece, late_out)
        out[...] = other[...] + across_sum(where, pl.ds(ROWS, ROWS), whole, far, pieces)

    return pl.pallas_call(
        kernel,
        out_shape=(SUMS, LATE),
        in_specs=[SMEM] + [VMEM] * 7,
        out_specs=(VMEM,) * 2,
        compiler_params=PARAMS,
        name="across_other",
    )(where, other, late, whole, far, *pieces)


def late_other(other, late, first, second):
    def kernel(other, late, first, second, out, tokens):
        stack([first, second], tokens)
        out[...] = other[...] + dot(tokens[:, ROWS:], late[...], ((0,), (0,)))

    return pl.pallas_call(
        kernel,
        out_shape=(SUMS, jax.ShapeDtypeStruct((HALF, 2 * ROWS), BF16)),
        in_specs=[VMEM] * 4,
        out_specs=(VMEM,) * 2,
        compiler_params=PARAMS,
        name="late",
    )(other, late, first, second)


def across_own(where, own, late, whole, far, last, pieces):
    def kernel(where, own, late, whole, far, last, *refs):
        pieces, out = refs[:3], refs[3]
        total = across_sum(where, pl.ds(0, ROWS), whole, far, pieces)
        out[...] = own[...] + total + dot(last[:, :ROWS], late[...], ((0,), (0,)))

    return pl.pallas_call(
        kernel,
        out_shape=SUMS,
        in_specs=[SMEM] + [VMEM] * 8,
        out_specs=VMEM,
        compiler_params=PARAMS,
        name="across_own",
    )(where, own, late, whole, far, last, *pieces)


def heads(value):
    return jnp.concatenate([value[:, 128 * i : 128 * (i + 1)] for i in range(3)], axis=0)


def attend(small, projection, block):
    first, count = 128 * block, 128 * (block + 1)
    key_at = iota((128, count), 1)
    query_at = first + iota((128, count), 0)
    row_at = first + iota((128, 1), 0)
    begin = jnp.zeros((128, 1), I32)
    start = 0
    for i in range(4):
        begin = jnp.where(row_at >= start, start, begin)
        start = start + small[LENGTHS + i]
    allowed = (key_at <= query_at) & (key_at >= begin)
    allowed = jnp.concatenate([allowed] * 3, axis=0)
    queries = heads(projection[first:count, 0:384])
    keys, values = projection[:count, 384:512], projection[:count, 512:640]
    scores = dot(queries, keys, ((1,), (1,))) * HEAD_WIDTH**-0.5
    scores = jnp.where(allowed, scores, MASKED_SCORE)
    weights = jnp.exp(scores - jnp.max(scores, axis=1, keepdims=True))
    probs = weights / jnp.sum(weights, axis=1, keepdims=True)
    rounded = probs.astype(BF16)
    return queries, keys, values, probs, rounded, dot(rounded, values)


def two_parts(value):
    high = value.astype(BF16)
    return high, (value - high.astype(F32)).astype(BF16)


def attention_kernel(small, own, received, upstream, advantage, out):
    scale = HEAD_WIDTH**-0.5
    projection = (own[...] + received[...]).astype(BF16)
    ref_projection, projection = projection[:, :COLS], projection[:, COLS:]
    grad_keys, grad_values = [0.0] * 3, [0.0] * 3
    for block in range(3):
        rows = slice(128 * block, 128 * (block + 1))
        out_ref = attend(small, ref_projection, block)[5]
        queries, keys, values, probs, rounded, out_policy = attend(small, projection, block)
        weight = jnp.concatenate([advantage[rows, :]] * 3, axis=0)
        grad_out = weight * heads(upstream[rows, :].astype(F32))
        grad_out = grad_out + KL_WEIGHT * (out_policy - out_ref)
        high, low = two_parts(grad_out * 12288**-0.5)
        grad_probs = dot(high, values, ((1,), (1,))) + dot(low, values, ((1,), (1,)))
        grad_scores = probs * (grad_probs - jnp.sum(grad_probs * probs, axis=1, keepdims=True))
        grad_scores = (grad_scores * scale).astype(BF16)
        grad_query = dot(grad_scores, keys)
        for i in range(3):
            out[rows, 128 * i : 128 * (i + 1)] = grad_query[128 * i : 128 * (i + 1)].astype(BF16)
        for_keys = dot(grad_scores, queries, ((0,), (0,)))
        for_values = dot(rounded, high, ((0,), (0,)))
        for k in range(block + 1):
            grad_keys[k] = grad_keys[k] + for_keys[128 * k : 128 * (k + 1)]
            grad_values[k] = grad_values[k] + for_values[128 * k : 128 * (k + 1)]
    for k in range(3):
        out[128 * k : 128 * (k + 1), 384:512] = grad_keys[k].astype(BF16)
        out[128 * k : 128 * (k + 1), 512:640] = grad_values[k].astype(BF16)


def attention(small, own, received, upstream, advantage):
    return pl.pallas_call(
        attention_kernel,
        out_shape=jax.ShapeDtypeStruct((ROWS, COLS), BF16),
        in_specs=[SMEM] + [VMEM] * 4,
        out_specs=VMEM,
        compiler_params=PARAMS,
        name="attention",
    )(small, own, received, upstream, advantage)


def gradient_dot(move, where, whole, far, last, grad):
    first, _, first_stride, second_stride = turned_place(where)
    parts = [(whole, 0), (far, 5 * HALF), (last, 7 * HALF)]
    rows = []
    for k in range(4):
        chunk = wrapped(first + move, 4) * first_stride + k * second_stride
        rows.append(chunk_rows(parts, slot_of(chunk, where[3])))
    return dot(jnp.concatenate(rows, axis=0), grad).astype(BF16)


PART = jax.ShapeDtypeStruct((4 * CHUNK, COLS), BF16)


def gradient_part(where, whole, far, last, own, other, move):
    def kernel(where, whole, far, last, own, other, out):
        grad = jnp.concatenate([own[...], other[...]], axis=0)
        out[...] = gradient_dot(move, where, whole, far, last, grad)

    return pl.pallas_call(
        kernel,
        out_shape=PART,
        in_specs=[SMEM] + [VMEM] * 5,
        out_specs=VMEM,
        compiler_params=PARAMS,
        name="gradient",
    )(where, whole, far, last, own, other)


def early_gradient(where, whole, far, last, own, move):
    def kernel(where, whole, far, last, own, out, other_rows):
        parts = [(whole, 0), (far, 5 * HALF), (last, 7 * HALF)]
        first, _, first_stride, second_stride = turned_place(where)
        rows = []
        for k in range(4):
            chunk = wrapped(first + move, 4) * first_stride + k * second_stride
            rows.append(chunk_rows(parts, slot_of(chunk, where[3])))
        rows = jnp.concatenate(rows, axis=0)
        other_rows[...] = rows[:, ROWS:]
        out[...] = dot(rows[:, :ROWS], own[...])

    return pl.pallas_call(
        kernel,
        out_shape=(
            jax.ShapeDtypeStruct((4 * CHUNK, COLS), F32),
            jax.ShapeDtypeStruct((4 * CHUNK, ROWS), BF16),
        ),
        in_specs=[SMEM] + [VMEM] * 4,
        out_specs=(VMEM,) * 2,
        compiler_params=PARAMS,
        name="early",
    )(where, whole, far, last, own)


def rest_gradient(early, rows, other):
    def kernel(early, rows, other, out):
        out[...] = (early[...] + dot(rows[...], other[...])).astype(BF16)

    return pl.pallas_call(
        kernel,
        out_shape=PART,
        in_specs=[VMEM] * 3,
        out_specs=VMEM,
        compiler_params=PARAMS,
        name="rest",
    )(early, rows, other)


def middle_kernel(where, own, *refs):
    pieces, outs = refs[:3], refs[3:]
    second = turned_place(where)[1]
    for move, out in zip((0, 1, -1, 2), outs):
        at = pl.ds(pl.multiple_of(wrapped(second + move, 4) * CHUNK, 16), CHUNK)
        total = (own[at, :].astype(F32) + pieces[0][at, :].astype(F32)) + (
            pieces[1][at, :].astype(F32) + pieces[2][at, :].astype(F32)
        )
        out[...] = total.astype(out.dtype)


def middle_sums(where, own, pieces):
    def shape(kind):
        return jax.ShapeDtypeStruct((CHUNK, COLS), kind)

    return pl.pallas_call(
        middle_kernel,
        out_shape=(shape(F32), shape(BF16), shape(BF16), shape(BF16)),
        in_specs=[SMEM] + [VMEM] * 4,
        out_specs=(VMEM,) * 4,
        compiler_params=PARAMS,
        name="middle",
    )(where, own, *pieces)


def final_kernel(own, first, second, third, out):
    out[:, 0, :] = (own[...] + first[...].astype(F32)) + (second[...].astype(F32) + third[...].astype(F32))


def final_sums(own, pieces):
    return pl.pallas_call(
        final_kernel,
        out_shape=jax.ShapeDtypeStruct((CHUNK, 1, COLS), F32),
        in_specs=[VMEM] * 4,
        out_specs=VMEM,
        compiler_params=PARAMS,
        name="final",
    )(own, *pieces)


def body(
    tokens,
    dest_shard,
    dest_offset,
    seg_lengths,
    rewards,
    groups,
    reference_head_weight,
    policy_head_weight,
    upstream,
):
    where = jnp.stack([lax.axis_index(name).astype(I32) for name in ("y", "x", "c", "z")])
    small = jnp.concatenate([where, rewards, groups, seg_lengths[0]])
    outgoing = route(rewards, groups, dest_shard, dest_offset, tokens)
    arrived = lax.all_to_all(outgoing, ("y", "x", "c"), split_axis=0, concat_axis=0, tiled=True)
    arrived, small = lax.optimization_barrier((arrived, small))
    _, weights, policy_weights = lax.optimization_barrier(
        (outgoing, reference_head_weight[:, 0], policy_head_weight[:, 0])
    )
    weights = jnp.concatenate([weights, policy_weights], axis=1)
    near = [weights, *(turned(weights, True, by) for by in (1, -1, 2))]
    block = place(arrived)
    _, near = lax.optimization_barrier((block, near))
    rows = join(near)
    across, right, left = (turned(rows, False, by) for by in (2, 1, -1))
    weights = [right, left, across]

    forward, backward = [block], [block]
    for _ in range(3):
        forward.append(shift(forward[-1], "z", 8, 1))
        backward.append(shift(backward[-1], "z", 8, -1))

    near = [forward[2], forward[1], block, backward[1], backward[2]]
    own, other, late, advantage, whole = project(small, arrived, near, rows)
    far = [backward[3], forward[3]]
    behind, ahead, own = lax.optimization_barrier((*far, own))
    first = shift(ahead[:CHUNK], "z", 8, 1)
    second = shift(behind[CHUNK:], "z", 8, -1)
    own, other, far = project_far(small, own, other, far, rows)
    swap = [(0, 1), (1, 0)]
    other, late = across_other(small, other, late, whole, far, weights)
    other, last = late_other(other, late, first, second)
    received = lax.ppermute(other, "c", swap)
    own = across_own(small, own, late, whole, far, last, weights)
    cotangent = upstream.reshape(ROWS, 3 * HEAD_WIDTH)
    grad = attention(small, own, received, cotangent, advantage)
    grad_other = lax.ppermute(grad, "c", swap)
    early, early_rows = early_gradient(small, whole, far, last, grad, 2)

    parts = []
    for move in (-1, 1, 2, 0):
        if move == 2:
            part = rest_gradient(early, early_rows, grad_other)
        else:
            part = gradient_part(small, whole, far, last, grad, grad_other, move)
        parts.append(turned(part, True, move) if move else part)
    sums = middle_sums(small, parts[3], parts[:3])
    parts = [turned(part, False, move) for move, part in zip((1, -1, 2), sums[1:])]
    return final_sums(sums[0], parts)


def solution(mesh):
    split = Mesh(mesh.devices.reshape(4, 4, 2, 8), ("y", "x", "c", "z"))
    roll = ("y", "x", "c")
    in_specs = (
        P(roll, "z"),
        P(roll),
        P(roll),
        P(roll, None),
        P(roll),
        P(roll),
        P(roll, "z", None),
        P(roll, "z", None),
        P(roll, "z", None),
    )
    out_specs = P(roll, "z", None)
    return jax.shard_map(body, mesh=split, in_specs=in_specs, out_specs=out_specs, check_vma=False)
```

```python
import jax
import jax.numpy as jnp
from jax import lax
from jax.experimental import pallas as pl
from jax.experimental.pallas import tpu as pltpu
from jax.sharding import Mesh
from jax.sharding import PartitionSpec as P

HEAD_WIDTH = 128
KL_WEIGHT = 1.0
MASKED_SCORE = -1e30

ROWS = 384
CAP = 24
MODEL_BLOCK = 640
COLS = 640
CHUNK = 160
HALF = 2 * CHUNK
LANES = 384
F32 = jnp.float32
BF16 = jnp.bfloat16
I32 = jnp.int32

REWARDS, GROUPS, LENGTHS = 4, 8, 12
NOTE_HIGH, NOTE_LOW, NOTE_REWARD, NOTE_GROUP = 64, 65, 66, 70

VMEM = pl.BlockSpec(memory_space=pltpu.VMEM)
SMEM = pl.BlockSpec(memory_space=pltpu.SMEM)
HBM = pl.BlockSpec(memory_space=pltpu.HBM)
ALONE = pltpu.CompilerParams(vmem_limit_bytes=60 * 1024 * 1024)
PARAMS = pltpu.CompilerParams(vmem_limit_bytes=28 * 1024 * 1024)


def iota(shape, dim):
    return lax.broadcasted_iota(I32, shape, dim)


def dot(a, b, contract=((1,), (0,))):
    return lax.dot_general(a, b, (contract, ((), ())), preferred_element_type=F32)


def fetch(pairs, semaphores):
    copies = [pltpu.make_async_copy(source, to, semaphores.at[i]) for i, (source, to) in enumerate(pairs)]
    for copy in copies:
        copy.start()
    return copies


def shift(value, axis, size, by):
    return lax.ppermute(value, axis, [(i, (i + by) % size) for i in range(size)])


def turned(value, first, by):
    pairs = []
    for y in range(4):
        for x in range(4):
            for c in range(2):
                to_y, to_x = (y, (x + by) % 4) if (c == 0) == first else ((y + by) % 4, x)
                pairs.append((8 * y + 2 * x + c, 8 * to_y + 2 * to_x + c))
    return lax.ppermute(value, ("y", "x", "c"), pairs)


def turned_place(where):
    y, x, odd = where[0], where[1], where[2]
    first = jnp.where(odd == 0, x, y)
    second = jnp.where(odd == 0, y, x)
    stride = jnp.where(odd == 0, 1, 4)
    return first, second, stride, 5 - stride


def wrapped(index, size):
    return lax.rem(index + size, size)


def route_kernel(rewards, groups, shard, offset, tokens, out, landed, semaphores):
    copy = fetch([(tokens, landed)], semaphores)[0]
    shard_row = shard[...].reshape(1, ROWS)
    offset_row = offset[...].reshape(1, ROWS)
    table = iota((32, ROWS), 0) == shard_row
    before = (iota((ROWS, ROWS), 0) < iota((ROWS, ROWS), 1)).astype(BF16)
    counts = dot(table.astype(BF16), before)
    rank = jnp.sum(jnp.where(table, counts, 0.0), axis=0, keepdims=True).astype(I32)
    slot = shard_row * CAP + rank
    hot = iota((32 * CAP, ROWS), 0) == slot
    lane = iota((MODEL_BLOCK, 2 * LANES), 1)
    half = (lane >= LANES).astype(I32)
    within = lane - half * LANES
    source = jnp.where(within < CHUNK, within, within + CHUNK) + CHUNK * half
    pick = (iota((MODEL_BLOCK, 2 * LANES), 0) == source) & (within < HALF)
    copy.wait()
    ordered = dot(landed[...], pick.astype(BF16)).astype(BF16)
    gathered = dot(hot.astype(BF16), ordered)
    odd = shard_row & 1
    note_lane = iota((1, 128), 1)
    common = jnp.zeros((1, 128), F32)
    for i in range(4):
        common = jnp.where(note_lane == NOTE_REWARD + i, rewards[i].astype(F32), common)
        common = jnp.where(note_lane == NOTE_GROUP + i, groups[i].astype(F32), common)
    for core in range(2):
        place = offset_row + 1 + ROWS * (odd ^ core)
        mark = jnp.sum(jnp.where(hot, place, 0), axis=1, keepdims=True)
        high = (mark >> 4).astype(F32)
        low = (mark & 15).astype(F32)
        notes = jnp.where(note_lane == NOTE_HIGH, high, jnp.where(note_lane == NOTE_LOW, low, common))
        first = LANES * core
        plain = gathered[:, first : first + 256].astype(BF16)
        last = (gathered[:, first + 256 : first + 384] + notes).astype(BF16)
        for chip in range(16):
            rows = slice(2 * CAP * chip, 2 * CAP * (chip + 1))
            out[2 * chip + core, :, 0:256] = plain[rows]
            out[2 * chip + core, :, 256:384] = last[rows]


def route(rewards, groups, shard, offset, tokens):
    return pl.pallas_call(
        route_kernel,
        out_shape=jax.ShapeDtypeStruct((32, 2 * CAP, LANES), BF16),
        in_specs=[SMEM, SMEM, VMEM, VMEM, HBM],
        out_specs=VMEM,
        scratch_shapes=[pltpu.VMEM((ROWS, MODEL_BLOCK), BF16), pltpu.SemaphoreType.DMA((1,))],
        compiler_params=ALONE,
        name="route",
    )(rewards, groups, shard, offset, tokens)


def place_kernel(arrived, out):
    rows = arrived[...].reshape(32 * 2 * CAP, LANES)
    notes = rows[:, 256:384].astype(F32)
    note_lane = iota((1, 128), 1)
    weight = jnp.where(note_lane == NOTE_HIGH, 16.0, jnp.where(note_lane == NOTE_LOW, 1.0, 0.0))
    mark = jnp.sum(notes * weight, axis=1, keepdims=True).astype(I32) - 1
    hot = (mark == iota((32 * 2 * CAP, 2 * ROWS), 1)).astype(BF16)
    out[...] = dot(rows, hot, ((0,), (0,)))[:HALF].astype(BF16)


def place(arrived):
    return pl.pallas_call(
        place_kernel,
        out_shape=jax.ShapeDtypeStruct((HALF, 2 * ROWS), BF16),
        in_specs=[VMEM],
        out_specs=VMEM,
        compiler_params=PARAMS,
        name="place",
    )(arrived)


def row_advantages(reward, group, small):
    position = iota((ROWS, 128), 0)
    result = jnp.zeros((ROWS, 128), F32)
    start = 0
    for i in range(4):
        member = group == small[GROUPS + i].astype(F32)
        count = jnp.sum(jnp.where(member, 1.0, 0.0), keepdims=True)
        total = jnp.sum(jnp.where(member, reward, 0.0), keepdims=True)
        square = jnp.sum(jnp.where(member, reward * reward, 0.0), keepdims=True)
        mean = total / count
        spread = jnp.maximum(jnp.sqrt(count * square - total * total) / count, 1.0)
        advantage = (small[REWARDS + i].astype(F32) - mean) / spread
        result = jnp.where(position >= start, advantage, result)
        start = start + small[LENGTHS + i]
    return result


def stack(pieces, out):
    at = 0
    for piece in pieces:
        out[at : at + piece.shape[0], :] = piece[...]
        at += piece.shape[0]


def join_kernel(*refs):
    stack(refs[:-1], refs[-1])


def join(pieces):
    return pl.pallas_call(
        join_kernel,
        out_shape=jax.ShapeDtypeStruct((4 * CHUNK, 2 * COLS), BF16),
        in_specs=[VMEM] * 4,
        out_specs=VMEM,
        compiler_params=PARAMS,
        name="join",
    )(*pieces)


STEPS = (-2, -1, 0, 1, 2, 3, -3, 4)


def slot_of(chunk, z):
    at = wrapped(lax.div(chunk, 2) - z + 2, 8)
    at = jnp.where(at == 6, 7, jnp.where(at == 7, 6, at))
    return pl.multiple_of((2 * at + lax.rem(chunk, 2)) * CHUNK, 16)


def chunk_rows(parts, slot):
    total = None
    for part, begin in parts:
        inside = (slot >= begin) & (slot < begin + part.shape[0])
        at = pl.multiple_of(jnp.where(inside, slot - begin, 0), 16)
        rows = part[pl.ds(at, CHUNK), :]
        rows = jnp.where(inside, rows, jnp.zeros_like(rows))
        total = rows if total is None else total + rows
    return total


def chunk_slots(where, step):
    first, second, first_stride, second_stride = turned_place(where)
    at = wrapped(second + step, 4) * second_stride
    return [slot_of(wrapped(first + near, 4) * first_stride + at, where[3]) for near in (0, -1, 1, 2)]


def chunk_slot(where, step, k):
    first, second, first_stride, second_stride = turned_place(where)
    near = jnp.where(k == 0, 0, jnp.where(k == 1, -1, k - 1))
    chunk = wrapped(first + near, 4) * first_stride + wrapped(second + step, 4) * second_stride
    return slot_of(chunk, where[3])


def keep_late(where, step, piece, late):
    def keep(k, carry):
        slot = chunk_slot(where, step, k)

        @pl.when(slot >= 7 * HALF)
        def _():
            at = pl.ds(pl.multiple_of(slot - 7 * HALF, 16), CHUNK)
            late[at, :] = piece[pl.ds(pl.multiple_of(k * CHUNK, 16), CHUNK), :]

        return carry

    lax.fori_loop(0, 4, keep, 0)


def project_kernel(where, arrived, *refs):
    tokens, piece = refs[:5], refs[5]
    own, other, late, advantage, whole = refs[6:]
    note = arrived[:, 0:16, 256:384][:, 0, :].astype(F32)
    advantage[...] = row_advantages(
        note[:, NOTE_REWARD : NOTE_REWARD + 4], note[:, NOTE_GROUP : NOTE_GROUP + 4], where
    )
    stack(tokens, whole)
    keep_late(where, 0, piece, late)
    rows = [chunk_rows([(whole, 0)], slot) for slot in chunk_slots(where, 0)]
    rows = jnp.concatenate(rows, axis=0)
    own[...] = dot(rows[:, :ROWS], piece[...], ((0,), (0,)))
    other[...] = dot(rows[:, ROWS:], piece[...], ((0,), (0,)))


SUMS = jax.ShapeDtypeStruct((ROWS, 2 * COLS), F32)
LATE = jax.ShapeDtypeStruct((HALF, 2 * COLS), BF16)


def project(where, arrived, tokens, piece):
    whole = jax.ShapeDtypeStruct((5 * HALF, 2 * ROWS), BF16)
    return pl.pallas_call(
        project_kernel,
        out_shape=(SUMS, SUMS, LATE, jax.ShapeDtypeStruct((ROWS, 128), F32), whole),
        in_specs=[SMEM] + [VMEM] * 7,
        out_specs=(VMEM,) * 5,
        compiler_params=PARAMS,
        name="project",
    )(where, arrived, *tokens, piece)


def far_kernel(where, own, other, *refs):
    tokens, piece = refs[:2], refs[2]
    own_out, other_out, far = refs[3:]
    stack(tokens, far)
    own_out[...] = own[...]
    other_out[...] = other[...]

    def add(k, carry):
        slot = chunk_slot(where, 0, k)

        @pl.when((slot >= 5 * HALF) & (slot < 7 * HALF))
        def _():
            at = pl.ds(pl.multiple_of(slot - 5 * HALF, 16), CHUNK)
            weights = piece[pl.ds(pl.multiple_of(k * CHUNK, 16), CHUNK), :]
            own_out[...] += dot(far[at, :ROWS], weights, ((0,), (0,)))
            other_out[...] += dot(far[at, ROWS:], weights, ((0,), (0,)))

        return carry

    lax.fori_loop(0, 4, add, 0)


def project_far(where, own, other, tokens, piece):
    far = jax.ShapeDtypeStruct((2 * HALF, 2 * ROWS), BF16)
    return pl.pallas_call(
        far_kernel,
        out_shape=(SUMS, SUMS, far),
        in_specs=[SMEM] + [VMEM] * 5,
        out_specs=(VMEM,) * 3,
        compiler_params=PARAMS,
        name="far",
    )(where, own, other, *tokens, piece)


def across_sum(where, columns, whole, far, pieces):
    total = None
    for piece, step in zip(pieces, (-1, 1, 2)):
        parts = [(whole.at[:, columns], 0), (far.at[:, columns], 5 * HALF)]
        rows = jnp.concatenate([chunk_rows(parts, slot) for slot in chunk_slots(where, step)], axis=0)
        result = dot(rows, piece[...], ((0,), (0,)))
        total = result if total is None else total + result
    return total


def across_other(where, other, late, whole, far, pieces):
    def kernel(where, other, late, whole, far, *refs):
        pieces, (out, late_out) = refs[:3], refs[3:]
        late_out[...] = late[...]
        for piece, step in zip(pieces, (-1, 1, 2)):
            keep_late(where, step, piece, late_out)
        out[...] = other[...] + across_sum(where, pl.ds(ROWS, ROWS), whole, far, pieces)

    return pl.pallas_call(
        kernel,
        out_shape=(SUMS, LATE),
        in_specs=[SMEM] + [VMEM] * 7,
        out_specs=(VMEM,) * 2,
        compiler_params=PARAMS,
        name="across_other",
    )(where, other, late, whole, far, *pieces)


def late_other(other, late, first, second):
    def kernel(other, late, first, second, out, tokens):
        stack([first, second], tokens)
        out[...] = other[...] + dot(tokens[:, ROWS:], late[...], ((0,), (0,)))

    return pl.pallas_call(
        kernel,
        out_shape=(SUMS, jax.ShapeDtypeStruct((HALF, 2 * ROWS), BF16)),
        in_specs=[VMEM] * 4,
        out_specs=(VMEM,) * 2,
        compiler_params=PARAMS,
        name="late",
    )(other, late, first, second)


def across_own(where, own, late, whole, far, last, pieces):
    def kernel(where, own, late, whole, far, last, *refs):
        pieces, out = refs[:3], refs[3]
        total = across_sum(where, pl.ds(0, ROWS), whole, far, pieces)
        out[...] = own[...] + total + dot(last[:, :ROWS], late[...], ((0,), (0,)))

    return pl.pallas_call(
        kernel,
        out_shape=SUMS,
        in_specs=[SMEM] + [VMEM] * 8,
        out_specs=VMEM,
        compiler_params=PARAMS,
        name="across_own",
    )(where, own, late, whole, far, last, *pieces)


def heads(value):
    return jnp.concatenate([value[:, 128 * i : 128 * (i + 1)] for i in range(3)], axis=0)


def attend(small, projection, block):
    first, count = 128 * block, 128 * (block + 1)
    key_at = iota((128, count), 1)
    query_at = first + iota((128, count), 0)
    row_at = first + iota((128, 1), 0)
    begin = jnp.zeros((128, 1), I32)
    start = 0
    for i in range(4):
        begin = jnp.where(row_at >= start, start, begin)
        start = start + small[LENGTHS + i]
    allowed = (key_at <= query_at) & (key_at >= begin)
    allowed = jnp.concatenate([allowed] * 3, axis=0)
    queries = heads(projection[first:count, 0:384])
    keys, values = projection[:count, 384:512], projection[:count, 512:640]
    scores = dot(queries, keys, ((1,), (1,))) * HEAD_WIDTH**-0.5
    scores = jnp.where(allowed, scores, MASKED_SCORE)
    weights = jnp.exp(scores - jnp.max(scores, axis=1, keepdims=True))
    probs = weights / jnp.sum(weights, axis=1, keepdims=True)
    rounded = probs.astype(BF16)
    return queries, keys, values, probs, rounded, dot(rounded, values)


def two_parts(value):
    high = value.astype(BF16)
    return high, (value - high.astype(F32)).astype(BF16)


def attention_kernel(small, own, received, upstream, advantage, out):
    scale = HEAD_WIDTH**-0.5
    projection = (own[...] + received[...]).astype(BF16)
    ref_projection, projection = projection[:, :COLS], projection[:, COLS:]
    grad_keys, grad_values = [0.0] * 3, [0.0] * 3
    for block in range(3):
        rows = slice(128 * block, 128 * (block + 1))
        out_ref = attend(small, ref_projection, block)[5]
        queries, keys, values, probs, rounded, out_policy = attend(small, projection, block)
        weight = jnp.concatenate([advantage[rows, :]] * 3, axis=0)
        grad_out = weight * heads(upstream[rows, :].astype(F32))
        grad_out = grad_out + KL_WEIGHT * (out_policy - out_ref)
        high, low = two_parts(grad_out * 12288**-0.5)
        grad_probs = dot(high, values, ((1,), (1,))) + dot(low, values, ((1,), (1,)))
        grad_scores = probs * (grad_probs - jnp.sum(grad_probs * probs, axis=1, keepdims=True))
        grad_scores = (grad_scores * scale).astype(BF16)
        grad_query = dot(grad_scores, keys)
        for i in range(3):
            out[rows, 128 * i : 128 * (i + 1)] = grad_query[128 * i : 128 * (i + 1)].astype(BF16)
        for_keys = dot(grad_scores, queries, ((0,), (0,)))
        for_values = dot(rounded, high, ((0,), (0,)))
        for k in range(block + 1):
            grad_keys[k] = grad_keys[k] + for_keys[128 * k : 128 * (k + 1)]
            grad_values[k] = grad_values[k] + for_values[128 * k : 128 * (k + 1)]
    for k in range(3):
        out[128 * k : 128 * (k + 1), 384:512] = grad_keys[k].astype(BF16)
        out[128 * k : 128 * (k + 1), 512:640] = grad_values[k].astype(BF16)


def attention(small, own, received, upstream, advantage):
    return pl.pallas_call(
        attention_kernel,
        out_shape=jax.ShapeDtypeStruct((ROWS, COLS), BF16),
        in_specs=[SMEM] + [VMEM] * 4,
        out_specs=VMEM,
        compiler_params=PARAMS,
        name="attention",
    )(small, own, received, upstream, advantage)


def gradient_dot(move, where, whole, far, last, grad):
    first, _, first_stride, second_stride = turned_place(where)
    parts = [(whole, 0), (far, 5 * HALF), (last, 7 * HALF)]
    rows = []
    for k in range(4):
        chunk = wrapped(first + move, 4) * first_stride + k * second_stride
        rows.append(chunk_rows(parts, slot_of(chunk, where[3])))
    return dot(jnp.concatenate(rows, axis=0), grad).astype(BF16)


PART = jax.ShapeDtypeStruct((4 * CHUNK, COLS), BF16)


def gradient_part(where, whole, far, last, own, other, move):
    def kernel(where, whole, far, last, own, other, out):
        grad = jnp.concatenate([own[...], other[...]], axis=0)
        out[...] = gradient_dot(move, where, whole, far, last, grad)

    return pl.pallas_call(
        kernel,
        out_shape=PART,
        in_specs=[SMEM] + [VMEM] * 5,
        out_specs=VMEM,
        compiler_params=PARAMS,
        name="gradient",
    )(where, whole, far, last, own, other)


def early_gradient(where, whole, far, last, own, move):
    def kernel(where, whole, far, last, own, out, other_rows):
        parts = [(whole, 0), (far, 5 * HALF), (last, 7 * HALF)]
        first, _, first_stride, second_stride = turned_place(where)
        rows = []
        for k in range(4):
            chunk = wrapped(first + move, 4) * first_stride + k * second_stride
            rows.append(chunk_rows(parts, slot_of(chunk, where[3])))
        rows = jnp.concatenate(rows, axis=0)
        other_rows[...] = rows[:, ROWS:]
        out[...] = dot(rows[:, :ROWS], own[...])

    return pl.pallas_call(
        kernel,
        out_shape=(
            jax.ShapeDtypeStruct((4 * CHUNK, COLS), F32),
            jax.ShapeDtypeStruct((4 * CHUNK, ROWS), BF16),
        ),
        in_specs=[SMEM] + [VMEM] * 4,
        out_specs=(VMEM,) * 2,
        compiler_params=PARAMS,
        name="early",
    )(where, whole, far, last, own)


def rest_gradient(early, rows, other):
    def kernel(early, rows, other, out):
        out[...] = (early[...] + dot(rows[...], other[...])).astype(BF16)

    return pl.pallas_call(
        kernel,
        out_shape=PART,
        in_specs=[VMEM] * 3,
        out_specs=VMEM,
        compiler_params=PARAMS,
        name="rest",
    )(early, rows, other)


def three_sum(own, first, second):
    def kernel(own, first, second, out):
        out[...] = own[...].astype(F32) + first[...].astype(F32) + second[...].astype(F32)

    return pl.pallas_call(
        kernel,
        out_shape=jax.ShapeDtypeStruct((4 * CHUNK, COLS), F32),
        in_specs=[VMEM] * 3,
        out_specs=VMEM,
        compiler_params=PARAMS,
        name="three",
    )(own, first, second)


def middle_kernel(where, three, piece, *outs):
    second = turned_place(where)[1]
    for move, out in zip((0, 1, -1, 2), outs):
        at = pl.ds(pl.multiple_of(wrapped(second + move, 4) * CHUNK, 16), CHUNK)
        out[...] = (three[at, :] + piece[at, :].astype(F32)).astype(out.dtype)


def middle_sums(where, three, piece):
    def shape(kind):
        return jax.ShapeDtypeStruct((CHUNK, COLS), kind)

    return pl.pallas_call(
        middle_kernel,
        out_shape=(shape(F32), shape(BF16), shape(BF16), shape(BF16)),
        in_specs=[SMEM] + [VMEM] * 2,
        out_specs=(VMEM,) * 4,
        compiler_params=PARAMS,
        name="middle",
    )(where, three, piece)


def final_kernel(own, first, second, third, out):
    out[:, 0, :] = (own[...] + first[...].astype(F32)) + (second[...].astype(F32) + third[...].astype(F32))


def final_sums(own, pieces):
    return pl.pallas_call(
        final_kernel,
        out_shape=jax.ShapeDtypeStruct((CHUNK, 1, COLS), F32),
        in_specs=[VMEM] * 4,
        out_specs=VMEM,
        compiler_params=PARAMS,
        name="final",
    )(own, *pieces)


def body(
    tokens,
    dest_shard,
    dest_offset,
    seg_lengths,
    rewards,
    groups,
    reference_head_weight,
    policy_head_weight,
    upstream,
):
    where = jnp.stack([lax.axis_index(name).astype(I32) for name in ("y", "x", "c", "z")])
    small = jnp.concatenate([where, rewards, groups, seg_lengths[0]])
    outgoing = route(rewards, groups, dest_shard, dest_offset, tokens)
    arrived = lax.all_to_all(outgoing, ("y", "x", "c"), split_axis=0, concat_axis=0, tiled=True)
    arrived, small = lax.optimization_barrier((arrived, small))
    _, weights, policy_weights = lax.optimization_barrier(
        (outgoing, reference_head_weight[:, 0], policy_head_weight[:, 0])
    )
    weights = jnp.concatenate([weights, policy_weights], axis=1)
    near = [weights, *(turned(weights, True, by) for by in (1, -1, 2))]
    block = place(arrived)
    _, near = lax.optimization_barrier((block, near))
    rows = join(near)
    across, right, left = (turned(rows, False, by) for by in (2, 1, -1))
    weights = [right, left, across]

    forward, backward = [block], [block]
    for _ in range(3):
        forward.append(shift(forward[-1], "z", 8, 1))
        backward.append(shift(backward[-1], "z", 8, -1))

    near = [forward[2], forward[1], block, backward[1], backward[2]]
    own, other, late, advantage, whole = project(small, arrived, near, rows)
    far = [backward[3], forward[3]]
    behind, ahead, own = lax.optimization_barrier((*far, own))
    first = shift(ahead[:CHUNK], "z", 8, 1)
    second = shift(behind[CHUNK:], "z", 8, -1)
    own, other, far = project_far(small, own, other, far, rows)
    swap = [(0, 1), (1, 0)]
    other, late = across_other(small, other, late, whole, far, weights)
    other, last = late_other(other, late, first, second)
    received = lax.ppermute(other, "c", swap)
    own = across_own(small, own, late, whole, far, last, weights)
    cotangent = upstream.reshape(ROWS, 3 * HEAD_WIDTH)
    grad = attention(small, own, received, cotangent, advantage)
    grad_other = lax.ppermute(grad, "c", swap)
    early, early_rows = early_gradient(small, whole, far, last, grad, 2)

    parts = []
    for move in (-1, 1, 2, 0):
        if move == 2:
            part = rest_gradient(early, early_rows, grad_other)
        else:
            part = gradient_part(small, whole, far, last, grad, grad_other, move)
        parts.append(turned(part, True, move) if move else part)
    sums = middle_sums(small, three_sum(parts[3], parts[2], parts[1]), parts[0])
    parts = [turned(part, False, move) for move, part in zip((1, -1, 2), sums[1:])]
    return final_sums(sums[0], parts)


def solution(mesh):
    split = Mesh(mesh.devices.reshape(4, 4, 2, 8), ("y", "x", "c", "z"))
    roll = ("y", "x", "c")
    in_specs = (
        P(roll, "z"),
        P(roll),
        P(roll),
        P(roll, None),
        P(roll),
        P(roll),
        P(roll, "z", None),
        P(roll, "z", None),
        P(roll, "z", None),
    )
    out_specs = P(roll, "z", None)
    return jax.shard_map(body, mesh=split, in_specs=in_specs, out_specs=out_specs, check_vma=False)
```
